32 devices in a mesh: ctx: 8 (over z, y), tp: 4 (over x, core).
Axes of the slice: x: 2, y: 2, z: 4, core: 2. Of those that a mesh axis runs over, the one named last changes fastest.
Arguments:
- query_heads: bfloat16 [1024, 32, 128], P('ctx', 'tp'), may hold values from -5 to 5
- key_heads: bfloat16 [1024, 4, 128], P('ctx', 'tp'), may hold values from -5 to 5
- value_heads: bfloat16 [1024, 4, 128], P('ctx', 'tp'), may hold values from -6 to 6
- parents: int32 [8], replicated, may hold values from -1 to 6, as said below
- out_weight: bfloat16 [4096, 4096], P('tp'), may hold values from -1 to 1
Outputs:
- projected: bfloat16 [1024, 4096], P('ctx', 'tp')
The draws below stay inside these ranges and needn't reach their ends.
Inputs may be any that keep to these rules, and one draw needn't show every extreme that they name: parents[0] is -1 and every other block's parent is an earlier block; block 7 has parent 8 - 2.
All inputs are finite; a program needn't handle non-finite values.
Results may differ from the reference program's by a relative error of at most 0.015.
Values may be sent and summed in bfloat16 or wider, within the bound.
No kernel may reach another device: no remote copies, remote signals or barrier semaphores. Data moves between devices by JAX's collectives and lax.ppermute only.
A program may use at most 128 MiB of HBM per device.

```python
import math
import jax
import jax.numpy as jnp
from jax import lax

HEADS = 32
KV_HEADS = 4
HEAD_DIM = 128
WIDTH_OUT = 4096
BLOCK = 128
SEQ = 1024
NBLK = 8


def draw_query_heads(key, part):
    shape_all = (SEQ, HEADS, HEAD_DIM)
    sample = 1.2 * jax.random.normal(jax.random.fold_in(key, 11), shape_all, jnp.float32)
    return jnp.clip(sample, -5.0, 5.0).astype(jnp.bfloat16)


def draw_key_heads(key, part):
    shape_all = (SEQ, KV_HEADS, HEAD_DIM)
    sample = 1.2 * jax.random.normal(jax.random.fold_in(key, 13), shape_all, jnp.float32)
    return jnp.clip(sample, -5.0, 5.0).astype(jnp.bfloat16)


def draw_parents(key, part):
    block_ids = jnp.arange(NBLK, dtype=jnp.int32)
    coins = jax.random.randint(jax.random.fold_in(key, 21), (NBLK,), 0, 3)
    jumps = jax.random.randint(jax.random.fold_in(key, 22), (NBLK,), 0, jnp.maximum(block_ids, 1))
    parent_ids = jnp.where(coins == 0, block_ids - 1, jumps)
    parent_ids = jnp.where(block_ids == NBLK - 1, block_ids - 1, parent_ids)
    parent_ids = jnp.where(block_ids == 0, -1, parent_ids)
    return parent_ids.astype(jnp.int32)


def strengthened(array, rng, source, target, shards_of, factor):
    def block_of(axis_at):
        return (jnp.arange(array.shape[axis_at]) // (array.shape[axis_at] // shards_of)).reshape((-1,) + (1,) * (array.ndim - 1 - axis_at))

    near = jax.random.permutation(rng, shards_of)[block_of(target)]
    far = (block_of(target) + shards_of // 2) % shards_of
    return jnp.where((block_of(source) == near) | (block_of(source) == far), factor * array, array)


def level_of(stream_key, extent, pieces, least, high):
    def one(position, parts):
        heights = jax.random.uniform(jax.random.fold_in(jax.random.fold_in(stream_key, 6), position), (parts,), jnp.float32, least / len(pieces), high / len(pieces))
        return jnp.repeat(jnp.exp(heights), extent[position] // parts).reshape((-1,) + (1,) * (len(extent) - position - 1))

    level = one(*pieces[0])
    for cut in pieces[1:]:
        level = level * one(*cut)
    return level


def normal_values(rng, shape, width, most, cuts=(), held_as=jnp.bfloat16):
    result = width * jax.random.normal(rng, shape, jnp.float32)
    if cuts:
        result = result * level_of(rng, shape, cuts, -0.22, 0.18)
    return jnp.clip(result, -most, most).astype(held_as)


def heavy_noise(own_key, dims, scale, most, pieces, heavy, kind=jnp.bfloat16):
    drawn = scale * jax.random.normal(own_key, dims, jnp.float32)
    if pieces:
        drawn = drawn * level_of(own_key, dims, pieces, -0.22, 0.18)
    return jnp.clip(strengthened(drawn, jax.random.fold_in(own_key, 3), *heavy), -most, most).astype(kind)


def setup_inputs(seed: int = 0) -> dict:
    key_of = jax.random.split(jax.random.key(seed), 6)
    query_heads = draw_query_heads(jax.random.fold_in(key_of[5], 71), 0)
    key_heads = draw_key_heads(jax.random.fold_in(key_of[5], 71), 0)
    value_heads = normal_values(key_of[2], (SEQ, KV_HEADS, HEAD_DIM), 1.0, 6.0, ((0, 8), (1, 4)))
    parents = draw_parents(jax.random.fold_in(key_of[5], 71), 0)
    out_weight = heavy_noise(key_of[4], (HEADS * HEAD_DIM, WIDTH_OUT), (HEADS * HEAD_DIM // 64) ** -0.5, 1.0, ((0, 4),), (0, 1, 4, 2.0))
    return {"query_heads": query_heads, "key_heads": key_heads, "value_heads": value_heads, "parents": parents, "out_weight": out_weight}


def lineage_table(parents):
    width_blocks = parents.shape[0]
    block_ids = jnp.arange(width_blocks, dtype=jnp.int32)
    lineage = (parents[:, None] == block_ids[None, :]).astype(jnp.int32)
    lineage = lineage + (block_ids[:, None] == block_ids[None, :]).astype(jnp.int32)
    for squaring in range(max(width_blocks - 1, 1).bit_length()):
        lineage = jnp.minimum(jnp.dot(lineage, lineage, preferred_element_type=jnp.int32), 1)
    return lineage

def reference(query_heads, key_heads, value_heads, parents, out_weight):
    group_size = HEADS // KV_HEADS
    score_scale = 1.0 / math.sqrt(HEAD_DIM)
    lineage = lineage_table(parents)
    positions = jnp.arange(SEQ, dtype=jnp.int32)
    key_blocks = positions // BLOCK
    key_float = key_heads.astype(jnp.float32)
    value_float = value_heads.astype(jnp.float32)

    def one_block(block_index):
        offset = (block_index * BLOCK).astype(jnp.int32)
        query_block = lax.dynamic_slice_in_dim(query_heads, offset, BLOCK, 0).astype(jnp.float32)
        grouped = query_block.reshape(BLOCK, KV_HEADS, group_size, HEAD_DIM)
        scores = jnp.einsum('tgjd,sgd->gjts', grouped, key_float) * score_scale
        lineage_row = lax.dynamic_index_in_dim(lineage, block_index, 0, keepdims=False)
        reached = jnp.take(lineage_row, key_blocks)
        query_ids = offset + jnp.arange(BLOCK, dtype=jnp.int32)
        visible_mask = (reached[None, :] > 0) & (positions[None, :] <= query_ids[:, None])
        scores = jnp.where(visible_mask, scores, -jnp.inf)
        row_max = lax.optimization_barrier(jnp.max(scores, axis=-1, keepdims=True))
        weights = jnp.exp(scores - row_max)
        running_sum = lax.optimization_barrier(jnp.sum(weights, axis=-1))
        rounded = lax.optimization_barrier(weights.astype(jnp.bfloat16)).astype(jnp.float32)
        numerator = jnp.einsum('gjts,sgd->gjtd', rounded, value_float)
        normalized = numerator / running_sum[..., None]
        return jnp.transpose(normalized, (2, 0, 1, 3)).reshape(BLOCK, HEADS * HEAD_DIM).astype(jnp.bfloat16)
    attended = lax.map(one_block, jnp.arange(NBLK, dtype=jnp.int32)).reshape(SEQ, HEADS * HEAD_DIM)
    return jnp.dot(attended, out_weight, preferred_element_type=jnp.float32).astype(jnp.bfloat16)
```

```python
import functools
import math

import jax
import jax.numpy as jnp
from jax import lax
from jax.experimental import pallas as pl
from jax.experimental.pallas import tpu as pltpu
from jax.sharding import PartitionSpec as P

BLOCK = 128
DIRECT_MOST = 8


def attend_project_kernel(n_pieces, gathered, tp_size, parents_ref, q_ref, *refs):
    kv_refs = refs[:n_pieces]
    w_hbm, keep_ref, send_ref, w_ref, m_ref, l_ref, acc_ref, att_ref, w_sem = refs[n_pieces:]
    rows, head_dim = q_ref.shape
    group = rows // BLOCK
    width = keep_ref.shape[2]
    scale = math.log2(math.e) / math.sqrt(head_dim)
    me = lax.axis_index("ctx")
    mine = lax.axis_index("tp")

    w_copy = pltpu.make_async_copy(w_hbm, w_ref, w_sem)
    w_copy.start()

    def scores_of(k):
        return lax.dot_general(k, q_ref[...], (((1,), (1,)), ((), ())), preferred_element_type=jnp.float32)

    def weighted(v, p):
        return lax.dot_general(v, p.astype(jnp.bfloat16), (((0,), (0,)), ((), ())), preferred_element_type=jnp.float32)

    own = kv_refs[0]
    s = scores_of(own[0:BLOCK, :])
    key_at = lax.broadcasted_iota(jnp.int32, s.shape, 0)
    query_at = lax.broadcasted_iota(jnp.int32, s.shape, 1) & (BLOCK - 1)
    s = jnp.where(key_at <= query_at, s, -1e30)
    m = jnp.max(s, axis=0, keepdims=True)
    p = jnp.exp2((s - m) * scale)
    m_ref[...] = m
    l_ref[...] = jnp.sum(p, axis=0, keepdims=True)
    acc_ref[...] = weighted(own[BLOCK:, :], p)

    def absorb(k, v):
        s = scores_of(k)
        m_old = m_ref[...]
        m_new = jnp.maximum(m_old, jnp.max(s, axis=0, keepdims=True))
        p = jnp.exp2((s - m_new) * scale)
        factor = jnp.exp2((m_old - m_new) * scale)
        m_ref[...] = m_new
        l_ref[...] = l_ref[...] * factor + jnp.sum(p, axis=0, keepdims=True)
        acc_ref[...] = acc_ref[...] * factor + weighted(v, p)

    ancestor = parents_ref[me]
    if gathered:
        piece = kv_refs[1]

        def visit(step, wanted):
            block = me - step
            hit = (block >= 0) & (block == wanted)

            @pl.when(hit)
            def _():
                start = pl.multiple_of(block * 2 * BLOCK, 2 * BLOCK)
                absorb(piece[pl.ds(start, BLOCK), :], piece[pl.ds(start + BLOCK, BLOCK), :])

            return jnp.where(hit, parents_ref[jnp.maximum(block, 0)], wanted)

        lax.fori_loop(1, parents_ref.shape[0], visit, ancestor)
    else:
        for step in range(1, n_pieces):
            block = me - step
            hit = (block >= 0) & (block == ancestor)

            @pl.when(hit)
            def _():
                absorb(kv_refs[step][0:BLOCK, :], kv_refs[step][BLOCK:, :])

            ancestor = jnp.where(hit, parents_ref[jnp.maximum(block, 0)], ancestor)

    for head in range(group):
        at = slice(head * BLOCK, (head + 1) * BLOCK)
        part = acc_ref[:, at] / l_ref[:, at]
        att_ref[:, head * head_dim:(head + 1) * head_dim] = part.T.astype(jnp.bfloat16)

    w_copy.wait()

    def project(block):
        start = pl.multiple_of(block * width, 128)
        return jnp.dot(att_ref[...], w_ref[:, pl.ds(start, width)], preferred_element_type=jnp.float32)

    if tp_size == 4:
        far = mine ^ 2
        send_ref[0] = project(far ^ 1).astype(jnp.bfloat16)
        send_ref[1] = project(mine ^ 1).astype(jnp.bfloat16)
        keep_ref[0] = project(far)
        keep_ref[1] = project(mine)
    else:
        for block in range(tp_size):
            send_ref[block] = project(block).astype(jnp.bfloat16)
        keep_ref[...] = jnp.zeros_like(keep_ref)


def shards(ctx_size, tp_size, query_heads, key_heads, value_heads, parents, out_weight):
    tok_rows, local_heads, head_dim = query_heads.shape
    assert tok_rows == BLOCK and key_heads.shape[1] == 1 and parents.shape[0] == ctx_size
    width = out_weight.shape[1] // tp_size
    rows = local_heads * tok_rows

    kv = jnp.concatenate([key_heads[:, 0, :], value_heads[:, 0, :]], axis=0)
    pieces = [kv]
    gathered = ctx_size > DIRECT_MOST
    if gathered:
        pieces.append(lax.all_gather(kv, "ctx", axis=0, tiled=True))
    else:
        for step in range(1, ctx_size):
            pieces.append(lax.ppermute(kv, "ctx", [(i, i + step) for i in range(ctx_size - step)]))
    q = jnp.transpose(query_heads, (1, 0, 2)).reshape(rows, head_dim)

    vmem = pl.BlockSpec(memory_space=pltpu.VMEM)
    n_send = 2 if tp_size == 4 else tp_size
    keep, send = pl.pallas_call(
        functools.partial(attend_project_kernel, len(pieces), gathered, tp_size),
        out_shape=(
            jax.ShapeDtypeStruct((2, tok_rows, width), jnp.float32),
            jax.ShapeDtypeStruct((n_send, tok_rows, width), jnp.bfloat16),
        ),
        in_specs=[pl.BlockSpec(memory_space=pltpu.SMEM), vmem] + [vmem] * len(pieces) + [pl.BlockSpec(memory_space=pl.ANY)],
        out_specs=(vmem, vmem),
        scratch_shapes=[
            pltpu.VMEM(out_weight.shape, jnp.bfloat16),
            pltpu.VMEM((1, rows), jnp.float32),
            pltpu.VMEM((1, rows), jnp.float32),
            pltpu.VMEM((head_dim, rows), jnp.float32),
            pltpu.VMEM((tok_rows, local_heads * head_dim), jnp.bfloat16),
            pltpu.SemaphoreType.DMA,
        ],
        compiler_params=pltpu.CompilerParams(vmem_limit_bytes=32 * 1024 * 1024),
        cost_estimate=pl.CostEstimate(flops=1_600_000_000, bytes_accessed=12_000_000, transcendentals=1_000_000),
    )(parents, q, *pieces, out_weight)

    if tp_size != 4:
        flat = jnp.transpose(send, (1, 0, 2)).reshape(tok_rows, tp_size * width)
        return lax.psum_scatter(flat, "tp", scatter_dimension=1, tiled=True)
    near_pairs = [(i, i ^ 1) for i in range(4)]
    far_pairs = [(i, i ^ 2) for i in range(4)]
    far_in = lax.ppermute(send[0], "tp", near_pairs)
    near_in = lax.ppermute(send[1], "tp", near_pairs)
    far_sum = (keep[0] + far_in.astype(jnp.float32)).astype(jnp.bfloat16)
    from_far = lax.ppermute(far_sum, "tp", far_pairs)
    return (keep[1] + near_in.astype(jnp.float32) + from_far.astype(jnp.float32)).astype(jnp.bfloat16)


def solution(mesh):
    return jax.shard_map(
        functools.partial(shards, mesh.shape["ctx"], mesh.shape["tp"]),
        mesh=mesh,
        in_specs=(
            P("ctx", "tp", None),
            P("ctx", "tp", None),
            P("ctx", "tp", None),
            P(),
            P("tp", None),
        ),
        out_specs=P("ctx", "tp"),
        check_vma=False,
    )
```

```python
import functools
import math

import jax
import jax.numpy as jnp
from jax import lax
from jax.experimental import pallas as pl
from jax.experimental.pallas import tpu as pltpu
from jax.sharding import PartitionSpec as P

BLOCK = 128
DIRECT_SIZE = 8
VMEM_LIMIT = 32 * 1024 * 1024


def scores_of(k, q):
    return lax.dot_general(k, q, (((1,), (1,)), ((), ())), preferred_element_type=jnp.float32)


def weighted(v, p):
    return lax.dot_general(v, p.astype(jnp.bfloat16), (((0,), (0,)), ((), ())), preferred_element_type=jnp.float32)


def exponent_scale(head_dim):
    return math.log2(math.e) / math.sqrt(head_dim)


def own_block_kernel(q_ref, kv_ref, w_hbm, m_ref, l_ref, acc_ref, w_ref, w_sem):
    w_copy = pltpu.make_async_copy(w_hbm, w_ref, w_sem)
    w_copy.start()
    scale = exponent_scale(q_ref.shape[1])
    s = scores_of(kv_ref[0:BLOCK, :], q_ref[...])
    key_at = lax.broadcasted_iota(jnp.int32, s.shape, 0)
    query_at = lax.broadcasted_iota(jnp.int32, s.shape, 1) & (BLOCK - 1)
    s = jnp.where(key_at <= query_at, s, -1e30)
    m = jnp.max(s, axis=0, keepdims=True)
    p = jnp.exp2((s - m) * scale)
    m_ref[...] = m
    l_ref[...] = jnp.sum(p, axis=0, keepdims=True)
    acc_ref[...] = weighted(kv_ref[BLOCK:, :], p)
    w_copy.wait()


def project(att, w_ref, block, width):
    start = pl.multiple_of(block * width, 128)
    return jnp.dot(att, w_ref[:, pl.ds(start, width)], preferred_element_type=jnp.float32)


def others_kernel(xors, parents_ref, q_ref, m_in, l_in, acc_in, *refs):
    kv_refs = refs[:max(len(xors), 1)]
    w_ref, att_ref, send_ref, keep_ref, m_ref, l_ref, acc_ref = refs[len(kv_refs):]
    rows, head_dim = q_ref.shape
    group = rows // BLOCK
    width = keep_ref.shape[1]
    scale = exponent_scale(head_dim)
    me = lax.axis_index("ctx")
    far = lax.axis_index("tp") ^ 2

    m_ref[...] = m_in[...]
    l_ref[...] = l_in[...]
    acc_ref[...] = acc_in[...]

    def absorb(k, v):
        s = scores_of(k, q_ref[...])
        m_old = m_ref[...]
        m_new = jnp.maximum(m_old, jnp.max(s, axis=0, keepdims=True))
        p = jnp.exp2((s - m_new) * scale)
        factor = jnp.exp2((m_old - m_new) * scale)
        m_ref[...] = m_new
        l_ref[...] = l_ref[...] * factor + jnp.sum(p, axis=0, keepdims=True)
        acc_ref[...] = acc_ref[...] * factor + weighted(v, p)

    if xors:
        wanted = parents_ref[me]
        reached = jnp.int32(0)
        for step in range(1, len(xors) + 1):
            block = me - step
            hit = (block >= 0) & (block == wanted)
            block = jnp.maximum(block, 0)
            reached = jnp.where(hit, reached | lax.shift_left(jnp.int32(1), block), reached)
            wanted = jnp.where(hit, parents_ref[block], wanted)
        for other, kv_ref in zip(xors, kv_refs):
            @pl.when((lax.shift_right_logical(reached, me ^ other) & 1) == 1)
            def _():
                absorb(kv_ref[0:BLOCK, :], kv_ref[BLOCK:, :])
    else:
        piece = kv_refs[0]

        def visit(step, wanted):
            block = me - step
            hit = (block >= 0) & (block == wanted)
            block = jnp.maximum(block, 0)

            @pl.when(hit)
            def _():
                start = pl.multiple_of(block * 2 * BLOCK, 2 * BLOCK)
                absorb(piece[pl.ds(start, BLOCK), :], piece[pl.ds(start + BLOCK, BLOCK), :])

            return jnp.where(hit, parents_ref[block], wanted)

        lax.fori_loop(1, parents_ref.shape[0], visit, parents_ref[me])

    for head in range(group):
        at = slice(head * BLOCK, (head + 1) * BLOCK)
        part = acc_ref[:, at] / l_ref[:, at]
        att_ref[:, head * head_dim:(head + 1) * head_dim] = part.T.astype(jnp.bfloat16)

    att = att_ref[...]
    send_ref[...] = project(att, w_ref, far ^ 1, width).astype(jnp.bfloat16)
    keep_ref[...] = project(att, w_ref, far, width)


def near_kernel(att_ref, w_ref, send_ref, keep_ref):
    mine = lax.axis_index("tp")
    width = keep_ref.shape[1]
    att = att_ref[...]
    send_ref[...] = project(att, w_ref, mine ^ 1, width).astype(jnp.bfloat16)
    keep_ref[...] = project(att, w_ref, mine, width)


def shards(ctx_size, tp_size, query_heads, key_heads, value_heads, parents, out_weight):
    tok_rows, local_heads, head_dim = query_heads.shape
    assert tok_rows == BLOCK and key_heads.shape[1] == 1 and parents.shape[0] == ctx_size and tp_size == 4
    width = out_weight.shape[1] // tp_size
    rows = local_heads * tok_rows
    params = pltpu.CompilerParams(vmem_limit_bytes=VMEM_LIMIT)
    vmem = pl.BlockSpec(memory_space=pltpu.VMEM)
    hbm = pl.BlockSpec(memory_space=pltpu.HBM)
    smem = pl.BlockSpec(memory_space=pltpu.SMEM)

    def swap(x, axis, size, other):
        return lax.ppermute(x, axis, [(i, i ^ other) for i in range(size)])

    kv = jnp.concatenate([key_heads[:, 0, :], value_heads[:, 0, :]], axis=0)
    if ctx_size == DIRECT_SIZE:
        columns = [swap(kv, "ctx", ctx_size, other) for other in (2, 4, 6)]
        beside = swap(kv, "ctx", ctx_size, 1)
    q = jnp.transpose(query_heads, (1, 0, 2)).reshape(rows, head_dim)

    m, l, acc, w = pl.pallas_call(
        own_block_kernel,
        out_shape=(
            jax.ShapeDtypeStruct((1, rows), jnp.float32),
            jax.ShapeDtypeStruct((1, rows), jnp.float32),
            jax.ShapeDtypeStruct((head_dim, rows), jnp.float32),
            jax.ShapeDtypeStruct(out_weight.shape, out_weight.dtype),
        ),
        in_specs=[vmem, vmem, hbm],
        out_specs=(vmem, vmem, vmem, vmem),
        scratch_shapes=[pltpu.SemaphoreType.DMA],
        compiler_params=params,
        cost_estimate=pl.CostEstimate(flops=67_000_000, bytes_accessed=9_000_000, transcendentals=130_000),
    )(q, kv, pltpu.with_memory_space_constraint(out_weight, pltpu.HBM))

    if ctx_size == DIRECT_SIZE:
        pairs = []
        for at in range(3):
            columns[at], m = lax.optimization_barrier((columns[at], m))
            pairs.append(swap(columns[at], "ctx", ctx_size, 1))
        pieces = columns + pairs + [beside]
        xors = (2, 4, 6, 3, 5, 7, 1)
    else:
        xors = ()
        pieces = [lax.all_gather(kv, "ctx", axis=0, tiled=True)]

    att, send_far, keep_far = pl.pallas_call(
        functools.partial(others_kernel, xors),
        out_shape=(
            jax.ShapeDtypeStruct((tok_rows, local_heads * head_dim), jnp.bfloat16),
            jax.ShapeDtypeStruct((tok_rows, width), jnp.bfloat16),
            jax.ShapeDtypeStruct((tok_rows, width), jnp.float32),
        ),
        in_specs=[smem] + [vmem] * (5 + len(pieces)),
        out_specs=(vmem, vmem, vmem),
        scratch_shapes=[
            pltpu.VMEM((1, rows), jnp.float32),
            pltpu.VMEM((1, rows), jnp.float32),
            pltpu.VMEM((head_dim, rows), jnp.float32),
        ],
        compiler_params=params,
        cost_estimate=pl.CostEstimate(flops=1_000_000_000, bytes_accessed=10_000_000, transcendentals=1_000_000),
    )(parents, q, m, l, acc, *pieces, w)

    far_in = swap(send_far, "tp", tp_size, 1)
    send_near, keep_near = pl.pallas_call(
        near_kernel,
        out_shape=(
            jax.ShapeDtypeStruct((tok_rows, width), jnp.bfloat16),
            jax.ShapeDtypeStruct((tok_rows, width), jnp.float32),
        ),
        in_specs=[vmem, vmem],
        out_specs=(vmem, vmem),
        compiler_params=params,
        cost_estimate=pl.CostEstimate(flops=540_000_000, bytes_accessed=4_000_000, transcendentals=0),
    )(att, w)
    near_in = swap(send_near, "tp", tp_size, 1)
    far_sum = (keep_far + far_in.astype(jnp.float32)).astype(jnp.bfloat16)
    from_far = swap(far_sum, "tp", tp_size, 2)
    return (keep_near + near_in.astype(jnp.float32) + from_far.astype(jnp.float32)).astype(jnp.bfloat16)


def solution(mesh):
    return jax.shard_map(
        functools.partial(shards, mesh.shape["ctx"], mesh.shape["tp"]),
        mesh=mesh,
        in_specs=(
            P("ctx", "tp", None),
            P("ctx", "tp", None),
            P("ctx", "tp", None),
            P(),
            P("tp", None),
        ),
        out_specs=P("ctx", "tp"),
        check_vma=False,
    )
```

```python
import functools
import math

import jax
import jax.numpy as jnp
from jax import lax
from jax.experimental import pallas as pl
from jax.experimental.pallas import tpu as pltpu
from jax.sharding import PartitionSpec as P

BLOCK = 128
DIRECT_SIZE = 8
VMEM_LIMIT = 32 * 1024 * 1024


def scores_of(k, q):
    return lax.dot_general(k, q, (((1,), (1,)), ((), ())), preferred_element_type=jnp.float32)


def weighted(v, p):
    return lax.dot_general(v, p.astype(jnp.bfloat16), (((0,), (0,)), ((), ())), preferred_element_type=jnp.float32)


def exponent_scale(head_dim):
    return math.log2(math.e) / math.sqrt(head_dim)


def pack_kernel(k_hbm, v_hbm, kv_ref, sems):
    k_copy = pltpu.make_async_copy(k_hbm, kv_ref.at[0:BLOCK, :], sems.at[0])
    v_copy = pltpu.make_async_copy(v_hbm, kv_ref.at[BLOCK:2 * BLOCK, :], sems.at[1])
    k_copy.start()
    v_copy.start()
    k_copy.wait()
    v_copy.wait()


def own_block_kernel(q_ref, kv_ref, m_ref, l_ref, acc_ref):
    scale = exponent_scale(q_ref.shape[1])
    s = scores_of(kv_ref[0:BLOCK, :], q_ref[...])
    key_at = lax.broadcasted_iota(jnp.int32, s.shape, 0)
    query_at = lax.broadcasted_iota(jnp.int32, s.shape, 1) & (BLOCK - 1)
    s = jnp.where(key_at <= query_at, s, -1e30)
    m = jnp.max(s, axis=0, keepdims=True)
    p = jnp.exp2((s - m) * scale)
    m_ref[...] = m
    l_ref[...] = jnp.sum(p, axis=0, keepdims=True)
    acc_ref[...] = weighted(kv_ref[BLOCK:, :], p)


def project(att, w_ref, block, width):
    start = pl.multiple_of(block * width, 128)
    return jnp.dot(att, w_ref[:, pl.ds(start, width)], preferred_element_type=jnp.float32)


def absorb(scale, q_ref, k, v, m_ref, l_ref, acc_ref):
    s = scores_of(k, q_ref[...])
    m_old = m_ref[...]
    m_new = jnp.maximum(m_old, jnp.max(s, axis=0, keepdims=True))
    p = jnp.exp2((s - m_new) * scale)
    factor = jnp.exp2((m_old - m_new) * scale)
    m_ref[...] = m_new
    l_ref[...] = l_ref[...] * factor + jnp.sum(p, axis=0, keepdims=True)
    acc_ref[...] = acc_ref[...] * factor + weighted(v, p)


def absorb_reached(xors, parents_ref, q_ref, kv_refs, state):
    scale = exponent_scale(q_ref.shape[1])
    me = lax.axis_index("ctx")
    wanted = parents_ref[me]
    reached = jnp.int32(0)
    for step in range(1, DIRECT_SIZE):
        block = me - step
        hit = (block >= 0) & (block == wanted)
        block = jnp.maximum(block, 0)
        reached = jnp.where(hit, reached | lax.shift_left(jnp.int32(1), block), reached)
        wanted = jnp.where(hit, parents_ref[block], wanted)
    for other, kv_ref in zip(xors, kv_refs):
        @pl.when((lax.shift_right_logical(reached, me ^ other) & 1) == 1)
        def _():
            absorb(scale, q_ref, kv_ref[0:BLOCK, :], kv_ref[BLOCK:, :], *state)


def absorb_walk(parents_ref, q_ref, piece, state):
    scale = exponent_scale(q_ref.shape[1])
    me = lax.axis_index("ctx")

    def visit(step, wanted):
        block = me - step
        hit = (block >= 0) & (block == wanted)
        block = jnp.maximum(block, 0)

        @pl.when(hit)
        def _():
            start = pl.multiple_of(block * 2 * BLOCK, 2 * BLOCK)
            absorb(scale, q_ref, piece[pl.ds(start, BLOCK), :], piece[pl.ds(start + BLOCK, BLOCK), :], *state)

        return jnp.where(hit, parents_ref[block], wanted)

    lax.fori_loop(1, parents_ref.shape[0], visit, parents_ref[me])


def first_others_kernel(xors, parents_ref, q_ref, m_in, l_in, acc_in, *refs):
    state = refs[len(xors):]
    absorb_reached(xors, parents_ref, q_ref, refs[:len(xors)], state)


def last_others_kernel(xors, parents_ref, q_ref, m_in, l_in, acc_in, *refs):
    kv_refs = refs[:max(len(xors), 1)]
    w_ref, att_ref, send_ref, keep_ref, *state = refs[len(kv_refs):]
    rows, head_dim = q_ref.shape
    group = rows // BLOCK
    width = keep_ref.shape[1]
    far = lax.axis_index("tp") ^ 2
    if xors:
        absorb_reached(xors, parents_ref, q_ref, kv_refs, state)
    else:
        absorb_walk(parents_ref, q_ref, kv_refs[0], state)
    m_ref, l_ref, acc_ref = state

    for head in range(group):
        at = slice(head * BLOCK, (head + 1) * BLOCK)
        part = acc_ref[:, at] / l_ref[:, at]
        att_ref[:, head * head_dim:(head + 1) * head_dim] = part.T.astype(jnp.bfloat16)

    att = att_ref[...]
    send_ref[...] = project(att, w_ref, far ^ 1, width).astype(jnp.bfloat16)
    keep_ref[...] = project(att, w_ref, far, width)


def near_kernel(att_ref, w_ref, send_ref, keep_ref):
    mine = lax.axis_index("tp")
    width = keep_ref.shape[1]
    att = att_ref[...]
    send_ref[...] = project(att, w_ref, mine ^ 1, width).astype(jnp.bfloat16)
    keep_ref[...] = project(att, w_ref, mine, width)


def shards(ctx_size, tp_size, query_heads, key_heads, value_heads, parents, out_weight):
    tok_rows, local_heads, head_dim = query_heads.shape
    assert tok_rows == BLOCK and key_heads.shape[1] == 1 and parents.shape[0] == ctx_size and tp_size == 4
    width = out_weight.shape[1] // tp_size
    rows = local_heads * tok_rows
    params = pltpu.CompilerParams(vmem_limit_bytes=VMEM_LIMIT)
    vmem = pl.BlockSpec(memory_space=pltpu.VMEM)
    hbm = pl.BlockSpec(memory_space=pltpu.HBM)
    smem = pl.BlockSpec(memory_space=pltpu.SMEM)

    def in_hbm(x):
        return pltpu.with_memory_space_constraint(x, pltpu.HBM)

    def swap(x, axis, size, other):
        return lax.ppermute(x, axis, [(i, i ^ other) for i in range(size)])

    kv = pl.pallas_call(
        pack_kernel,
        out_shape=jax.ShapeDtypeStruct((2 * tok_rows, head_dim), jnp.bfloat16),
        in_specs=[hbm, hbm],
        out_specs=vmem,
        scratch_shapes=[pltpu.SemaphoreType.DMA((2,))],
        compiler_params=params,
        cost_estimate=pl.CostEstimate(flops=8_000_000_000, bytes_accessed=130_000, transcendentals=0),
    )(in_hbm(key_heads[:, 0, :]), in_hbm(value_heads[:, 0, :]))
    if ctx_size == DIRECT_SIZE:
        columns = [swap(kv, "ctx", ctx_size, other) for other in (6, 4, 2)]
    q = jnp.transpose(query_heads, (1, 0, 2)).reshape(rows, head_dim)

    m, l, acc = pl.pallas_call(
        own_block_kernel,
        out_shape=(
            jax.ShapeDtypeStruct((1, rows), jnp.float32),
            jax.ShapeDtypeStruct((1, rows), jnp.float32),
            jax.ShapeDtypeStruct((head_dim, rows), jnp.float32),
        ),
        in_specs=[vmem, vmem],
        out_specs=(vmem, vmem, vmem),
        compiler_params=params,
        cost_estimate=pl.CostEstimate(flops=67_000_000, bytes_accessed=1_000_000, transcendentals=130_000),
    )(q, kv)

    state = (m, l, acc)
    state_shapes = tuple(jax.ShapeDtypeStruct(x.shape, x.dtype) for x in state)
    if ctx_size == DIRECT_SIZE:
        late, m = lax.optimization_barrier((kv, m))
        state = (m, l, acc)
        beside = swap(late, "ctx", ctx_size, 1)
        pieces = [swap(x, "ctx", ctx_size, 1) for x in columns]
        xors = (6, 4, 2, 1)
        state = pl.pallas_call(
            functools.partial(first_others_kernel, xors),
            out_shape=state_shapes,
            in_specs=[smem] + [vmem] * (4 + len(xors)),
            out_specs=(vmem,) * 3,
            input_output_aliases={2: 0, 3: 1, 4: 2},
            compiler_params=params,
            cost_estimate=pl.CostEstimate(flops=270_000_000, bytes_accessed=1_000_000, transcendentals=500_000),
        )(parents, q, *state, *columns, beside)
        xors = (7, 5, 3)
    else:
        xors = ()
        pieces = [lax.all_gather(kv, "ctx", axis=0, tiled=True)]

    att, send_far, keep_far, *_ = pl.pallas_call(
        functools.partial(last_others_kernel, xors),
        out_shape=(
            jax.ShapeDtypeStruct((tok_rows, local_heads * head_dim), jnp.bfloat16),
            jax.ShapeDtypeStruct((tok_rows, width), jnp.bfloat16),
            jax.ShapeDtypeStruct((tok_rows, width), jnp.float32),
        ) + state_shapes,
        in_specs=[smem] + [vmem] * (5 + len(pieces)),
        out_specs=(vmem,) * 6,
        input_output_aliases={2: 3, 3: 4, 4: 5},
        compiler_params=params,
        cost_estimate=pl.CostEstimate(flops=1_000_000_000, bytes_accessed=10_000_000, transcendentals=1_000_000),
    )(parents, q, *state, *pieces, out_weight)

    far_in = swap(send_far, "tp", tp_size, 1)
    send_near, keep_near = pl.pallas_call(
        near_kernel,
        out_shape=(
            jax.ShapeDtypeStruct((tok_rows, width), jnp.bfloat16),
            jax.ShapeDtypeStruct((tok_rows, width), jnp.float32),
        ),
        in_specs=[vmem, vmem],
        out_specs=(vmem, vmem),
        compiler_params=params,
        cost_estimate=pl.CostEstimate(flops=540_000_000, bytes_accessed=4_000_000, transcendentals=0),
    )(att, out_weight)
    near_in = swap(send_near, "tp", tp_size, 1)
    far_sum = (keep_far + far_in.astype(jnp.float32)).astype(jnp.bfloat16)
    from_far = swap(far_sum, "tp", tp_size, 2)
    return (keep_near + near_in.astype(jnp.float32) + from_far.astype(jnp.float32)).astype(jnp.bfloat16)


def solution(mesh):
    return jax.shard_map(
        functools.partial(shards, mesh.shape["ctx"], mesh.shape["tp"]),
        mesh=mesh,
        in_specs=(
            P("ctx", "tp", None),
            P("ctx", "tp", None),
            P("ctx", "tp", None),
            P(),
            P("tp", None),
        ),
        out_specs=P("ctx", "tp"),
        check_vma=False,
    )
```

```python
import functools
import math

import jax
import jax.numpy as jnp
from jax import lax
from jax.experimental import pallas as pl
from jax.experimental.pallas import tpu as pltpu
from jax.sharding import PartitionSpec as P

BLOCK = 128
DIRECT_SIZE = 8
VMEM_LIMIT = 32 * 1024 * 1024


def scores_of(k, q):
    return lax.dot_general(k, q, (((1,), (1,)), ((), ())), preferred_element_type=jnp.float32)


def weighted(v, p):
    return lax.dot_general(v, p.astype(jnp.bfloat16), (((0,), (0,)), ((), ())), preferred_element_type=jnp.float32)


def exponent_scale(head_dim):
    return math.log2(math.e) / math.sqrt(head_dim)


def pack_kernel(k_hbm, v_hbm, kv_ref, sems):
    k_copy = pltpu.make_async_copy(k_hbm, kv_ref.at[0:BLOCK, :], sems.at[0])
    v_copy = pltpu.make_async_copy(v_hbm, kv_ref.at[BLOCK:2 * BLOCK, :], sems.at[1])
    k_copy.start()
    v_copy.start()
    k_copy.wait()
    v_copy.wait()


def own_block_kernel(q_ref, kv_ref, m_ref, l_ref, acc_ref):
    scale = exponent_scale(q_ref.shape[1])
    s = scores_of(kv_ref[0:BLOCK, :], q_ref[...])
    key_at = lax.broadcasted_iota(jnp.int32, s.shape, 0)
    query_at = lax.broadcasted_iota(jnp.int32, s.shape, 1) & (BLOCK - 1)
    s = jnp.where(key_at <= query_at, s, -1e30)
    m = jnp.max(s, axis=0, keepdims=True)
    p = jnp.exp2((s - m) * scale)
    m_ref[...] = m
    l_ref[...] = jnp.sum(p, axis=0, keepdims=True)
    acc_ref[...] = weighted(kv_ref[BLOCK:, :], p)


def project(att, w_ref, block, width):
    start = pl.multiple_of(block * width, 128)
    return jnp.dot(att, w_ref[:, pl.ds(start, width)], preferred_element_type=jnp.float32)


def absorb(scale, q_ref, k, v, m_ref, l_ref, acc_ref):
    s = scores_of(k, q_ref[...])
    m_old = m_ref[...]
    m_new = jnp.maximum(m_old, jnp.max(s, axis=0, keepdims=True))
    p = jnp.exp2((s - m_new) * scale)
    factor = jnp.exp2((m_old - m_new) * scale)
    m_ref[...] = m_new
    l_ref[...] = l_ref[...] * factor + jnp.sum(p, axis=0, keepdims=True)
    acc_ref[...] = acc_ref[...] * factor + weighted(v, p)


def absorb_reached(xors, parents_ref, q_ref, kv_refs, state):
    scale = exponent_scale(q_ref.shape[1])
    me = lax.axis_index("ctx")
    wanted = parents_ref[me]
    reached = jnp.int32(0)
    for step in range(1, DIRECT_SIZE):
        block = me - step
        hit = (block >= 0) & (block == wanted)
        block = jnp.maximum(block, 0)
        reached = jnp.where(hit, reached | lax.shift_left(jnp.int32(1), block), reached)
        wanted = jnp.where(hit, parents_ref[block], wanted)
    for other, kv_ref in zip(xors, kv_refs):
        @pl.when((lax.shift_right_logical(reached, me ^ other) & 1) == 1)
        def _():
            absorb(scale, q_ref, kv_ref[0:BLOCK, :], kv_ref[BLOCK:, :], *state)


def absorb_walk(parents_ref, q_ref, piece, state):
    scale = exponent_scale(q_ref.shape[1])
    me = lax.axis_index("ctx")

    def visit(step, wanted):
        block = me - step
        hit = (block >= 0) & (block == wanted)
        block = jnp.maximum(block, 0)

        @pl.when(hit)
        def _():
            start = pl.multiple_of(block * 2 * BLOCK, 2 * BLOCK)
            absorb(scale, q_ref, piece[pl.ds(start, BLOCK), :], piece[pl.ds(start + BLOCK, BLOCK), :], *state)

        return jnp.where(hit, parents_ref[block], wanted)

    lax.fori_loop(1, parents_ref.shape[0], visit, parents_ref[me])


def others_kernel(xors, parents_ref, q_ref, m_in, l_in, acc_in, *refs):
    state = refs[len(xors):]
    absorb_reached(xors, parents_ref, q_ref, refs[:len(xors)], state)


def last_kernel(xors, parents_ref, q_ref, m_in, l_in, acc_in, *refs):
    kv_refs = refs[:max(len(xors), 1)]
    w_ref, att_ref, send_ref, keep_ref, *state = refs[len(kv_refs):]
    rows, head_dim = q_ref.shape
    group = rows // BLOCK
    width = keep_ref.shape[1]
    far = lax.axis_index("tp") ^ 2
    if xors:
        absorb_reached(xors, parents_ref, q_ref, kv_refs, state)
    else:
        absorb_walk(parents_ref, q_ref, kv_refs[0], state)
    m_ref, l_ref, acc_ref = state

    for head in range(group):
        at = slice(head * BLOCK, (head + 1) * BLOCK)
        part = acc_ref[:, at] / l_ref[:, at]
        att_ref[:, head * head_dim:(head + 1) * head_dim] = part.T.astype(jnp.bfloat16)

    att = att_ref[...]
    send_ref[...] = project(att, w_ref, far ^ 1, width).astype(jnp.bfloat16)
    keep_ref[...] = project(att, w_ref, far, width)


def near_kernel(att_ref, w_ref, send_ref, keep_ref):
    mine = lax.axis_index("tp")
    width = keep_ref.shape[1]
    att = att_ref[...]
    send_ref[...] = project(att, w_ref, mine ^ 1, width).astype(jnp.bfloat16)
    keep_ref[...] = project(att, w_ref, mine, width)


def shards(ctx_size, tp_size, query_heads, key_heads, value_heads, parents, out_weight):
    tok_rows, local_heads, head_dim = query_heads.shape
    assert tok_rows == BLOCK and key_heads.shape[1] == 1 and parents.shape[0] == ctx_size and tp_size == 4
    width = out_weight.shape[1] // tp_size
    rows = local_heads * tok_rows
    params = pltpu.CompilerParams(vmem_limit_bytes=VMEM_LIMIT)
    vmem = pl.BlockSpec(memory_space=pltpu.VMEM)
    hbm = pl.BlockSpec(memory_space=pltpu.HBM)
    smem = pl.BlockSpec(memory_space=pltpu.SMEM)

    def in_hbm(x):
        return pltpu.with_memory_space_constraint(x, pltpu.HBM)

    def swap(x, axis, size, other):
        return lax.ppermute(x, axis, [(i, i ^ other) for i in range(size)])

    kv = pl.pallas_call(
        pack_kernel,
        out_shape=jax.ShapeDtypeStruct((2 * tok_rows, head_dim), jnp.bfloat16),
        in_specs=[hbm, hbm],
        out_specs=vmem,
        scratch_shapes=[pltpu.SemaphoreType.DMA((2,))],
        compiler_params=params,
        cost_estimate=pl.CostEstimate(flops=8_000_000_000, bytes_accessed=130_000, transcendentals=0),
    )(in_hbm(key_heads[:, 0, :]), in_hbm(value_heads[:, 0, :]))
    if ctx_size == DIRECT_SIZE:
        columns = [swap(kv, "ctx", ctx_size, other) for other in (4, 2, 6)]
    q = jnp.transpose(query_heads, (1, 0, 2)).reshape(rows, head_dim)

    m, l, acc = pl.pallas_call(
        own_block_kernel,
        out_shape=(
            jax.ShapeDtypeStruct((1, rows), jnp.float32),
            jax.ShapeDtypeStruct((1, rows), jnp.float32),
            jax.ShapeDtypeStruct((head_dim, rows), jnp.float32),
        ),
        in_specs=[vmem, vmem],
        out_specs=(vmem, vmem, vmem),
        compiler_params=params,
        cost_estimate=pl.CostEstimate(flops=67_000_000, bytes_accessed=1_000_000, transcendentals=130_000),
    )(q, kv)

    state = (m, l, acc)
    state_shapes = tuple(jax.ShapeDtypeStruct(x.shape, x.dtype) for x in state)
    if ctx_size == DIRECT_SIZE:
        late, m = lax.optimization_barrier((kv, m))
        state = (m, l, acc)
        beside = swap(late, "ctx", ctx_size, 1)
        pairs = [swap(x, "ctx", ctx_size, 1) for x in columns]

        def absorbed(state, xors, arrived):
            return pl.pallas_call(
                functools.partial(others_kernel, xors),
                out_shape=state_shapes,
                in_specs=[smem] + [vmem] * (4 + len(xors)),
                out_specs=(vmem,) * 3,
                input_output_aliases={2: 0, 3: 1, 4: 2},
                compiler_params=params,
                cost_estimate=pl.CostEstimate(flops=270_000_000, bytes_accessed=1_000_000, transcendentals=500_000),
            )(parents, q, *state, *arrived)

        state = absorbed(state, (4, 2, 6, 1), [*columns, beside])
        state = absorbed(state, (3, 7), pairs[1:])
        xors, pieces = (5,), pairs[:1]
    else:
        xors = ()
        pieces = [lax.all_gather(kv, "ctx", axis=0, tiled=True)]

    att, send_far, keep_far, *_ = pl.pallas_call(
        functools.partial(last_kernel, xors),
        out_shape=(
            jax.ShapeDtypeStruct((tok_rows, local_heads * head_dim), jnp.bfloat16),
            jax.ShapeDtypeStruct((tok_rows, width), jnp.bfloat16),
            jax.ShapeDtypeStruct((tok_rows, width), jnp.float32),
        ) + state_shapes,
        in_specs=[smem] + [vmem] * (5 + len(pieces)),
        out_specs=(vmem,) * 6,
        input_output_aliases={2: 3, 3: 4, 4: 5},
        compiler_params=params,
        cost_estimate=pl.CostEstimate(flops=1_000_000_000, bytes_accessed=10_000_000, transcendentals=1_000_000),
    )(parents, q, *state, *pieces, out_weight)

    far_in = swap(send_far, "tp", tp_size, 1)
    send_near, keep_near = pl.pallas_call(
        near_kernel,
        out_shape=(
            jax.ShapeDtypeStruct((tok_rows, width), jnp.bfloat16),
            jax.ShapeDtypeStruct((tok_rows, width), jnp.float32),
        ),
        in_specs=[vmem, vmem],
        out_specs=(vmem, vmem),
        compiler_params=params,
        cost_estimate=pl.CostEstimate(flops=540_000_000, bytes_accessed=4_000_000, transcendentals=0),
    )(att, out_weight)
    far_sum = (keep_far + far_in.astype(jnp.float32)).astype(jnp.bfloat16)
    from_far = swap(far_sum, "tp", tp_size, 2)
    send_near, _ = lax.optimization_barrier((send_near, far_sum))
    near_in = swap(send_near, "tp", tp_size, 1)
    return (keep_near + near_in.astype(jnp.float32) + from_far.astype(jnp.float32)).astype(jnp.bfloat16)


def solution(mesh):
    return jax.shard_map(
        functools.partial(shards, mesh.shape["ctx"], mesh.shape["tp"]),
        mesh=mesh,
        in_specs=(
            P("ctx", "tp", None),
            P("ctx", "tp", None),
            P("ctx", "tp", None),
            P(),
            P("tp", None),
        ),
        out_specs=P("ctx", "tp"),
        check_vma=False,
    )
```

```python
import functools
import math

import jax
import jax.numpy as jnp
from jax import lax
from jax.experimental import pallas as pl
from jax.experimental.pallas import tpu as pltpu
from jax.sharding import PartitionSpec as P

BLOCK = 128
DIRECT_SIZE = 8
VMEM_LIMIT = 32 * 1024 * 1024


def scores_of(k, q):
    return lax.dot_general(k, q, (((1,), (1,)), ((), ())), preferred_element_type=jnp.float32)


def weighted(v, p):
    return lax.dot_general(v, p.astype(jnp.bfloat16), (((0,), (0,)), ((), ())), preferred_element_type=jnp.float32)


def exponent_scale(head_dim):
    return math.log2(math.e) / math.sqrt(head_dim)


def pack_kernel(k_hbm, v_hbm, kv_ref, sems):
    k_copy = pltpu.make_async_copy(k_hbm, kv_ref.at[0:BLOCK, :], sems.at[0])
    v_copy = pltpu.make_async_copy(v_hbm, kv_ref.at[BLOCK:2 * BLOCK, :], sems.at[1])
    k_copy.start()
    v_copy.start()
    k_copy.wait()
    v_copy.wait()


def reached_mask(parents_ref):
    me = lax.axis_index("ctx")
    wanted = parents_ref[me]
    reached = jnp.int32(0)
    for step in range(1, DIRECT_SIZE):
        block = me - step
        hit = (block >= 0) & (block == wanted)
        block = jnp.maximum(block, 0)
        reached = jnp.where(hit, reached | lax.shift_left(jnp.int32(1), block), reached)
        wanted = jnp.where(hit, parents_ref[block], wanted)
    return reached


def own_block_kernel(parents_ref, q_ref, kv_ref, reached_ref, m_ref, l_ref, acc_ref):
    scale = exponent_scale(q_ref.shape[1])
    s = scores_of(kv_ref[0:BLOCK, :], q_ref[...])
    key_at = lax.broadcasted_iota(jnp.int32, s.shape, 0)
    query_at = lax.broadcasted_iota(jnp.int32, s.shape, 1) & (BLOCK - 1)
    s = jnp.where(key_at <= query_at, s, -1e30)
    m = jnp.max(s, axis=0, keepdims=True)
    p = jnp.exp2((s - m) * scale)
    m_ref[...] = m
    l_ref[...] = jnp.sum(p, axis=0, keepdims=True)
    acc_ref[...] = weighted(kv_ref[BLOCK:, :], p)
    reached_ref[...] = jnp.full(reached_ref.shape, reached_mask(parents_ref), jnp.int32)


def project(att, w_ref, start, width):
    start = pl.multiple_of(start, 128)
    return jnp.dot(att, w_ref[:, pl.ds(start, width)], preferred_element_type=jnp.float32)


def absorb(scale, q_ref, k, v, m_ref, l_ref, acc_ref):
    s = scores_of(k, q_ref[...])
    m_old = m_ref[...]
    m_new = jnp.maximum(m_old, jnp.max(s, axis=0, keepdims=True))
    p = jnp.exp2((s - m_new) * scale)
    factor = jnp.exp2((m_old - m_new) * scale)
    m_ref[...] = m_new
    l_ref[...] = l_ref[...] * factor + jnp.sum(p, axis=0, keepdims=True)
    acc_ref[...] = acc_ref[...] * factor + weighted(v, p)


def absorb_reached(xors, reached_ref, q_ref, kv_refs, state):
    scale = exponent_scale(q_ref.shape[1])
    me = lax.axis_index("ctx")
    reached = jnp.max(reached_ref[...])
    for other, kv_ref in zip(xors, kv_refs):
        @pl.when((lax.shift_right_logical(reached, me ^ other) & 1) == 1)
        def _():
            absorb(scale, q_ref, kv_ref[0:BLOCK, :], kv_ref[BLOCK:, :], *state)


def absorb_walk(parents_ref, q_ref, piece, state):
    scale = exponent_scale(q_ref.shape[1])
    me = lax.axis_index("ctx")

    def visit(step, wanted):
        block = me - step
        hit = (block >= 0) & (block == wanted)
        block = jnp.maximum(block, 0)

        @pl.when(hit)
        def _():
            start = pl.multiple_of(block * 2 * BLOCK, 2 * BLOCK)
            absorb(scale, q_ref, piece[pl.ds(start, BLOCK), :], piece[pl.ds(start + BLOCK, BLOCK), :], *state)

        return jnp.where(hit, parents_ref[block], wanted)

    lax.fori_loop(1, parents_ref.shape[0], visit, parents_ref[me])


def others_kernel(xors, reached_ref, q_ref, m_in, l_in, acc_in, *refs):
    state = refs[len(xors):]
    absorb_reached(xors, reached_ref, q_ref, refs[:len(xors)], state)


def last_kernel(xors, tree_ref, q_ref, m_in, l_in, acc_in, *refs):
    kv_refs = refs[:max(len(xors), 1)]
    w_ref, att_ref, send_ref, keep_ref, *state = refs[len(kv_refs):]
    rows, head_dim = q_ref.shape
    if xors:
        absorb_reached(xors, tree_ref, q_ref, kv_refs, state)
    else:
        absorb_walk(tree_ref, q_ref, kv_refs[0], state)
    m_ref, l_ref, acc_ref = state

    for head in range(rows // BLOCK):
        at = slice(head * BLOCK, (head + 1) * BLOCK)
        part = acc_ref[:, at] / l_ref[:, at]
        att_ref[:, head * head_dim:(head + 1) * head_dim] = part.T.astype(jnp.bfloat16)

    project_pair(2, 0, att_ref, w_ref, send_ref, keep_ref)


def project_pair(flip, half, att_ref, w_ref, send_ref, keep_ref):
    target = lax.axis_index("tp") ^ flip
    width = w_ref.shape[1] // 4
    cols = keep_ref.shape[1]
    att = att_ref[...]
    send_ref[...] = project(att, w_ref, (target ^ 1) * width + half * cols, cols).astype(jnp.bfloat16)
    keep_ref[...] = project(att, w_ref, target * width + half * cols, cols)


def shards(ctx_size, tp_size, query_heads, key_heads, value_heads, parents, out_weight):
    tok_rows, local_heads, head_dim = query_heads.shape
    assert tok_rows == BLOCK and key_heads.shape[1] == 1 and parents.shape[0] == ctx_size and tp_size == 4
    width = out_weight.shape[1] // tp_size
    rows = local_heads * tok_rows
    params = pltpu.CompilerParams(vmem_limit_bytes=VMEM_LIMIT)
    vmem = pl.BlockSpec(memory_space=pltpu.VMEM)
    hbm = pl.BlockSpec(memory_space=pltpu.HBM)
    smem = pl.BlockSpec(memory_space=pltpu.SMEM)

    def in_hbm(x):
        return pltpu.with_memory_space_constraint(x, pltpu.HBM)

    def swap(x, axis, size, other):
        return lax.ppermute(x, axis, [(i, i ^ other) for i in range(size)])

    kv = pl.pallas_call(
        pack_kernel,
        out_shape=jax.ShapeDtypeStruct((2 * tok_rows, head_dim), jnp.bfloat16),
        in_specs=[hbm, hbm],
        out_specs=vmem,
        scratch_shapes=[pltpu.SemaphoreType.DMA((2,))],
        compiler_params=params,
        cost_estimate=pl.CostEstimate(flops=8_000_000_000, bytes_accessed=130_000, transcendentals=0),
    )(in_hbm(key_heads[:, 0, :]), in_hbm(value_heads[:, 0, :]))
    if ctx_size == DIRECT_SIZE:
        columns = [swap(kv, "ctx", ctx_size, other) for other in (4, 2, 6)]
    q = jnp.transpose(query_heads, (1, 0, 2)).reshape(rows, head_dim)

    reached, m, l, acc = pl.pallas_call(
        own_block_kernel,
        out_shape=(
            jax.ShapeDtypeStruct((8, 128), jnp.int32),
            jax.ShapeDtypeStruct((1, rows), jnp.float32),
            jax.ShapeDtypeStruct((1, rows), jnp.float32),
            jax.ShapeDtypeStruct((head_dim, rows), jnp.float32),
        ),
        in_specs=[smem, vmem, vmem],
        out_specs=(vmem,) * 4,
        compiler_params=params,
        cost_estimate=pl.CostEstimate(flops=67_000_000, bytes_accessed=1_000_000, transcendentals=130_000),
    )(parents, q, kv)

    if ctx_size == DIRECT_SIZE:
        late, m = lax.optimization_barrier((kv, m))
        beside = swap(late, "ctx", ctx_size, 1)
    state = (m, l, acc)
    state_shapes = tuple(jax.ShapeDtypeStruct(x.shape, x.dtype) for x in state)
    if ctx_size == DIRECT_SIZE:
        late, m = lax.optimization_barrier((kv, m))
        state = (m, l, acc)
        beside = swap(late, "ctx", ctx_size, 1)
        pairs = [swap(x, "ctx", ctx_size, 1) for x in columns]

        def absorbed(state, xors, arrived):
            return pl.pallas_call(
                functools.partial(others_kernel, xors),
                out_shape=state_shapes,
                in_specs=[vmem] * (5 + len(xors)),
                out_specs=(vmem,) * 3,
                input_output_aliases={2: 0, 3: 1, 4: 2},
                compiler_params=params,
                cost_estimate=pl.CostEstimate(flops=270_000_000, bytes_accessed=1_000_000, transcendentals=500_000),
            )(reached, q, *state, *arrived)

        state = absorbed(state, (4, 2, 6, 1), [*columns, beside])
        state = absorbed(state, (3, 7), pairs[1:])
        xors, pieces, tree, tree_spec = (5,), pairs[:1], reached, vmem
    else:
        xors, pieces, tree, tree_spec = (), [lax.all_gather(kv, "ctx", axis=0, tiled=True)], parents, smem

    half = width // 2
    pair_shapes = (
        jax.ShapeDtypeStruct((tok_rows, half), jnp.bfloat16),
        jax.ShapeDtypeStruct((tok_rows, half), jnp.float32),
    )
    att, send_a, keep_a, *_ = pl.pallas_call(
        functools.partial(last_kernel, xors),
        out_shape=(jax.ShapeDtypeStruct((tok_rows, local_heads * head_dim), jnp.bfloat16),) + pair_shapes + state_shapes,
        in_specs=[tree_spec] + [vmem] * (5 + len(pieces)),
        out_specs=(vmem,) * 6,
        input_output_aliases={2: 3, 3: 4, 4: 5},
        compiler_params=params,
        cost_estimate=pl.CostEstimate(flops=1_000_000_000, bytes_accessed=10_000_000, transcendentals=1_000_000),
    )(tree, q, *state, *pieces, out_weight)

    def projected(flip, part, shapes, att):
        return pl.pallas_call(
            functools.partial(project_pair, flip, part),
            out_shape=shapes,
            in_specs=[vmem, vmem],
            out_specs=(vmem, vmem),
            compiler_params=params,
            cost_estimate=pl.CostEstimate(flops=540_000_000, bytes_accessed=4_000_000, transcendentals=0),
        )(att, out_weight)

    def added(keep, arrived):
        return (keep + arrived.astype(jnp.float32)).astype(jnp.bfloat16)

    in_a = swap(send_a, "tp", tp_size, 1)
    send_b, keep_b = projected(2, 1, pair_shapes, att)
    in_b = swap(send_b, "tp", tp_size, 1)
    far_a = added(keep_a, in_a)
    from_a = swap(far_a, "tp", tp_size, 2)
    far_b = added(keep_b, in_b)
    from_b = swap(far_b, "tp", tp_size, 2)
    att, _ = lax.optimization_barrier((att, far_a))
    send_near, keep_near = projected(
        0,
        0,
        (jax.ShapeDtypeStruct((tok_rows, width), jnp.bfloat16), jax.ShapeDtypeStruct((tok_rows, width), jnp.float32)),
        att,
    )
    near_in = swap(send_near, "tp", tp_size, 1)
    from_far = jnp.concatenate([from_a, from_b], axis=1).astype(jnp.float32)
    return (keep_near + near_in.astype(jnp.float32) + from_far).astype(jnp.bfloat16)


def solution(mesh):
    return jax.shard_map(
        functools.partial(shards, mesh.shape["ctx"], mesh.shape["tp"]),
        mesh=mesh,
        in_specs=(
            P("ctx", "tp", None),
            P("ctx", "tp", None),
            P("ctx", "tp", None),
            P(),
            P("tp", None),
        ),
        out_specs=P("ctx", "tp"),
        check_vma=False,
    )
```

```python
import functools
import math

import jax
import jax.numpy as jnp
from jax import lax
from jax.experimental import pallas as pl
from jax.experimental.pallas import tpu as pltpu
from jax.sharding import PartitionSpec as P

BLOCK = 128
DIRECT_SIZE = 8
VMEM_LIMIT = 32 * 1024 * 1024


def scores_of(k, q):
    return lax.dot_general(k, q, (((1,), (1,)), ((), ())), preferred_element_type=jnp.float32)


def weighted(v, p):
    return lax.dot_general(v, p.astype(jnp.bfloat16), (((0,), (0,)), ((), ())), preferred_element_type=jnp.float32)


def exponent_scale(head_dim):
    return math.log2(math.e) / math.sqrt(head_dim)


def reached_mask(parents_ref):
    me = lax.axis_index("ctx")
    wanted = parents_ref[me]
    reached = jnp.int32(0)
    for step in range(1, DIRECT_SIZE):
        block = me - step
        hit = (block >= 0) & (block == wanted)
        block = jnp.maximum(block, 0)
        reached = jnp.where(hit, reached | lax.shift_left(jnp.int32(1), block), reached)
        wanted = jnp.where(hit, parents_ref[block], wanted)
    return reached


def pack_kernel(walk, k_hbm, v_hbm, parents_hbm, kv_ref, reached_ref, parents_ref, sems):
    copies = [
        pltpu.make_async_copy(parents_hbm, parents_ref, sems.at[0]),
        pltpu.make_async_copy(k_hbm, kv_ref.at[0:BLOCK, :], sems.at[1]),
        pltpu.make_async_copy(v_hbm, kv_ref.at[BLOCK:2 * BLOCK, :], sems.at[2]),
    ]
    for copy in copies:
        copy.start()
    copies[0].wait()
    reached = reached_mask(parents_ref) if walk else jnp.int32(0)
    reached_ref[...] = jnp.full(reached_ref.shape, reached, jnp.int32)
    copies[1].wait()
    copies[2].wait()


def project(att, w_ref, start, width):
    start = pl.multiple_of(start, 128)
    return jnp.dot(att, w_ref[:, pl.ds(start, width)], preferred_element_type=jnp.float32)


def absorb(scale, q_ref, k, v, m_ref, l_ref, acc_ref):
    s = scores_of(k, q_ref[...])
    m_old = m_ref[...]
    m_new = jnp.maximum(m_old, jnp.max(s, axis=0, keepdims=True))
    p = jnp.exp2((s - m_new) * scale)
    factor = jnp.exp2((m_old - m_new) * scale)
    m_ref[...] = m_new
    l_ref[...] = l_ref[...] * factor + jnp.sum(p, axis=0, keepdims=True)
    acc_ref[...] = acc_ref[...] * factor + weighted(v, p)


def absorb_reached(xors, reached_ref, q_ref, kv_refs, state):
    scale = exponent_scale(q_ref.shape[1])
    me = lax.axis_index("ctx")
    reached = jnp.max(reached_ref[...])
    for other, kv_ref in zip(xors, kv_refs):
        @pl.when((lax.shift_right_logical(reached, me ^ other) & 1) == 1)
        def _():
            absorb(scale, q_ref, kv_ref[0:BLOCK, :], kv_ref[BLOCK:, :], *state)


def absorb_walk(parents_ref, q_ref, piece, state):
    scale = exponent_scale(q_ref.shape[1])
    me = lax.axis_index("ctx")

    def visit(step, wanted):
        block = me - step
        hit = (block >= 0) & (block == wanted)
        block = jnp.maximum(block, 0)

        @pl.when(hit)
        def _():
            start = pl.multiple_of(block * 2 * BLOCK, 2 * BLOCK)
            absorb(scale, q_ref, piece[pl.ds(start, BLOCK), :], piece[pl.ds(start + BLOCK, BLOCK), :], *state)

        return jnp.where(hit, parents_ref[block], wanted)

    lax.fori_loop(1, parents_ref.shape[0], visit, parents_ref[me])


def own_block_kernel(xors, reached_ref, q_ref, kv_ref, *refs):
    state = refs[len(xors):]
    m_ref, l_ref, acc_ref = state
    scale = exponent_scale(q_ref.shape[1])
    s = scores_of(kv_ref[0:BLOCK, :], q_ref[...])
    key_at = lax.broadcasted_iota(jnp.int32, s.shape, 0)
    query_at = lax.broadcasted_iota(jnp.int32, s.shape, 1) & (BLOCK - 1)
    s = jnp.where(key_at <= query_at, s, -1e30)
    m = jnp.max(s, axis=0, keepdims=True)
    p = jnp.exp2((s - m) * scale)
    m_ref[...] = m
    l_ref[...] = jnp.sum(p, axis=0, keepdims=True)
    acc_ref[...] = weighted(kv_ref[BLOCK:, :], p)
    absorb_reached(xors, reached_ref, q_ref, refs[:len(xors)], state)


def others_kernel(xors, reached_ref, q_ref, m_in, l_in, acc_in, *refs):
    state = refs[len(xors):]
    absorb_reached(xors, reached_ref, q_ref, refs[:len(xors)], state)


def last_kernel(xors, tree_ref, q_ref, m_in, l_in, acc_in, *refs):
    kv_refs = refs[:max(len(xors), 1)]
    w_ref, att_ref, send_ref, keep_ref, *state = refs[len(kv_refs):]
    rows, head_dim = q_ref.shape
    if xors:
        absorb_reached(xors, tree_ref, q_ref, kv_refs, state)
    else:
        absorb_walk(tree_ref, q_ref, kv_refs[0], state)
    m_ref, l_ref, acc_ref = state

    for head in range(rows // BLOCK):
        at = slice(head * BLOCK, (head + 1) * BLOCK)
        part = acc_ref[:, at] / l_ref[:, at]
        att_ref[:, head * head_dim:(head + 1) * head_dim] = part.T.astype(jnp.bfloat16)

    project_pair(2, 0, att_ref, w_ref, send_ref, keep_ref)


def project_pair(flip, half, att_ref, w_ref, send_ref, keep_ref):
    target = lax.axis_index("tp") ^ flip
    width = w_ref.shape[1] // 4
    cols = keep_ref.shape[1]
    att = att_ref[...]
    send_ref[...] = project(att, w_ref, (target ^ 1) * width + half * cols, cols).astype(jnp.bfloat16)
    keep_ref[...] = project(att, w_ref, target * width + half * cols, cols)


def shards(ctx_size, tp_size, query_heads, key_heads, value_heads, parents, out_weight):
    tok_rows, local_heads, head_dim = query_heads.shape
    assert tok_rows == BLOCK and key_heads.shape[1] == 1 and parents.shape[0] == ctx_size and tp_size == 4
    width = out_weight.shape[1] // tp_size
    rows = local_heads * tok_rows
    params = pltpu.CompilerParams(vmem_limit_bytes=VMEM_LIMIT)
    vmem = pl.BlockSpec(memory_space=pltpu.VMEM)
    hbm = pl.BlockSpec(memory_space=pltpu.HBM)
    smem = pl.BlockSpec(memory_space=pltpu.SMEM)

    def in_hbm(x):
        return pltpu.with_memory_space_constraint(x, pltpu.HBM)

    def swap(x, axis, size, other):
        return lax.ppermute(x, axis, [(i, i ^ other) for i in range(size)])

    kv, reached = pl.pallas_call(
        functools.partial(pack_kernel, ctx_size == DIRECT_SIZE),
        out_shape=(
            jax.ShapeDtypeStruct((2 * tok_rows, head_dim), jnp.bfloat16),
            jax.ShapeDtypeStruct((8, 128), jnp.int32),
        ),
        in_specs=[hbm, hbm, hbm],
        out_specs=(vmem, vmem),
        scratch_shapes=[pltpu.SMEM(parents.shape, jnp.int32), pltpu.SemaphoreType.DMA((3,))],
        compiler_params=params,
        cost_estimate=pl.CostEstimate(flops=8_000_000_000, bytes_accessed=130_000, transcendentals=0),
    )(in_hbm(key_heads[:, 0, :]), in_hbm(value_heads[:, 0, :]), in_hbm(parents))
    early = []
    if ctx_size == DIRECT_SIZE:
        columns = [swap(kv, "ctx", ctx_size, other) for other in (4, 2, 6)]
        early = [swap(kv, "ctx", ctx_size, 1)]
    q = jnp.transpose(query_heads, (1, 0, 2)).reshape(rows, head_dim)

    m, l, acc = pl.pallas_call(
        functools.partial(own_block_kernel, (1,) * len(early)),
        out_shape=(
            jax.ShapeDtypeStruct((1, rows), jnp.float32),
            jax.ShapeDtypeStruct((1, rows), jnp.float32),
            jax.ShapeDtypeStruct((head_dim, rows), jnp.float32),
        ),
        in_specs=[vmem] * (3 + len(early)),
        out_specs=(vmem,) * 3,
        compiler_params=params,
        cost_estimate=pl.CostEstimate(flops=130_000_000, bytes_accessed=1_000_000, transcendentals=260_000),
    )(reached, q, kv, *early)

    if ctx_size == DIRECT_SIZE:
        columns[0], m = lax.optimization_barrier((columns[0], m))
    state = (m, l, acc)
    state_shapes = tuple(jax.ShapeDtypeStruct(x.shape, x.dtype) for x in state)
    if ctx_size == DIRECT_SIZE:
        late, m = lax.optimization_barrier((kv, m))
        state = (m, l, acc)
        beside = swap(late, "ctx", ctx_size, 1)
        pairs = [swap(x, "ctx", ctx_size, 1) for x in columns]

        def absorbed(state, xors, arrived):
            return pl.pallas_call(
                functools.partial(others_kernel, xors),
                out_shape=state_shapes,
                in_specs=[vmem] * (5 + len(xors)),
                out_specs=(vmem,) * 3,
                input_output_aliases={2: 0, 3: 1, 4: 2},
                compiler_params=params,
                cost_estimate=pl.CostEstimate(flops=270_000_000, bytes_accessed=1_000_000, transcendentals=500_000),
            )(reached, q, *state, *arrived)

        state = absorbed(state, (4, 2, 6), columns)
        state = absorbed(state, (3, 7), pairs[1:])
        xors, pieces, tree, tree_spec = (5,), pairs[:1], reached, vmem
    else:
        xors, pieces, tree, tree_spec = (), [lax.all_gather(kv, "ctx", axis=0, tiled=True)], parents, smem

    half = width // 2
    pair_shapes = (
        jax.ShapeDtypeStruct((tok_rows, half), jnp.bfloat16),
        jax.ShapeDtypeStruct((tok_rows, half), jnp.float32),
    )
    att, send_a, keep_a, *_ = pl.pallas_call(
        functools.partial(last_kernel, xors),
        out_shape=(jax.ShapeDtypeStruct((tok_rows, local_heads * head_dim), jnp.bfloat16),) + pair_shapes + state_shapes,
        in_specs=[tree_spec] + [vmem] * (5 + len(pieces)),
        out_specs=(vmem,) * 6,
        input_output_aliases={2: 3, 3: 4, 4: 5},
        compiler_params=params,
        cost_estimate=pl.CostEstimate(flops=1_000_000_000, bytes_accessed=10_000_000, transcendentals=1_000_000),
    )(tree, q, *state, *pieces, out_weight)

    def projected(flip, part, shapes, att):
        return pl.pallas_call(
            functools.partial(project_pair, flip, part),
            out_shape=shapes,
            in_specs=[vmem, vmem],
            out_specs=(vmem, vmem),
            compiler_params=params,
            cost_estimate=pl.CostEstimate(flops=540_000_000, bytes_accessed=4_000_000, transcendentals=0),
        )(att, out_weight)

    def added(keep, arrived):
        return (keep + arrived.astype(jnp.float32)).astype(jnp.bfloat16)

    in_a = swap(send_a, "tp", tp_size, 1)
    send_b, keep_b = projected(2, 1, pair_shapes, att)
    in_b = swap(send_b, "tp", tp_size, 1)
    far_a = added(keep_a, in_a)
    from_a = swap(far_a, "tp", tp_size, 2)
    far_b = added(keep_b, in_b)
    from_b = swap(far_b, "tp", tp_size, 2)
    att, _ = lax.optimization_barrier((att, far_a))
    send_near, keep_near = projected(
        0,
        0,
        (jax.ShapeDtypeStruct((tok_rows, width), jnp.bfloat16), jax.ShapeDtypeStruct((tok_rows, width), jnp.float32)),
        att,
    )
    near_in = swap(send_near, "tp", tp_size, 1)
    from_far = jnp.concatenate([from_a, from_b], axis=1).astype(jnp.float32)
    return (keep_near + near_in.astype(jnp.float32) + from_far).astype(jnp.bfloat16)


def solution(mesh):
    return jax.shard_map(
        functools.partial(shards, mesh.shape["ctx"], mesh.shape["tp"]),
        mesh=mesh,
        in_specs=(
            P("ctx", "tp", None),
            P("ctx", "tp", None),
            P("ctx", "tp", None),
            P(),
            P("tp", None),
        ),
        out_specs=P("ctx", "tp"),
        check_vma=False,
    )
```

```python
import functools
import math

import jax
import jax.numpy as jnp
from jax import lax
from jax.experimental import pallas as pl
from jax.experimental.pallas import tpu as pltpu
from jax.sharding import PartitionSpec as P

BLOCK = 128
DIRECT_SIZE = 8
VMEM_LIMIT = 32 * 1024 * 1024


def scores_of(k, q):
    return lax.dot_general(k, q, (((1,), (1,)), ((), ())), preferred_element_type=jnp.float32)


def weighted(v, p):
    return lax.dot_general(v, p.astype(jnp.bfloat16), (((0,), (0,)), ((), ())), preferred_element_type=jnp.float32)


def exponent_scale(head_dim):
    return math.log2(math.e) / math.sqrt(head_dim)


def reached_mask(parents_ref):
    me = lax.axis_index("ctx")
    wanted = parents_ref[me]
    reached = jnp.int32(0)
    for step in range(1, DIRECT_SIZE):
        block = me - step
        hit = (block >= 0) & (block == wanted)
        block = jnp.maximum(block, 0)
        reached = jnp.where(hit, reached | lax.shift_left(jnp.int32(1), block), reached)
        wanted = jnp.where(hit, parents_ref[block], wanted)
    return reached


def pack_kernel(walk, k_hbm, v_hbm, parents_hbm, kv_ref, reached_ref, parents_ref, sems):
    copies = [
        pltpu.make_async_copy(parents_hbm, parents_ref, sems.at[0]),
        pltpu.make_async_copy(k_hbm, kv_ref.at[0:BLOCK, :], sems.at[1]),
        pltpu.make_async_copy(v_hbm, kv_ref.at[BLOCK:2 * BLOCK, :], sems.at[2]),
    ]
    for copy in copies:
        copy.start()
    copies[0].wait()
    reached = reached_mask(parents_ref) if walk else jnp.int32(0)
    reached_ref[...] = jnp.full(reached_ref.shape, reached, jnp.int32)
    copies[1].wait()
    copies[2].wait()


def project(att, w_ref, start, width):
    start = pl.multiple_of(start, 128)
    return jnp.dot(att, w_ref[:, pl.ds(start, width)], preferred_element_type=jnp.float32)


def absorb(scale, q_ref, k, v, m_ref, l_ref, acc_ref):
    s = scores_of(k, q_ref[...])
    m_old = m_ref[...]
    m_new = jnp.maximum(m_old, jnp.max(s, axis=0, keepdims=True))
    p = jnp.exp2((s - m_new) * scale)
    factor = jnp.exp2((m_old - m_new) * scale)
    m_ref[...] = m_new
    l_ref[...] = l_ref[...] * factor + jnp.sum(p, axis=0, keepdims=True)
    acc_ref[...] = acc_ref[...] * factor + weighted(v, p)


def absorb_reached(xors, reached_ref, q_ref, kv_refs, state):
    scale = exponent_scale(q_ref.shape[1])
    me = lax.axis_index("ctx")
    reached = jnp.max(reached_ref[...])
    for other, kv_ref in zip(xors, kv_refs):
        @pl.when((lax.shift_right_logical(reached, me ^ other) & 1) == 1)
        def _():
            absorb(scale, q_ref, kv_ref[0:BLOCK, :], kv_ref[BLOCK:, :], *state)


def absorb_walk(parents_ref, q_ref, piece, state):
    scale = exponent_scale(q_ref.shape[1])
    me = lax.axis_index("ctx")

    def visit(step, wanted):
        block = me - step
        hit = (block >= 0) & (block == wanted)
        block = jnp.maximum(block, 0)

        @pl.when(hit)
        def _():
            start = pl.multiple_of(block * 2 * BLOCK, 2 * BLOCK)
            absorb(scale, q_ref, piece[pl.ds(start, BLOCK), :], piece[pl.ds(start + BLOCK, BLOCK), :], *state)

        return jnp.where(hit, parents_ref[block], wanted)

    lax.fori_loop(1, parents_ref.shape[0], visit, parents_ref[me])


def own_block_kernel(xors, reached_ref, q_ref, kv_ref, *refs):
    state = refs[len(xors):]
    m_ref, l_ref, acc_ref = state
    scale = exponent_scale(q_ref.shape[1])
    s = scores_of(kv_ref[0:BLOCK, :], q_ref[...])
    key_at = lax.broadcasted_iota(jnp.int32, s.shape, 0)
    query_at = lax.broadcasted_iota(jnp.int32, s.shape, 1) & (BLOCK - 1)
    s = jnp.where(key_at <= query_at, s, -1e30)
    m = jnp.max(s, axis=0, keepdims=True)
    p = jnp.exp2((s - m) * scale)
    m_ref[...] = m
    l_ref[...] = jnp.sum(p, axis=0, keepdims=True)
    acc_ref[...] = weighted(kv_ref[BLOCK:, :], p)
    absorb_reached(xors, reached_ref, q_ref, refs[:len(xors)], state)


def others_kernel(xors, reached_ref, q_ref, m_in, l_in, acc_in, *refs):
    state = refs[len(xors):]
    absorb_reached(xors, reached_ref, q_ref, refs[:len(xors)], state)


def last_kernel(xors, tree_ref, q_ref, m_in, l_in, acc_in, *refs):
    kv_refs = refs[:max(len(xors), 1)]
    w_ref, att_ref, send_ref, keep_ref, *state = refs[len(kv_refs):]
    rows, head_dim = q_ref.shape
    if xors:
        absorb_reached(xors, tree_ref, q_ref, kv_refs, state)
    else:
        absorb_walk(tree_ref, q_ref, kv_refs[0], state)
    m_ref, l_ref, acc_ref = state

    for head in range(rows // BLOCK):
        at = slice(head * BLOCK, (head + 1) * BLOCK)
        part = acc_ref[:, at] / l_ref[:, at]
        att_ref[:, head * head_dim:(head + 1) * head_dim] = part.T.astype(jnp.bfloat16)

    project_pair(2, 0, att_ref, w_ref, send_ref, keep_ref)


def project_pair(flip, half, att_ref, w_ref, send_ref, keep_ref):
    target = lax.axis_index("tp") ^ flip
    width = w_ref.shape[1] // 4
    cols = keep_ref.shape[1]
    att = att_ref[...]
    send_ref[...] = project(att, w_ref, (target ^ 1) * width + half * cols, cols).astype(jnp.bfloat16)
    keep_ref[...] = project(att, w_ref, target * width + half * cols, cols)


def shards(ctx_size, tp_size, query_heads, key_heads, value_heads, parents, out_weight):
    tok_rows, local_heads, head_dim = query_heads.shape
    assert tok_rows == BLOCK and key_heads.shape[1] == 1 and parents.shape[0] == ctx_size and tp_size == 4
    width = out_weight.shape[1] // tp_size
    rows = local_heads * tok_rows
    params = pltpu.CompilerParams(vmem_limit_bytes=VMEM_LIMIT)
    vmem = pl.BlockSpec(memory_space=pltpu.VMEM)
    hbm = pl.BlockSpec(memory_space=pltpu.HBM)
    smem = pl.BlockSpec(memory_space=pltpu.SMEM)

    def in_hbm(x):
        return pltpu.with_memory_space_constraint(x, pltpu.HBM)

    def swap(x, axis, size, other):
        return lax.ppermute(x, axis, [(i, i ^ other) for i in range(size)])

    kv, reached = pl.pallas_call(
        functools.partial(pack_kernel, ctx_size == DIRECT_SIZE),
        out_shape=(
            jax.ShapeDtypeStruct((2 * tok_rows, head_dim), jnp.bfloat16),
            jax.ShapeDtypeStruct((8, 128), jnp.int32),
        ),
        in_specs=[hbm, hbm, hbm],
        out_specs=(vmem, vmem),
        scratch_shapes=[pltpu.SMEM(parents.shape, jnp.int32), pltpu.SemaphoreType.DMA((3,))],
        compiler_params=params,
        cost_estimate=pl.CostEstimate(flops=8_000_000_000, bytes_accessed=130_000, transcendentals=0),
    )(in_hbm(key_heads[:, 0, :]), in_hbm(value_heads[:, 0, :]), in_hbm(parents))
    if ctx_size == DIRECT_SIZE:
        columns = [swap(kv, "ctx", ctx_size, other) for other in (4, 2, 6)]
        beside = swap(kv, "ctx", ctx_size, 1)
        pairs = [swap(x, "ctx", ctx_size, 1) for x in columns]
        early, early_xors = [beside, *columns], (1, 4, 2, 6)
    else:
        early, early_xors = [], ()
    q = jnp.transpose(query_heads, (1, 0, 2)).reshape(rows, head_dim)

    m, l, acc = pl.pallas_call(
        functools.partial(own_block_kernel, early_xors),
        out_shape=(
            jax.ShapeDtypeStruct((1, rows), jnp.float32),
            jax.ShapeDtypeStruct((1, rows), jnp.float32),
            jax.ShapeDtypeStruct((head_dim, rows), jnp.float32),
        ),
        in_specs=[vmem] * (3 + len(early)),
        out_specs=(vmem,) * 3,
        compiler_params=params,
        cost_estimate=pl.CostEstimate(flops=130_000_000, bytes_accessed=1_000_000, transcendentals=260_000),
    )(reached, q, kv, *early)

    state = (m, l, acc)
    state_shapes = tuple(jax.ShapeDtypeStruct(x.shape, x.dtype) for x in state)
    if ctx_size == DIRECT_SIZE:
        def absorbed(state, xors, arrived):
            return pl.pallas_call(
                functools.partial(others_kernel, xors),
                out_shape=state_shapes,
                in_specs=[vmem] * (5 + len(xors)),
                out_specs=(vmem,) * 3,
                input_output_aliases={2: 0, 3: 1, 4: 2},
                compiler_params=params,
                cost_estimate=pl.CostEstimate(flops=270_000_000, bytes_accessed=1_000_000, transcendentals=500_000),
            )(reached, q, *state, *arrived)

        state = absorbed(state, (3, 7), pairs[1:])
        xors, pieces, tree, tree_spec = (5,), pairs[:1], reached, vmem
    else:
        xors, pieces, tree, tree_spec = (), [lax.all_gather(kv, "ctx", axis=0, tiled=True)], parents, smem

    half = width // 2
    pair_shapes = (
        jax.ShapeDtypeStruct((tok_rows, half), jnp.bfloat16),
        jax.ShapeDtypeStruct((tok_rows, half), jnp.float32),
    )
    att, send_a, keep_a, *_ = pl.pallas_call(
        functools.partial(last_kernel, xors),
        out_shape=(jax.ShapeDtypeStruct((tok_rows, local_heads * head_dim), jnp.bfloat16),) + pair_shapes + state_shapes,
        in_specs=[tree_spec] + [vmem] * (5 + len(pieces)),
        out_specs=(vmem,) * 6,
        input_output_aliases={2: 3, 3: 4, 4: 5},
        compiler_params=params,
        cost_estimate=pl.CostEstimate(flops=1_000_000_000, bytes_accessed=10_000_000, transcendentals=1_000_000),
    )(tree, q, *state, *pieces, out_weight)

    def projected(flip, part, shapes, att):
        return pl.pallas_call(
            functools.partial(project_pair, flip, part),
            out_shape=shapes,
            in_specs=[vmem, vmem],
            out_specs=(vmem, vmem),
            compiler_params=params,
            cost_estimate=pl.CostEstimate(flops=540_000_000, bytes_accessed=4_000_000, transcendentals=0),
        )(att, out_weight)

    def added(keep, arrived):
        return (keep + arrived.astype(jnp.float32)).astype(jnp.bfloat16)

    in_a = swap(send_a, "tp", tp_size, 1)
    send_b, keep_b = projected(2, 1, pair_shapes, att)
    in_b = swap(send_b, "tp", tp_size, 1)
    far_a = added(keep_a, in_a)
    from_a = swap(far_a, "tp", tp_size, 2)
    far_b = added(keep_b, in_b)
    from_b = swap(far_b, "tp", tp_size, 2)
    att, _ = lax.optimization_barrier((att, far_a))
    send_near, keep_near = projected(
        0,
        0,
        (jax.ShapeDtypeStruct((tok_rows, width), jnp.bfloat16), jax.ShapeDtypeStruct((tok_rows, width), jnp.float32)),
        att,
    )
    near_in = swap(send_near, "tp", tp_size, 1)
    from_far = jnp.concatenate([from_a, from_b], axis=1).astype(jnp.float32)
    return (keep_near + near_in.astype(jnp.float32) + from_far).astype(jnp.bfloat16)


def solution(mesh):
    return jax.shard_map(
        functools.partial(shards, mesh.shape["ctx"], mesh.shape["tp"]),
        mesh=mesh,
        in_specs=(
            P("ctx", "tp", None),
            P("ctx", "tp", None),
            P("ctx", "tp", None),
            P(),
            P("tp", None),
        ),
        out_specs=P("ctx", "tp"),
        check_vma=False,
    )
```

```python
import functools
import math

import jax
import jax.numpy as jnp
from jax import lax
from jax.experimental import pallas as pl
from jax.experimental.pallas import tpu as pltpu
from jax.sharding import PartitionSpec as P

BLOCK = 128
DIRECT_SIZE = 8
VMEM_LIMIT = 32 * 1024 * 1024


def scores_of(k, q):
    return lax.dot_general(k, q, (((1,), (1,)), ((), ())), preferred_element_type=jnp.float32)


def weighted(v, p):
    return lax.dot_general(v, p.astype(jnp.bfloat16), (((0,), (0,)), ((), ())), preferred_element_type=jnp.float32)


def exponent_scale(head_dim):
    return math.log2(math.e) / math.sqrt(head_dim)


def reached_mask(parents_ref):
    me = lax.axis_index("ctx")
    wanted = parents_ref[me]
    reached = jnp.int32(0)
    for step in range(1, DIRECT_SIZE):
        block = me - step
        hit = (block >= 0) & (block == wanted)
        block = jnp.maximum(block, 0)
        reached = jnp.where(hit, reached | lax.shift_left(jnp.int32(1), block), reached)
        wanted = jnp.where(hit, parents_ref[block], wanted)
    return reached


def pack_kernel(walk, k_hbm, v_hbm, parents_hbm, kv_ref, reached_ref, parents_ref, sems):
    copies = [
        pltpu.make_async_copy(parents_hbm, parents_ref, sems.at[0]),
        pltpu.make_async_copy(k_hbm, kv_ref.at[0:BLOCK, :], sems.at[1]),
        pltpu.make_async_copy(v_hbm, kv_ref.at[BLOCK:2 * BLOCK, :], sems.at[2]),
    ]
    for copy in copies:
        copy.start()
    copies[0].wait()
    reached = reached_mask(parents_ref) if walk else jnp.int32(0)
    reached_ref[...] = jnp.full(reached_ref.shape, reached, jnp.int32)
    copies[1].wait()
    copies[2].wait()


def project(att, w_ref, start, width):
    start = pl.multiple_of(start, 128)
    return jnp.dot(att, w_ref[:, pl.ds(start, width)], preferred_element_type=jnp.float32)


def absorb(scale, q_ref, k, v, m_ref, l_ref, acc_ref):
    s = scores_of(k, q_ref[...])
    m_old = m_ref[...]
    m_new = jnp.maximum(m_old, jnp.max(s, axis=0, keepdims=True))
    p = jnp.exp2((s - m_new) * scale)
    factor = jnp.exp2((m_old - m_new) * scale)
    m_ref[...] = m_new
    l_ref[...] = l_ref[...] * factor + jnp.sum(p, axis=0, keepdims=True)
    acc_ref[...] = acc_ref[...] * factor + weighted(v, p)


def absorb_reached(xors, reached_ref, q_ref, kv_refs, state):
    scale = exponent_scale(q_ref.shape[1])
    me = lax.axis_index("ctx")
    reached = jnp.max(reached_ref[...])
    for others, kv_ref in zip(xors, kv_refs):
        for at, other in enumerate(others):
            keys = slice(2 * at * BLOCK, (2 * at + 1) * BLOCK)
            values = slice((2 * at + 1) * BLOCK, (2 * at + 2) * BLOCK)

            @pl.when((lax.shift_right_logical(reached, me ^ other) & 1) == 1)
            def _():
                absorb(scale, q_ref, kv_ref[keys, :], kv_ref[values, :], *state)


def absorb_walk(parents_ref, q_ref, piece, state):
    scale = exponent_scale(q_ref.shape[1])
    me = lax.axis_index("ctx")

    def visit(step, wanted):
        block = me - step
        hit = (block >= 0) & (block == wanted)
        block = jnp.maximum(block, 0)

        @pl.when(hit)
        def _():
            start = pl.multiple_of(block * 2 * BLOCK, 2 * BLOCK)
            absorb(scale, q_ref, piece[pl.ds(start, BLOCK), :], piece[pl.ds(start + BLOCK, BLOCK), :], *state)

        return jnp.where(hit, parents_ref[block], wanted)

    lax.fori_loop(1, parents_ref.shape[0], visit, parents_ref[me])


def own_block_kernel(xors, reached_ref, q_ref, kv_ref, *refs):
    state = refs[len(xors):]
    m_ref, l_ref, acc_ref = state
    scale = exponent_scale(q_ref.shape[1])
    s = scores_of(kv_ref[0:BLOCK, :], q_ref[...])
    key_at = lax.broadcasted_iota(jnp.int32, s.shape, 0)
    query_at = lax.broadcasted_iota(jnp.int32, s.shape, 1) & (BLOCK - 1)
    s = jnp.where(key_at <= query_at, s, -1e30)
    m = jnp.max(s, axis=0, keepdims=True)
    p = jnp.exp2((s - m) * scale)
    m_ref[...] = m
    l_ref[...] = jnp.sum(p, axis=0, keepdims=True)
    acc_ref[...] = weighted(kv_ref[BLOCK:, :], p)
    absorb_reached(xors, reached_ref, q_ref, refs[:len(xors)], state)


def others_kernel(xors, reached_ref, q_ref, m_in, l_in, acc_in, *refs):
    state = refs[len(xors):]
    absorb_reached(xors, reached_ref, q_ref, refs[:len(xors)], state)


def last_kernel(xors, tree_ref, q_ref, m_in, l_in, acc_in, *refs):
    kv_refs = refs[:max(len(xors), 1)]
    w_ref, att_ref, send_ref, keep_ref, *state = refs[len(kv_refs):]
    rows, head_dim = q_ref.shape
    if xors:
        absorb_reached(xors, tree_ref, q_ref, kv_refs, state)
    else:
        absorb_walk(tree_ref, q_ref, kv_refs[0], state)
    m_ref, l_ref, acc_ref = state

    for head in range(rows // BLOCK):
        at = slice(head * BLOCK, (head + 1) * BLOCK)
        part = acc_ref[:, at] / l_ref[:, at]
        att_ref[:, head * head_dim:(head + 1) * head_dim] = part.T.astype(jnp.bfloat16)

    project_pair(2, 0, att_ref, w_ref, send_ref, keep_ref)


def project_pair(flip, half, att_ref, w_ref, send_ref, keep_ref):
    target = lax.axis_index("tp") ^ flip
    width = w_ref.shape[1] // 4
    cols = keep_ref.shape[1]
    att = att_ref[...]
    send_ref[...] = project(att, w_ref, (target ^ 1) * width + half * cols, cols).astype(jnp.bfloat16)
    keep_ref[...] = project(att, w_ref, target * width + half * cols, cols)


def shards(ctx_size, tp_size, query_heads, key_heads, value_heads, parents, out_weight):
    tok_rows, local_heads, head_dim = query_heads.shape
    assert tok_rows == BLOCK and key_heads.shape[1] == 1 and parents.shape[0] == ctx_size and tp_size == 4
    width = out_weight.shape[1] // tp_size
    rows = local_heads * tok_rows
    params = pltpu.CompilerParams(vmem_limit_bytes=VMEM_LIMIT)
    vmem = pl.BlockSpec(memory_space=pltpu.VMEM)
    hbm = pl.BlockSpec(memory_space=pltpu.HBM)
    smem = pl.BlockSpec(memory_space=pltpu.SMEM)

    def in_hbm(x):
        return pltpu.with_memory_space_constraint(x, pltpu.HBM)

    def swap(x, axis, size, other):
        return lax.ppermute(x, axis, [(i, i ^ other) for i in range(size)])

    kv, reached = pl.pallas_call(
        functools.partial(pack_kernel, ctx_size == DIRECT_SIZE),
        out_shape=(
            jax.ShapeDtypeStruct((2 * tok_rows, head_dim), jnp.bfloat16),
            jax.ShapeDtypeStruct((8, 128), jnp.int32),
        ),
        in_specs=[hbm, hbm, hbm],
        out_specs=(vmem, vmem),
        scratch_shapes=[pltpu.SMEM(parents.shape, jnp.int32), pltpu.SemaphoreType.DMA((3,))],
        compiler_params=params,
        cost_estimate=pl.CostEstimate(flops=8_000_000_000, bytes_accessed=130_000, transcendentals=0),
    )(in_hbm(key_heads[:, 0, :]), in_hbm(value_heads[:, 0, :]), in_hbm(parents))
    if ctx_size == DIRECT_SIZE:
        by_4 = swap(kv, "ctx", ctx_size, 4)
        by_1 = swap(kv, "ctx", ctx_size, 1)
        by_6 = swap(kv, "ctx", ctx_size, 6)
        held, _ = lax.optimization_barrier((by_1, by_6))
        by_23 = swap(jnp.concatenate([kv, held], axis=0), "ctx", ctx_size, 2)
        by_7 = swap(by_6, "ctx", ctx_size, 1)
        by_5 = swap(by_4, "ctx", ctx_size, 1)
        early, early_xors = [by_1, by_6, by_4], ((1,), (6,), (4,))
    else:
        early, early_xors = [], ()
    q = jnp.transpose(query_heads, (1, 0, 2)).reshape(rows, head_dim)

    m, l, acc = pl.pallas_call(
        functools.partial(own_block_kernel, early_xors),
        out_shape=(
            jax.ShapeDtypeStruct((1, rows), jnp.float32),
            jax.ShapeDtypeStruct((1, rows), jnp.float32),
            jax.ShapeDtypeStruct((head_dim, rows), jnp.float32),
        ),
        in_specs=[vmem] * (3 + len(early)),
        out_specs=(vmem,) * 3,
        compiler_params=params,
        cost_estimate=pl.CostEstimate(flops=130_000_000, bytes_accessed=1_000_000, transcendentals=260_000),
    )(reached, q, kv, *early)

    state = (m, l, acc)
    state_shapes = tuple(jax.ShapeDtypeStruct(x.shape, x.dtype) for x in state)
    if ctx_size == DIRECT_SIZE:
        xors = ((7,),)
        state = pl.pallas_call(
            functools.partial(others_kernel, xors),
            out_shape=state_shapes,
            in_specs=[vmem] * (5 + len(xors)),
            out_specs=(vmem,) * 3,
            input_output_aliases={2: 0, 3: 1, 4: 2},
            compiler_params=params,
            cost_estimate=pl.CostEstimate(flops=270_000_000, bytes_accessed=1_000_000, transcendentals=500_000),
        )(reached, q, *state, by_7)
        xors, pieces, tree, tree_spec = ((2, 3), (5,)), [by_23, by_5], reached, vmem
    else:
        xors, pieces, tree, tree_spec = (), [lax.all_gather(kv, "ctx", axis=0, tiled=True)], parents, smem

    half = width // 2
    pair_shapes = (
        jax.ShapeDtypeStruct((tok_rows, half), jnp.bfloat16),
        jax.ShapeDtypeStruct((tok_rows, half), jnp.float32),
    )
    att, send_a, keep_a, *_ = pl.pallas_call(
        functools.partial(last_kernel, xors),
        out_shape=(jax.ShapeDtypeStruct((tok_rows, local_heads * head_dim), jnp.bfloat16),) + pair_shapes + state_shapes,
        in_specs=[tree_spec] + [vmem] * (5 + len(pieces)),
        out_specs=(vmem,) * 6,
        input_output_aliases={2: 3, 3: 4, 4: 5},
        compiler_params=params,
        cost_estimate=pl.CostEstimate(flops=1_000_000_000, bytes_accessed=10_000_000, transcendentals=1_000_000),
    )(tree, q, *state, *pieces, out_weight)

    def projected(flip, part, shapes, att):
        return pl.pallas_call(
            functools.partial(project_pair, flip, part),
            out_shape=shapes,
            in_specs=[vmem, vmem],
            out_specs=(vmem, vmem),
            compiler_params=params,
            cost_estimate=pl.CostEstimate(flops=540_000_000, bytes_accessed=4_000_000, transcendentals=0),
        )(att, out_weight)

    def added(keep, arrived):
        return (keep + arrived.astype(jnp.float32)).astype(jnp.bfloat16)

    in_a = swap(send_a, "tp", tp_size, 1)
    send_b, keep_b = projected(2, 1, pair_shapes, att)
    in_b = swap(send_b, "tp", tp_size, 1)
    far_a = added(keep_a, in_a)
    from_a = swap(far_a, "tp", tp_size, 2)
    far_b = added(keep_b, in_b)
    from_b = swap(far_b, "tp", tp_size, 2)
    att, _ = lax.optimization_barrier((att, far_a))
    send_near, keep_near = projected(
        0,
        0,
        (jax.ShapeDtypeStruct((tok_rows, width), jnp.bfloat16), jax.ShapeDtypeStruct((tok_rows, width), jnp.float32)),
        att,
    )
    near_in = swap(send_near, "tp", tp_size, 1)
    from_far = jnp.concatenate([from_a, from_b], axis=1).astype(jnp.float32)
    return (keep_near + near_in.astype(jnp.float32) + from_far).astype(jnp.bfloat16)


def solution(mesh):
    return jax.shard_map(
        functools.partial(shards, mesh.shape["ctx"], mesh.shape["tp"]),
        mesh=mesh,
        in_specs=(
            P("ctx", "tp", None),
            P("ctx", "tp", None),
            P("ctx", "tp", None),
            P(),
            P("tp", None),
        ),
        out_specs=P("ctx", "tp"),
        check_vma=False,
    )
```

```python
import functools
import math

import jax
import jax.numpy as jnp
from jax import lax
from jax.experimental import pallas as pl
from jax.experimental.pallas import tpu as pltpu
from jax.sharding import PartitionSpec as P

BLOCK = 128
DIRECT_SIZE = 8
VMEM_LIMIT = 32 * 1024 * 1024


def scores_of(k, q):
    return lax.dot_general(k, q, (((1,), (1,)), ((), ())), preferred_element_type=jnp.float32)


def weighted(v, p):
    return lax.dot_general(v, p.astype(jnp.bfloat16), (((0,), (0,)), ((), ())), preferred_element_type=jnp.float32)


def exponent_scale(head_dim):
    return math.log2(math.e) / math.sqrt(head_dim)


def reached_mask(parents_ref):
    me = lax.axis_index("ctx")
    wanted = parents_ref[me]
    reached = jnp.int32(0)
    for step in range(1, DIRECT_SIZE):
        block = me - step
        hit = (block >= 0) & (block == wanted)
        block = jnp.maximum(block, 0)
        reached = jnp.where(hit, reached | lax.shift_left(jnp.int32(1), block), reached)
        wanted = jnp.where(hit, parents_ref[block], wanted)
    return reached


def pack_kernel(walk, k_hbm, v_hbm, parents_hbm, kv_ref, reached_ref, parents_ref, sems):
    copies = [
        pltpu.make_async_copy(parents_hbm, parents_ref, sems.at[0]),
        pltpu.make_async_copy(k_hbm, kv_ref.at[0:BLOCK, :], sems.at[1]),
        pltpu.make_async_copy(v_hbm, kv_ref.at[BLOCK:2 * BLOCK, :], sems.at[2]),
    ]
    for copy in copies:
        copy.start()
    copies[0].wait()
    reached = reached_mask(parents_ref) if walk else jnp.int32(0)
    reached_ref[...] = jnp.full(reached_ref.shape, reached, jnp.int32)
    copies[1].wait()
    copies[2].wait()


def project(att, w_ref, start, width):
    start = pl.multiple_of(start, 128)
    return jnp.dot(att, w_ref[:, pl.ds(start, width)], preferred_element_type=jnp.float32)


def absorb(scale, q_ref, k, v, m_ref, l_ref, acc_ref):
    s = scores_of(k, q_ref[...])
    m_old = m_ref[...]
    m_new = jnp.maximum(m_old, jnp.max(s, axis=0, keepdims=True))
    p = jnp.exp2((s - m_new) * scale)
    factor = jnp.exp2((m_old - m_new) * scale)
    m_ref[...] = m_new
    l_ref[...] = l_ref[...] * factor + jnp.sum(p, axis=0, keepdims=True)
    acc_ref[...] = acc_ref[...] * factor + weighted(v, p)


def absorb_reached(xors, reached_ref, q_ref, kv_refs, state):
    scale = exponent_scale(q_ref.shape[1])
    me = lax.axis_index("ctx")
    reached = jnp.max(reached_ref[...])
    for other, kv_ref in zip(xors, kv_refs):
        @pl.when((lax.shift_right_logical(reached, me ^ other) & 1) == 1)
        def _():
            absorb(scale, q_ref, kv_ref[0:BLOCK, :], kv_ref[BLOCK:, :], *state)


def absorb_walk(parents_ref, q_ref, piece, state):
    scale = exponent_scale(q_ref.shape[1])
    me = lax.axis_index("ctx")

    def visit(step, wanted):
        block = me - step
        hit = (block >= 0) & (block == wanted)
        block = jnp.maximum(block, 0)

        @pl.when(hit)
        def _():
            start = pl.multiple_of(block * 2 * BLOCK, 2 * BLOCK)
            absorb(scale, q_ref, piece[pl.ds(start, BLOCK), :], piece[pl.ds(start + BLOCK, BLOCK), :], *state)

        return jnp.where(hit, parents_ref[block], wanted)

    lax.fori_loop(1, parents_ref.shape[0], visit, parents_ref[me])


def own_block_kernel(xors, reached_ref, q_ref, kv_ref, *refs):
    state = refs[len(xors):]
    m_ref, l_ref, acc_ref = state
    scale = exponent_scale(q_ref.shape[1])
    s = scores_of(kv_ref[0:BLOCK, :], q_ref[...])
    key_at = lax.broadcasted_iota(jnp.int32, s.shape, 0)
    query_at = lax.broadcasted_iota(jnp.int32, s.shape, 1) & (BLOCK - 1)
    s = jnp.where(key_at <= query_at, s, -1e30)
    m = jnp.max(s, axis=0, keepdims=True)
    p = jnp.exp2((s - m) * scale)
    m_ref[...] = m
    l_ref[...] = jnp.sum(p, axis=0, keepdims=True)
    acc_ref[...] = weighted(kv_ref[BLOCK:, :], p)
    absorb_reached(xors, reached_ref, q_ref, refs[:len(xors)], state)


def others_kernel(xors, reached_ref, q_ref, m_in, l_in, acc_in, *refs):
    state = refs[len(xors):]
    absorb_reached(xors, reached_ref, q_ref, refs[:len(xors)], state)


def last_kernel(xors, tree_ref, q_ref, m_in, l_in, acc_in, *refs):
    kv_refs = refs[:max(len(xors), 1)]
    w_ref, att_ref, send_ref, keep_ref, *state = refs[len(kv_refs):]
    rows, head_dim = q_ref.shape
    if xors:
        absorb_reached(xors, tree_ref, q_ref, kv_refs, state)
    else:
        absorb_walk(tree_ref, q_ref, kv_refs[0], state)
    m_ref, l_ref, acc_ref = state

    for head in range(rows // BLOCK):
        at = slice(head * BLOCK, (head + 1) * BLOCK)
        part = acc_ref[:, at] / l_ref[:, at]
        att_ref[:, head * head_dim:(head + 1) * head_dim] = part.T.astype(jnp.bfloat16)

    project_pair(2, 0, att_ref, w_ref, send_ref, keep_ref)


def project_pair(flip, half, att_ref, w_ref, send_ref, keep_ref):
    target = lax.axis_index("tp") ^ flip
    width = w_ref.shape[1] // 4
    cols = keep_ref.shape[1]
    att = att_ref[...]
    send_ref[...] = project(att, w_ref, (target ^ 1) * width + half * cols, cols).astype(jnp.bfloat16)
    keep_ref[...] = project(att, w_ref, target * width + half * cols, cols)


def shards(ctx_size, tp_size, query_heads, key_heads, value_heads, parents, out_weight):
    tok_rows, local_heads, head_dim = query_heads.shape
    assert tok_rows == BLOCK and key_heads.shape[1] == 1 and parents.shape[0] == ctx_size and tp_size == 4
    width = out_weight.shape[1] // tp_size
    rows = local_heads * tok_rows
    params = pltpu.CompilerParams(vmem_limit_bytes=VMEM_LIMIT)
    vmem = pl.BlockSpec(memory_space=pltpu.VMEM)
    hbm = pl.BlockSpec(memory_space=pltpu.HBM)
    smem = pl.BlockSpec(memory_space=pltpu.SMEM)

    def in_hbm(x):
        return pltpu.with_memory_space_constraint(x, pltpu.HBM)

    def swap(x, axis, size, other):
        return lax.ppermute(x, axis, [(i, i ^ other) for i in range(size)])

    def forward(x, other):
        route = [(i, i ^ 1 if i ^ other < i else i) for i in range(ctx_size)]
        return lax.ppermute(x, "ctx", route)

    kv, reached = pl.pallas_call(
        functools.partial(pack_kernel, ctx_size == DIRECT_SIZE),
        out_shape=(
            jax.ShapeDtypeStruct((2 * tok_rows, head_dim), jnp.bfloat16),
            jax.ShapeDtypeStruct((8, 128), jnp.int32),
        ),
        in_specs=[hbm, hbm, hbm],
        out_specs=(vmem, vmem),
        scratch_shapes=[pltpu.SMEM(parents.shape, jnp.int32), pltpu.SemaphoreType.DMA((3,))],
        compiler_params=params,
        cost_estimate=pl.CostEstimate(flops=8_000_000_000, bytes_accessed=130_000, transcendentals=0),
    )(in_hbm(key_heads[:, 0, :]), in_hbm(value_heads[:, 0, :]), in_hbm(parents))
    if ctx_size == DIRECT_SIZE:
        columns = [swap(kv, "ctx", ctx_size, other) for other in (4, 2, 6)]
        beside = swap(kv, "ctx", ctx_size, 1)
        pairs = [forward(x, other) for x, other in zip(columns, (4, 2, 6))]
        early, early_xors = [beside, *columns], (1, 4, 2, 6)
    else:
        early, early_xors = [], ()
    q = jnp.transpose(query_heads, (1, 0, 2)).reshape(rows, head_dim)

    m, l, acc = pl.pallas_call(
        functools.partial(own_block_kernel, early_xors),
        out_shape=(
            jax.ShapeDtypeStruct((1, rows), jnp.float32),
            jax.ShapeDtypeStruct((1, rows), jnp.float32),
            jax.ShapeDtypeStruct((head_dim, rows), jnp.float32),
        ),
        in_specs=[vmem] * (3 + len(early)),
        out_specs=(vmem,) * 3,
        compiler_params=params,
        cost_estimate=pl.CostEstimate(flops=130_000_000, bytes_accessed=1_000_000, transcendentals=260_000),
    )(reached, q, kv, *early)

    state = (m, l, acc)
    state_shapes = tuple(jax.ShapeDtypeStruct(x.shape, x.dtype) for x in state)
    if ctx_size == DIRECT_SIZE:
        def absorbed(state, xors, arrived):
            return pl.pallas_call(
                functools.partial(others_kernel, xors),
                out_shape=state_shapes,
                in_specs=[vmem] * (5 + len(xors)),
                out_specs=(vmem,) * 3,
                input_output_aliases={2: 0, 3: 1, 4: 2},
                compiler_params=params,
                cost_estimate=pl.CostEstimate(flops=270_000_000, bytes_accessed=1_000_000, transcendentals=500_000),
            )(reached, q, *state, *arrived)

        state = absorbed(state, (3, 7), pairs[1:])
        xors, pieces, tree, tree_spec = (5,), pairs[:1], reached, vmem
    else:
        xors, pieces, tree, tree_spec = (), [lax.all_gather(kv, "ctx", axis=0, tiled=True)], parents, smem

    half = width // 2
    pair_shapes = (
        jax.ShapeDtypeStruct((tok_rows, half), jnp.bfloat16),
        jax.ShapeDtypeStruct((tok_rows, half), jnp.float32),
    )
    att, send_a, keep_a, *_ = pl.pallas_call(
        functools.partial(last_kernel, xors),
        out_shape=(jax.ShapeDtypeStruct((tok_rows, local_heads * head_dim), jnp.bfloat16),) + pair_shapes + state_shapes,
        in_specs=[tree_spec] + [vmem] * (5 + len(pieces)),
        out_specs=(vmem,) * 6,
        input_output_aliases={2: 3, 3: 4, 4: 5},
        compiler_params=params,
        cost_estimate=pl.CostEstimate(flops=1_000_000_000, bytes_accessed=10_000_000, transcendentals=1_000_000),
    )(tree, q, *state, *pieces, out_weight)

    def projected(flip, part, shapes, att):
        return pl.pallas_call(
            functools.partial(project_pair, flip, part),
            out_shape=shapes,
            in_specs=[vmem, vmem],
            out_specs=(vmem, vmem),
            compiler_params=params,
            cost_estimate=pl.CostEstimate(flops=540_000_000, bytes_accessed=4_000_000, transcendentals=0),
        )(att, out_weight)

    def added(keep, arrived):
        return (keep + arrived.astype(jnp.float32)).astype(jnp.bfloat16)

    in_a = swap(send_a, "tp", tp_size, 1)
    send_b, keep_b = projected(2, 1, pair_shapes, att)
    in_b = swap(send_b, "tp", tp_size, 1)
    far_a = added(keep_a, in_a)
    from_a = swap(far_a, "tp", tp_size, 2)
    far_b = added(keep_b, in_b)
    from_b = swap(far_b, "tp", tp_size, 2)
    att, _ = lax.optimization_barrier((att, far_a))
    send_near, keep_near = projected(
        0,
        0,
        (jax.ShapeDtypeStruct((tok_rows, width), jnp.bfloat16), jax.ShapeDtypeStruct((tok_rows, width), jnp.float32)),
        att,
    )
    near_in = swap(send_near, "tp", tp_size, 1)
    from_far = jnp.concatenate([from_a, from_b], axis=1).astype(jnp.float32)
    return (keep_near + near_in.astype(jnp.float32) + from_far).astype(jnp.bfloat16)


def solution(mesh):
    return jax.shard_map(
        functools.partial(shards, mesh.shape["ctx"], mesh.shape["tp"]),
        mesh=mesh,
        in_specs=(
            P("ctx", "tp", None),
            P("ctx", "tp", None),
            P("ctx", "tp", None),
            P(),
            P("tp", None),
        ),
        out_specs=P("ctx", "tp"),
        check_vma=False,
    )
```

```python
import functools
import math

import jax
import jax.numpy as jnp
from jax import lax
from jax.experimental import pallas as pl
from jax.experimental.pallas import tpu as pltpu
from jax.sharding import PartitionSpec as P

BLOCK = 128
DIRECT_SIZE = 8
VMEM_LIMIT = 32 * 1024 * 1024


def scores_of(k, q):
    return lax.dot_general(k, q, (((1,), (1,)), ((), ())), preferred_element_type=jnp.float32)


def weighted(v, p):
    return lax.dot_general(v, p.astype(jnp.bfloat16), (((0,), (0,)), ((), ())), preferred_element_type=jnp.float32)


def exponent_scale(head_dim):
    return math.log2(math.e) / math.sqrt(head_dim)


def reached_mask(parents_ref):
    me = lax.axis_index("ctx")
    wanted = parents_ref[me]
    reached = jnp.int32(0)
    for step in range(1, DIRECT_SIZE):
        block = me - step
        hit = (block >= 0) & (block == wanted)
        block = jnp.maximum(block, 0)
        reached = jnp.where(hit, reached | lax.shift_left(jnp.int32(1), block), reached)
        wanted = jnp.where(hit, parents_ref[block], wanted)
    return reached


def pack_kernel(walk, k_hbm, v_hbm, parents_hbm, kv_ref, reached_ref, parents_ref, sems):
    copies = [
        pltpu.make_async_copy(parents_hbm, parents_ref, sems.at[0]),
        pltpu.make_async_copy(k_hbm, kv_ref.at[0:BLOCK, :], sems.at[1]),
        pltpu.make_async_copy(v_hbm, kv_ref.at[BLOCK:2 * BLOCK, :], sems.at[2]),
    ]
    for copy in copies:
        copy.start()
    copies[0].wait()
    reached = reached_mask(parents_ref) if walk else jnp.int32(0)
    reached_ref[...] = jnp.full(reached_ref.shape, reached, jnp.int32)
    copies[1].wait()
    copies[2].wait()


def project(att, w_ref, start, width):
    start = pl.multiple_of(start, 128)
    return jnp.dot(att, w_ref[:, pl.ds(start, width)], preferred_element_type=jnp.float32)


def absorb(scale, q_ref, k, v, m_ref, l_ref, acc_ref):
    s = scores_of(k, q_ref[...])
    m_old = m_ref[...]
    m_new = jnp.maximum(m_old, jnp.max(s, axis=0, keepdims=True))
    p = jnp.exp2((s - m_new) * scale)
    factor = jnp.exp2((m_old - m_new) * scale)
    m_ref[...] = m_new
    l_ref[...] = l_ref[...] * factor + jnp.sum(p, axis=0, keepdims=True)
    acc_ref[...] = acc_ref[...] * factor + weighted(v, p)


def absorb_reached(xors, reached_ref, q_ref, kv_refs, state):
    scale = exponent_scale(q_ref.shape[1])
    me = lax.axis_index("ctx")
    reached = jnp.max(reached_ref[...])
    for others, kv_ref in zip(xors, kv_refs):
        for at, other in enumerate(others):
            keys = slice(2 * at * BLOCK, (2 * at + 1) * BLOCK)
            values = slice((2 * at + 1) * BLOCK, (2 * at + 2) * BLOCK)

            @pl.when((lax.shift_right_logical(reached, me ^ other) & 1) == 1)
            def _():
                absorb(scale, q_ref, kv_ref[keys, :], kv_ref[values, :], *state)


def absorb_walk(parents_ref, q_ref, piece, state):
    scale = exponent_scale(q_ref.shape[1])
    me = lax.axis_index("ctx")

    def visit(step, wanted):
        block = me - step
        hit = (block >= 0) & (block == wanted)
        block = jnp.maximum(block, 0)

        @pl.when(hit)
        def _():
            start = pl.multiple_of(block * 2 * BLOCK, 2 * BLOCK)
            absorb(scale, q_ref, piece[pl.ds(start, BLOCK), :], piece[pl.ds(start + BLOCK, BLOCK), :], *state)

        return jnp.where(hit, parents_ref[block], wanted)

    lax.fori_loop(1, parents_ref.shape[0], visit, parents_ref[me])


def own_block_kernel(xors, reached_ref, q_ref, kv_ref, *refs):
    state = refs[len(xors):]
    m_ref, l_ref, acc_ref = state
    scale = exponent_scale(q_ref.shape[1])
    s = scores_of(kv_ref[0:BLOCK, :], q_ref[...])
    key_at = lax.broadcasted_iota(jnp.int32, s.shape, 0)
    query_at = lax.broadcasted_iota(jnp.int32, s.shape, 1) & (BLOCK - 1)
    s = jnp.where(key_at <= query_at, s, -1e30)
    m = jnp.max(s, axis=0, keepdims=True)
    p = jnp.exp2((s - m) * scale)
    m_ref[...] = m
    l_ref[...] = jnp.sum(p, axis=0, keepdims=True)
    acc_ref[...] = weighted(kv_ref[BLOCK:, :], p)
    absorb_reached(xors, reached_ref, q_ref, refs[:len(xors)], state)


def others_kernel(xors, reached_ref, q_ref, m_in, l_in, acc_in, *refs):
    state = refs[len(xors):]
    absorb_reached(xors, reached_ref, q_ref, refs[:len(xors)], state)


def last_kernel(xors, tree_ref, q_ref, m_in, l_in, acc_in, *refs):
    kv_refs = refs[:max(len(xors), 1)]
    w_ref, att_ref, send_ref, keep_ref, *state = refs[len(kv_refs):]
    rows, head_dim = q_ref.shape
    if xors:
        absorb_reached(xors, tree_ref, q_ref, kv_refs, state)
    else:
        absorb_walk(tree_ref, q_ref, kv_refs[0], state)
    m_ref, l_ref, acc_ref = state

    for head in range(rows // BLOCK):
        at = slice(head * BLOCK, (head + 1) * BLOCK)
        part = acc_ref[:, at] / l_ref[:, at]
        att_ref[:, head * head_dim:(head + 1) * head_dim] = part.T.astype(jnp.bfloat16)

    project_pair(2, 0, att_ref, w_ref, send_ref, keep_ref)


def project_pair(flip, half, att_ref, w_ref, send_ref, keep_ref):
    target = lax.axis_index("tp") ^ flip
    width = w_ref.shape[1] // 4
    cols = keep_ref.shape[1]
    att = att_ref[...]
    send_ref[...] = project(att, w_ref, (target ^ 1) * width + half * cols, cols).astype(jnp.bfloat16)
    keep_ref[...] = project(att, w_ref, target * width + half * cols, cols)


def shards(ctx_size, tp_size, query_heads, key_heads, value_heads, parents, out_weight):
    tok_rows, local_heads, head_dim = query_heads.shape
    assert tok_rows == BLOCK and key_heads.shape[1] == 1 and parents.shape[0] == ctx_size and tp_size == 4
    width = out_weight.shape[1] // tp_size
    rows = local_heads * tok_rows
    params = pltpu.CompilerParams(vmem_limit_bytes=VMEM_LIMIT)
    vmem = pl.BlockSpec(memory_space=pltpu.VMEM)
    hbm = pl.BlockSpec(memory_space=pltpu.HBM)
    smem = pl.BlockSpec(memory_space=pltpu.SMEM)

    def in_hbm(x):
        return pltpu.with_memory_space_constraint(x, pltpu.HBM)

    def swap(x, axis, size, other):
        return lax.ppermute(x, axis, [(i, i ^ other) for i in range(size)])

    kv, reached = pl.pallas_call(
        functools.partial(pack_kernel, ctx_size == DIRECT_SIZE),
        out_shape=(
            jax.ShapeDtypeStruct((2 * tok_rows, head_dim), jnp.bfloat16),
            jax.ShapeDtypeStruct((8, 128), jnp.int32),
        ),
        in_specs=[hbm, hbm, hbm],
        out_specs=(vmem, vmem),
        scratch_shapes=[pltpu.SMEM(parents.shape, jnp.int32), pltpu.SemaphoreType.DMA((3,))],
        compiler_params=params,
        cost_estimate=pl.CostEstimate(flops=8_000_000_000, bytes_accessed=130_000, transcendentals=0),
    )(in_hbm(key_heads[:, 0, :]), in_hbm(value_heads[:, 0, :]), in_hbm(parents))
    if ctx_size == DIRECT_SIZE:
        by_4 = swap(kv, "ctx", ctx_size, 4)
        by_2 = swap(kv, "ctx", ctx_size, 2)
        by_1 = swap(kv, "ctx", ctx_size, 1)
        held, _ = lax.optimization_barrier((by_4, by_1))
        by_6 = swap(held, "ctx", ctx_size, 2)
        by_5 = swap(by_4, "ctx", ctx_size, 1)
        by_3 = swap(by_2, "ctx", ctx_size, 1)
        by_7 = swap(by_6, "ctx", ctx_size, 1)
        early, early_xors = [by_1, by_2, by_4, by_6], ((1,), (2,), (4,), (6,))
    else:
        early, early_xors = [], ()
    q = jnp.transpose(query_heads, (1, 0, 2)).reshape(rows, head_dim)

    m, l, acc = pl.pallas_call(
        functools.partial(own_block_kernel, early_xors),
        out_shape=(
            jax.ShapeDtypeStruct((1, rows), jnp.float32),
            jax.ShapeDtypeStruct((1, rows), jnp.float32),
            jax.ShapeDtypeStruct((head_dim, rows), jnp.float32),
        ),
        in_specs=[vmem] * (3 + len(early)),
        out_specs=(vmem,) * 3,
        compiler_params=params,
        cost_estimate=pl.CostEstimate(flops=130_000_000, bytes_accessed=1_000_000, transcendentals=260_000),
    )(reached, q, kv, *early)

    state = (m, l, acc)
    state_shapes = tuple(jax.ShapeDtypeStruct(x.shape, x.dtype) for x in state)
    if ctx_size == DIRECT_SIZE:
        xors = ((5,), (3,))
        state = pl.pallas_call(
            functools.partial(others_kernel, xors),
            out_shape=state_shapes,
            in_specs=[vmem] * (5 + len(xors)),
            out_specs=(vmem,) * 3,
            input_output_aliases={2: 0, 3: 1, 4: 2},
            compiler_params=params,
            cost_estimate=pl.CostEstimate(flops=270_000_000, bytes_accessed=1_000_000, transcendentals=500_000),
        )(reached, q, *state, by_5, by_3)
        xors, pieces, tree, tree_spec = ((7,),), [by_7], reached, vmem
    else:
        xors, pieces, tree, tree_spec = (), [lax.all_gather(kv, "ctx", axis=0, tiled=True)], parents, smem

    half = width // 2
    pair_shapes = (
        jax.ShapeDtypeStruct((tok_rows, half), jnp.bfloat16),
        jax.ShapeDtypeStruct((tok_rows, half), jnp.float32),
    )
    att, send_a, keep_a, *_ = pl.pallas_call(
        functools.partial(last_kernel, xors),
        out_shape=(jax.ShapeDtypeStruct((tok_rows, local_heads * head_dim), jnp.bfloat16),) + pair_shapes + state_shapes,
        in_specs=[tree_spec] + [vmem] * (5 + len(pieces)),
        out_specs=(vmem,) * 6,
        input_output_aliases={2: 3, 3: 4, 4: 5},
        compiler_params=params,
        cost_estimate=pl.CostEstimate(flops=1_000_000_000, bytes_accessed=10_000_000, transcendentals=1_000_000),
    )(tree, q, *state, *pieces, out_weight)

    def projected(flip, part, shapes, att):
        return pl.pallas_call(
            functools.partial(project_pair, flip, part),
            out_shape=shapes,
            in_specs=[vmem, vmem],
            out_specs=(vmem, vmem),
            compiler_params=params,
            cost_estimate=pl.CostEstimate(flops=540_000_000, bytes_accessed=4_000_000, transcendentals=0),
        )(att, out_weight)

    def added(keep, arrived):
        return (keep + arrived.astype(jnp.float32)).astype(jnp.bfloat16)

    in_a = swap(send_a, "tp", tp_size, 1)
    send_b, keep_b = projected(2, 1, pair_shapes, att)
    in_b = swap(send_b, "tp", tp_size, 1)
    far_a = added(keep_a, in_a)
    from_a = swap(far_a, "tp", tp_size, 2)
    far_b = added(keep_b, in_b)
    from_b = swap(far_b, "tp", tp_size, 2)
    att, _ = lax.optimization_barrier((att, far_a))
    send_near, keep_near = projected(
        0,
        0,
        (jax.ShapeDtypeStruct((tok_rows, width), jnp.bfloat16), jax.ShapeDtypeStruct((tok_rows, width), jnp.float32)),
        att,
    )
    near_in = swap(send_near, "tp", tp_size, 1)
    from_far = jnp.concatenate([from_a, from_b], axis=1).astype(jnp.float32)
    return (keep_near + near_in.astype(jnp.float32) + from_far).astype(jnp.bfloat16)


def solution(mesh):
    return jax.shard_map(
        functools.partial(shards, mesh.shape["ctx"], mesh.shape["tp"]),
        mesh=mesh,
        in_specs=(
            P("ctx", "tp", None),
            P("ctx", "tp", None),
            P("ctx", "tp", None),
            P(),
            P("tp", None),
        ),
        out_specs=P("ctx", "tp"),
        check_vma=False,
    )
```

```python
import functools
import math

import jax
import jax.numpy as jnp
from jax import lax
from jax.experimental import pallas as pl
from jax.experimental.pallas import tpu as pltpu
from jax.sharding import PartitionSpec as P

BLOCK = 128
DIRECT_SIZE = 8
VMEM_LIMIT = 32 * 1024 * 1024


def scores_of(k, q):
    return lax.dot_general(k, q, (((1,), (1,)), ((), ())), preferred_element_type=jnp.float32)


def weighted(v, p):
    return lax.dot_general(v, p.astype(jnp.bfloat16), (((0,), (0,)), ((), ())), preferred_element_type=jnp.float32)


def exponent_scale(head_dim):
    return math.log2(math.e) / math.sqrt(head_dim)


def reached_mask(parents_ref):
    me = lax.axis_index("ctx")
    wanted = parents_ref[me]
    reached = jnp.int32(0)
    for step in range(1, DIRECT_SIZE):
        block = me - step
        hit = (block >= 0) & (block == wanted)
        block = jnp.maximum(block, 0)
        reached = jnp.where(hit, reached | lax.shift_left(jnp.int32(1), block), reached)
        wanted = jnp.where(hit, parents_ref[block], wanted)
    return reached


def pack_kernel(walk, k_hbm, v_hbm, parents_hbm, kv_ref, reached_ref, parents_ref, sems):
    copies = [
        pltpu.make_async_copy(parents_hbm, parents_ref, sems.at[0]),
        pltpu.make_async_copy(k_hbm, kv_ref.at[0:BLOCK, :], sems.at[1]),
        pltpu.make_async_copy(v_hbm, kv_ref.at[BLOCK:2 * BLOCK, :], sems.at[2]),
    ]
    for copy in copies:
        copy.start()
    copies[0].wait()
    reached = reached_mask(parents_ref) if walk else jnp.int32(0)
    reached_ref[...] = jnp.full(reached_ref.shape, reached, jnp.int32)
    copies[1].wait()
    copies[2].wait()


def project(att, w_ref, start, width):
    start = pl.multiple_of(start, 128)
    return jnp.dot(att, w_ref[:, pl.ds(start, width)], preferred_element_type=jnp.float32)


def absorb(scale, q_ref, k, v, m_ref, l_ref, acc_ref):
    s = scores_of(k, q_ref[...])
    m_old = m_ref[...]
    m_new = jnp.maximum(m_old, jnp.max(s, axis=0, keepdims=True))
    p = jnp.exp2((s - m_new) * scale)
    factor = jnp.exp2((m_old - m_new) * scale)
    m_ref[...] = m_new
    l_ref[...] = l_ref[...] * factor + jnp.sum(p, axis=0, keepdims=True)
    acc_ref[...] = acc_ref[...] * factor + weighted(v, p)


def absorb_reached(xors, reached_ref, q_ref, kv_refs, state):
    scale = exponent_scale(q_ref.shape[1])
    me = lax.axis_index("ctx")
    reached = jnp.max(reached_ref[...])
    for other, kv_ref in zip(xors, kv_refs):
        @pl.when((lax.shift_right_logical(reached, me ^ other) & 1) == 1)
        def _():
            absorb(scale, q_ref, kv_ref[0:BLOCK, :], kv_ref[BLOCK:, :], *state)


def absorb_walk(parents_ref, q_ref, piece, state):
    scale = exponent_scale(q_ref.shape[1])
    me = lax.axis_index("ctx")

    def visit(step, wanted):
        block = me - step
        hit = (block >= 0) & (block == wanted)
        block = jnp.maximum(block, 0)

        @pl.when(hit)
        def _():
            start = pl.multiple_of(block * 2 * BLOCK, 2 * BLOCK)
            absorb(scale, q_ref, piece[pl.ds(start, BLOCK), :], piece[pl.ds(start + BLOCK, BLOCK), :], *state)

        return jnp.where(hit, parents_ref[block], wanted)

    lax.fori_loop(1, parents_ref.shape[0], visit, parents_ref[me])


def own_block_kernel(xors, reached_ref, q_ref, kv_ref, *refs):
    state = refs[len(xors):]
    m_ref, l_ref, acc_ref = state
    scale = exponent_scale(q_ref.shape[1])
    s = scores_of(kv_ref[0:BLOCK, :], q_ref[...])
    key_at = lax.broadcasted_iota(jnp.int32, s.shape, 0)
    query_at = lax.broadcasted_iota(jnp.int32, s.shape, 1) & (BLOCK - 1)
    s = jnp.where(key_at <= query_at, s, -1e30)
    m = jnp.max(s, axis=0, keepdims=True)
    p = jnp.exp2((s - m) * scale)
    m_ref[...] = m
    l_ref[...] = jnp.sum(p, axis=0, keepdims=True)
    acc_ref[...] = weighted(kv_ref[BLOCK:, :], p)
    absorb_reached(xors, reached_ref, q_ref, refs[:len(xors)], state)


def others_kernel(xors, reached_ref, q_ref, m_in, l_in, acc_in, *refs):
    state = refs[len(xors):]
    absorb_reached(xors, reached_ref, q_ref, refs[:len(xors)], state)


def last_kernel(xors, tree_ref, q_ref, m_in, l_in, acc_in, *refs):
    kv_refs = refs[:max(len(xors), 1)]
    w_ref, att_ref, send_ref, keep_ref, *state = refs[len(kv_refs):]
    rows, head_dim = q_ref.shape
    if xors:
        absorb_reached(xors, tree_ref, q_ref, kv_refs, state)
    else:
        absorb_walk(tree_ref, q_ref, kv_refs[0], state)
    m_ref, l_ref, acc_ref = state

    for head in range(rows // BLOCK):
        at = slice(head * BLOCK, (head + 1) * BLOCK)
        part = acc_ref[:, at] / l_ref[:, at]
        att_ref[:, head * head_dim:(head + 1) * head_dim] = part.T.astype(jnp.bfloat16)

    project_pair(2, 0, att_ref, w_ref, send_ref, keep_ref)


def project_pair(flip, half, att_ref, w_ref, send_ref, keep_ref):
    target = lax.axis_index("tp") ^ flip
    width = w_ref.shape[1] // 4
    cols = keep_ref.shape[1]
    att = att_ref[...]
    send_ref[...] = project(att, w_ref, (target ^ 1) * width + half * cols, cols).astype(jnp.bfloat16)
    keep_ref[...] = project(att, w_ref, target * width + half * cols, cols)


def shards(ctx_size, tp_size, query_heads, key_heads, value_heads, parents, out_weight):
    tok_rows, local_heads, head_dim = query_heads.shape
    assert tok_rows == BLOCK and key_heads.shape[1] == 1 and parents.shape[0] == ctx_size and tp_size == 4
    width = out_weight.shape[1] // tp_size
    rows = local_heads * tok_rows
    params = pltpu.CompilerParams(vmem_limit_bytes=VMEM_LIMIT)
    vmem = pl.BlockSpec(memory_space=pltpu.VMEM)
    hbm = pl.BlockSpec(memory_space=pltpu.HBM)
    smem = pl.BlockSpec(memory_space=pltpu.SMEM)

    def in_hbm(x):
        return pltpu.with_memory_space_constraint(x, pltpu.HBM)

    def swap(x, axis, size, other):
        return lax.ppermute(x, axis, [(i, i ^ other) for i in range(size)])

    kv, reached = pl.pallas_call(
        functools.partial(pack_kernel, ctx_size == DIRECT_SIZE),
        out_shape=(
            jax.ShapeDtypeStruct((2 * tok_rows, head_dim), jnp.bfloat16),
            jax.ShapeDtypeStruct((8, 128), jnp.int32),
        ),
        in_specs=[hbm, hbm, hbm],
        out_specs=(vmem, vmem),
        scratch_shapes=[pltpu.SMEM(parents.shape, jnp.int32), pltpu.SemaphoreType.DMA((3,))],
        compiler_params=params,
        cost_estimate=pl.CostEstimate(flops=8_000_000_000, bytes_accessed=130_000, transcendentals=0),
    )(in_hbm(key_heads[:, 0, :]), in_hbm(value_heads[:, 0, :]), in_hbm(parents))
    if ctx_size == DIRECT_SIZE:
        columns = [swap(kv, "ctx", ctx_size, other) for other in (4, 2, 6)]
        beside = swap(kv, "ctx", ctx_size, 1)
        by_3 = swap(beside, "ctx", ctx_size, 2)
        by_7 = swap(columns[2], "ctx", ctx_size, 1)
        by_5 = swap(columns[0], "ctx", ctx_size, 1)
        pairs = [by_5, by_3, by_7]
        early, early_xors = [beside, *columns], (1, 4, 2, 6)
    else:
        early, early_xors = [], ()
    q = jnp.transpose(query_heads, (1, 0, 2)).reshape(rows, head_dim)

    m, l, acc = pl.pallas_call(
        functools.partial(own_block_kernel, early_xors),
        out_shape=(
            jax.ShapeDtypeStruct((1, rows), jnp.float32),
            jax.ShapeDtypeStruct((1, rows), jnp.float32),
            jax.ShapeDtypeStruct((head_dim, rows), jnp.float32),
        ),
        in_specs=[vmem] * (3 + len(early)),
        out_specs=(vmem,) * 3,
        compiler_params=params,
        cost_estimate=pl.CostEstimate(flops=130_000_000, bytes_accessed=1_000_000, transcendentals=260_000),
    )(reached, q, kv, *early)

    state = (m, l, acc)
    state_shapes = tuple(jax.ShapeDtypeStruct(x.shape, x.dtype) for x in state)
    if ctx_size == DIRECT_SIZE:
        def absorbed(state, xors, arrived):
            return pl.pallas_call(
                functools.partial(others_kernel, xors),
                out_shape=state_shapes,
                in_specs=[vmem] * (5 + len(xors)),
                out_specs=(vmem,) * 3,
                input_output_aliases={2: 0, 3: 1, 4: 2},
                compiler_params=params,
                cost_estimate=pl.CostEstimate(flops=270_000_000, bytes_accessed=1_000_000, transcendentals=500_000),
            )(reached, q, *state, *arrived)

        state = absorbed(state, (7,), [by_7])
        xors, pieces, tree, tree_spec = (3, 5), [by_3, by_5], reached, vmem
    else:
        xors, pieces, tree, tree_spec = (), [lax.all_gather(kv, "ctx", axis=0, tiled=True)], parents, smem

    half = width // 2
    pair_shapes = (
        jax.ShapeDtypeStruct((tok_rows, half), jnp.bfloat16),
        jax.ShapeDtypeStruct((tok_rows, half), jnp.float32),
    )
    att, send_a, keep_a, *_ = pl.pallas_call(
        functools.partial(last_kernel, xors),
        out_shape=(jax.ShapeDtypeStruct((tok_rows, local_heads * head_dim), jnp.bfloat16),) + pair_shapes + state_shapes,
        in_specs=[tree_spec] + [vmem] * (5 + len(pieces)),
        out_specs=(vmem,) * 6,
        input_output_aliases={2: 3, 3: 4, 4: 5},
        compiler_params=params,
        cost_estimate=pl.CostEstimate(flops=1_000_000_000, bytes_accessed=10_000_000, transcendentals=1_000_000),
    )(tree, q, *state, *pieces, out_weight)

    def projected(flip, part, shapes, att):
        return pl.pallas_call(
            functools.partial(project_pair, flip, part),
            out_shape=shapes,
            in_specs=[vmem, vmem],
            out_specs=(vmem, vmem),
            compiler_params=params,
            cost_estimate=pl.CostEstimate(flops=540_000_000, bytes_accessed=4_000_000, transcendentals=0),
        )(att, out_weight)

    def added(keep, arrived):
        return (keep + arrived.astype(jnp.float32)).astype(jnp.bfloat16)

    in_a = swap(send_a, "tp", tp_size, 1)
    send_b, keep_b = projected(2, 1, pair_shapes, att)
    in_b = swap(send_b, "tp", tp_size, 1)
    far_a = added(keep_a, in_a)
    from_a = swap(far_a, "tp", tp_size, 2)
    far_b = added(keep_b, in_b)
    from_b = swap(far_b, "tp", tp_size, 2)
    att, _ = lax.optimization_barrier((att, far_a))
    send_near, keep_near = projected(
        0,
        0,
        (jax.ShapeDtypeStruct((tok_rows, width), jnp.bfloat16), jax.ShapeDtypeStruct((tok_rows, width), jnp.float32)),
        att,
    )
    near_in = swap(send_near, "tp", tp_size, 1)
    from_far = jnp.concatenate([from_a, from_b], axis=1).astype(jnp.float32)
    return (keep_near + near_in.astype(jnp.float32) + from_far).astype(jnp.bfloat16)


def solution(mesh):
    return jax.shard_map(
        functools.partial(shards, mesh.shape["ctx"], mesh.shape["tp"]),
        mesh=mesh,
        in_specs=(
            P("ctx", "tp", None),
            P("ctx", "tp", None),
            P("ctx", "tp", None),
            P(),
            P("tp", None),
        ),
        out_specs=P("ctx", "tp"),
        check_vma=False,
    )
```

```python
import functools
import math

import jax
import jax.numpy as jnp
from jax import lax
from jax.experimental import pallas as pl
from jax.experimental.pallas import tpu as pltpu
from jax.sharding import PartitionSpec as P

BLOCK = 128
DIRECT_SIZE = 8
VMEM_LIMIT = 32 * 1024 * 1024


def scores_of(k, q):
    return lax.dot_general(k, q, (((1,), (1,)), ((), ())), preferred_element_type=jnp.float32)


def weighted(v, p):
    return lax.dot_general(v, p.astype(jnp.bfloat16), (((0,), (0,)), ((), ())), preferred_element_type=jnp.float32)


def exponent_scale(head_dim):
    return math.log2(math.e) / math.sqrt(head_dim)


def reached_mask(parents_ref):
    me = lax.axis_index("ctx")
    wanted = parents_ref[me]
    reached = jnp.int32(0)
    for step in range(1, DIRECT_SIZE):
        block = me - step
        hit = (block >= 0) & (block == wanted)
        block = jnp.maximum(block, 0)
        reached = jnp.where(hit, reached | lax.shift_left(jnp.int32(1), block), reached)
        wanted = jnp.where(hit, parents_ref[block], wanted)
    return reached


def pack_kernel(walk, k_hbm, v_hbm, parents_hbm, kv_ref, reached_ref, parents_ref, sems):
    copies = [
        pltpu.make_async_copy(parents_hbm, parents_ref, sems.at[0]),
        pltpu.make_async_copy(k_hbm, kv_ref.at[0:BLOCK, :], sems.at[1]),
        pltpu.make_async_copy(v_hbm, kv_ref.at[BLOCK:2 * BLOCK, :], sems.at[2]),
    ]
    for copy in copies:
        copy.start()
    copies[0].wait()
    reached = reached_mask(parents_ref) if walk else jnp.int32(0)
    reached_ref[...] = jnp.full(reached_ref.shape, reached, jnp.int32)
    copies[1].wait()
    copies[2].wait()


def project(att, w_ref, start, width):
    start = pl.multiple_of(start, 128)
    return jnp.dot(att, w_ref[:, pl.ds(start, width)], preferred_element_type=jnp.float32)


def absorb(scale, q_ref, k, v, m_ref, l_ref, acc_ref):
    s = scores_of(k, q_ref[...])
    m_old = m_ref[...]
    m_new = jnp.maximum(m_old, jnp.max(s, axis=0, keepdims=True))
    p = jnp.exp2((s - m_new) * scale)
    factor = jnp.exp2((m_old - m_new) * scale)
    m_ref[...] = m_new
    l_ref[...] = l_ref[...] * factor + jnp.sum(p, axis=0, keepdims=True)
    acc_ref[...] = acc_ref[...] * factor + weighted(v, p)


def absorb_reached(xors, reached_ref, q_ref, kv_refs, state):
    scale = exponent_scale(q_ref.shape[1])
    me = lax.axis_index("ctx")
    reached = jnp.max(reached_ref[...])
    for other, kv_ref in zip(xors, kv_refs):
        @pl.when((lax.shift_right_logical(reached, me ^ other) & 1) == 1)
        def _():
            absorb(scale, q_ref, kv_ref[0:BLOCK, :], kv_ref[BLOCK:, :], *state)


def absorb_walk(parents_ref, q_ref, piece, state):
    scale = exponent_scale(q_ref.shape[1])
    me = lax.axis_index("ctx")

    def visit(step, wanted):
        block = me - step
        hit = (block >= 0) & (block == wanted)
        block = jnp.maximum(block, 0)

        @pl.when(hit)
        def _():
            start = pl.multiple_of(block * 2 * BLOCK, 2 * BLOCK)
            absorb(scale, q_ref, piece[pl.ds(start, BLOCK), :], piece[pl.ds(start + BLOCK, BLOCK), :], *state)

        return jnp.where(hit, parents_ref[block], wanted)

    lax.fori_loop(1, parents_ref.shape[0], visit, parents_ref[me])


def own_block_kernel(xors, reached_ref, q_ref, kv_ref, *refs):
    state = refs[len(xors):]
    m_ref, l_ref, acc_ref = state
    scale = exponent_scale(q_ref.shape[1])
    s = scores_of(kv_ref[0:BLOCK, :], q_ref[...])
    key_at = lax.broadcasted_iota(jnp.int32, s.shape, 0)
    query_at = lax.broadcasted_iota(jnp.int32, s.shape, 1) & (BLOCK - 1)
    s = jnp.where(key_at <= query_at, s, -1e30)
    m = jnp.max(s, axis=0, keepdims=True)
    p = jnp.exp2((s - m) * scale)
    m_ref[...] = m
    l_ref[...] = jnp.sum(p, axis=0, keepdims=True)
    acc_ref[...] = weighted(kv_ref[BLOCK:, :], p)
    absorb_reached(xors, reached_ref, q_ref, refs[:len(xors)], state)


def others_kernel(xors, reached_ref, q_ref, m_in, l_in, acc_in, *refs):
    state = refs[len(xors):]
    absorb_reached(xors, reached_ref, q_ref, refs[:len(xors)], state)


def last_kernel(xors, tree_ref, q_ref, m_in, l_in, acc_in, *refs):
    kv_refs = refs[:max(len(xors), 1)]
    w_ref, att_ref, send_ref, keep_ref, *state = refs[len(kv_refs):]
    rows, head_dim = q_ref.shape
    if xors:
        absorb_reached(xors, tree_ref, q_ref, kv_refs, state)
    else:
        absorb_walk(tree_ref, q_ref, kv_refs[0], state)
    m_ref, l_ref, acc_ref = state

    for head in range(rows // BLOCK):
        at = slice(head * BLOCK, (head + 1) * BLOCK)
        part = acc_ref[:, at] / l_ref[:, at]
        att_ref[:, head * head_dim:(head + 1) * head_dim] = part.T.astype(jnp.bfloat16)

    project_pair(2, 0, att_ref, w_ref, send_ref, keep_ref)


def project_pair(flip, half, att_ref, w_ref, send_ref, keep_ref):
    target = lax.axis_index("tp") ^ flip
    width = w_ref.shape[1] // 4
    cols = keep_ref.shape[1]
    att = att_ref[...]
    send_ref[...] = project(att, w_ref, (target ^ 1) * width + half * cols, cols).astype(jnp.bfloat16)
    keep_ref[...] = project(att, w_ref, target * width + half * cols, cols)


def shards(ctx_size, tp_size, query_heads, key_heads, value_heads, parents, out_weight):
    tok_rows, local_heads, head_dim = query_heads.shape
    assert tok_rows == BLOCK and key_heads.shape[1] == 1 and parents.shape[0] == ctx_size and tp_size == 4
    width = out_weight.shape[1] // tp_size
    rows = local_heads * tok_rows
    params = pltpu.CompilerParams(vmem_limit_bytes=VMEM_LIMIT)
    vmem = pl.BlockSpec(memory_space=pltpu.VMEM)
    hbm = pl.BlockSpec(memory_space=pltpu.HBM)
    smem = pl.BlockSpec(memory_space=pltpu.SMEM)

    def in_hbm(x):
        return pltpu.with_memory_space_constraint(x, pltpu.HBM)

    def swap(x, axis, size, other):
        return lax.ppermute(x, axis, [(i, i ^ other) for i in range(size)])

    def forward(x, other):
        route = []
        for i in range(ctx_size):
            for j in range(tp_size):
                target = (i ^ 1, j) if i ^ other < i else (i, j ^ 1)
                route.append((i * tp_size + j, target[0] * tp_size + target[1]))
        return lax.ppermute(x, ("ctx", "tp"), route)

    kv, reached = pl.pallas_call(
        functools.partial(pack_kernel, ctx_size == DIRECT_SIZE),
        out_shape=(
            jax.ShapeDtypeStruct((2 * tok_rows, head_dim), jnp.bfloat16),
            jax.ShapeDtypeStruct((8, 128), jnp.int32),
        ),
        in_specs=[hbm, hbm, hbm],
        out_specs=(vmem, vmem),
        scratch_shapes=[pltpu.SMEM(parents.shape, jnp.int32), pltpu.SemaphoreType.DMA((3,))],
        compiler_params=params,
        cost_estimate=pl.CostEstimate(flops=8_000_000_000, bytes_accessed=130_000, transcendentals=0),
    )(in_hbm(key_heads[:, 0, :]), in_hbm(value_heads[:, 0, :]), in_hbm(parents))
    if ctx_size == DIRECT_SIZE:
        columns = [swap(kv, "ctx", ctx_size, other) for other in (4, 2, 6)]
        beside = swap(kv, "ctx", ctx_size, 1)
        pairs = [forward(x, other) for x, other in zip(columns, (4, 2, 6))]
        early, early_xors = [beside, *columns], (1, 4, 2, 6)
    else:
        early, early_xors = [], ()
    q = jnp.transpose(query_heads, (1, 0, 2)).reshape(rows, head_dim)

    m, l, acc = pl.pallas_call(
        functools.partial(own_block_kernel, early_xors),
        out_shape=(
            jax.ShapeDtypeStruct((1, rows), jnp.float32),
            jax.ShapeDtypeStruct((1, rows), jnp.float32),
            jax.ShapeDtypeStruct((head_dim, rows), jnp.float32),
        ),
        in_specs=[vmem] * (3 + len(early)),
        out_specs=(vmem,) * 3,
        compiler_params=params,
        cost_estimate=pl.CostEstimate(flops=130_000_000, bytes_accessed=1_000_000, transcendentals=260_000),
    )(reached, q, kv, *early)

    state = (m, l, acc)
    state_shapes = tuple(jax.ShapeDtypeStruct(x.shape, x.dtype) for x in state)
    if ctx_size == DIRECT_SIZE:
        def absorbed(state, xors, arrived):
            return pl.pallas_call(
                functools.partial(others_kernel, xors),
                out_shape=state_shapes,
                in_specs=[vmem] * (5 + len(xors)),
                out_specs=(vmem,) * 3,
                input_output_aliases={2: 0, 3: 1, 4: 2},
                compiler_params=params,
                cost_estimate=pl.CostEstimate(flops=270_000_000, bytes_accessed=1_000_000, transcendentals=500_000),
            )(reached, q, *state, *arrived)

        state = absorbed(state, (3, 7), pairs[1:])
        xors, pieces, tree, tree_spec = (5,), pairs[:1], reached, vmem
    else:
        xors, pieces, tree, tree_spec = (), [lax.all_gather(kv, "ctx", axis=0, tiled=True)], parents, smem

    half = width // 2
    pair_shapes = (
        jax.ShapeDtypeStruct((tok_rows, half), jnp.bfloat16),
        jax.ShapeDtypeStruct((tok_rows, half), jnp.float32),
    )
    att, send_a, keep_a, *_ = pl.pallas_call(
        functools.partial(last_kernel, xors),
        out_shape=(jax.ShapeDtypeStruct((tok_rows, local_heads * head_dim), jnp.bfloat16),) + pair_shapes + state_shapes,
        in_specs=[tree_spec] + [vmem] * (5 + len(pieces)),
        out_specs=(vmem,) * 6,
        input_output_aliases={2: 3, 3: 4, 4: 5},
        compiler_params=params,
        cost_estimate=pl.CostEstimate(flops=1_000_000_000, bytes_accessed=10_000_000, transcendentals=1_000_000),
    )(tree, q, *state, *pieces, out_weight)

    def projected(flip, part, shapes, att):
        return pl.pallas_call(
            functools.partial(project_pair, flip, part),
            out_shape=shapes,
            in_specs=[vmem, vmem],
            out_specs=(vmem, vmem),
            compiler_params=params,
            cost_estimate=pl.CostEstimate(flops=540_000_000, bytes_accessed=4_000_000, transcendentals=0),
        )(att, out_weight)

    def added(keep, arrived):
        return (keep + arrived.astype(jnp.float32)).astype(jnp.bfloat16)

    in_a = swap(send_a, "tp", tp_size, 1)
    send_b, keep_b = projected(2, 1, pair_shapes, att)
    in_b = swap(send_b, "tp", tp_size, 1)
    far_a = added(keep_a, in_a)
    from_a = swap(far_a, "tp", tp_size, 2)
    far_b = added(keep_b, in_b)
    from_b = swap(far_b, "tp", tp_size, 2)
    att, _ = lax.optimization_barrier((att, far_a))
    send_near, keep_near = projected(
        0,
        0,
        (jax.ShapeDtypeStruct((tok_rows, width), jnp.bfloat16), jax.ShapeDtypeStruct((tok_rows, width), jnp.float32)),
        att,
    )
    near_in = swap(send_near, "tp", tp_size, 1)
    from_far = jnp.concatenate([from_a, from_b], axis=1).astype(jnp.float32)
    return (keep_near + near_in.astype(jnp.float32) + from_far).astype(jnp.bfloat16)


def solution(mesh):
    return jax.shard_map(
        functools.partial(shards, mesh.shape["ctx"], mesh.shape["tp"]),
        mesh=mesh,
        in_specs=(
            P("ctx", "tp", None),
            P("ctx", "tp", None),
            P("ctx", "tp", None),
            P(),
            P("tp", None),
        ),
        out_specs=P("ctx", "tp"),
        check_vma=False,
    )
```

```python
import functools
import math

import jax
import jax.numpy as jnp
from jax import lax
from jax.experimental import pallas as pl
from jax.experimental.pallas import tpu as pltpu
from jax.sharding import PartitionSpec as P

BLOCK = 128
DIRECT_SIZE = 8
VMEM_LIMIT = 32 * 1024 * 1024


CHUNK = 256


def scores_of(k, q):
    return lax.dot_general(k, q, (((1,), (1,)), ((), ())), preferred_element_type=jnp.float32)


def weighted(v_turned, p):
    return jnp.dot(v_turned, p.astype(jnp.bfloat16), preferred_element_type=jnp.float32)


def exponent_scale(head_dim):
    return math.log2(math.e) / math.sqrt(head_dim)


def reached_mask(parents_ref):
    me = lax.axis_index("ctx")
    wanted = parents_ref[me]
    reached = jnp.int32(0)
    for step in range(1, DIRECT_SIZE):
        block = me - step
        hit = (block >= 0) & (block == wanted)
        block = jnp.maximum(block, 0)
        reached = jnp.where(hit, reached | lax.shift_left(jnp.int32(1), block), reached)
        wanted = jnp.where(hit, parents_ref[block], wanted)
    return reached


def pack_kernel(walk, k_hbm, v_hbm, parents_hbm, kv_ref, reached_ref, parents_ref, sems):
    copies = [
        pltpu.make_async_copy(parents_hbm, parents_ref, sems.at[0]),
        pltpu.make_async_copy(k_hbm, kv_ref.at[0:BLOCK, :], sems.at[1]),
        pltpu.make_async_copy(v_hbm, kv_ref.at[BLOCK:2 * BLOCK, :], sems.at[2]),
    ]
    for copy in copies:
        copy.start()
    copies[0].wait()
    reached = reached_mask(parents_ref) if walk else jnp.int32(0)
    reached_ref[...] = jnp.full(reached_ref.shape, reached, jnp.int32)
    copies[1].wait()
    copies[2].wait()


def project(att, w_ref, start, width):
    start = pl.multiple_of(start, 128)
    return jnp.dot(att, w_ref[:, pl.ds(start, width)], preferred_element_type=jnp.float32)


def absorb(scale, q_ref, k, v, m_ref, l_ref, acc_ref):
    v_turned = v.T
    for start in range(0, q_ref.shape[0], CHUNK):
        at = slice(start, start + CHUNK)
        s = scores_of(k, q_ref[at, :])
        m_old = m_ref[:, at]
        m_new = jnp.maximum(m_old, jnp.max(s, axis=0, keepdims=True))
        p = jnp.exp2((s - m_new) * scale)
        factor = jnp.exp2((m_old - m_new) * scale)
        m_ref[:, at] = m_new
        l_ref[:, at] = l_ref[:, at] * factor + jnp.sum(p, axis=0, keepdims=True)
        acc_ref[:, at] = acc_ref[:, at] * factor + weighted(v_turned, p)


def absorb_reached(xors, reached_ref, q_ref, kv_refs, state):
    scale = exponent_scale(q_ref.shape[1])
    me = lax.axis_index("ctx")
    reached = jnp.max(reached_ref[...])
    for other, kv_ref in zip(xors, kv_refs):
        @pl.when((lax.shift_right_logical(reached, me ^ other) & 1) == 1)
        def _():
            absorb(scale, q_ref, kv_ref[0:BLOCK, :], kv_ref[BLOCK:, :], *state)


def absorb_walk(parents_ref, q_ref, piece, state):
    scale = exponent_scale(q_ref.shape[1])
    me = lax.axis_index("ctx")

    def visit(step, wanted):
        block = me - step
        hit = (block >= 0) & (block == wanted)
        block = jnp.maximum(block, 0)

        @pl.when(hit)
        def _():
            start = pl.multiple_of(block * 2 * BLOCK, 2 * BLOCK)
            absorb(scale, q_ref, piece[pl.ds(start, BLOCK), :], piece[pl.ds(start + BLOCK, BLOCK), :], *state)

        return jnp.where(hit, parents_ref[block], wanted)

    lax.fori_loop(1, parents_ref.shape[0], visit, parents_ref[me])


def own_block_kernel(xors, reached_ref, q_ref, kv_ref, *refs):
    state = refs[len(xors):]
    m_ref, l_ref, acc_ref = state
    scale = exponent_scale(q_ref.shape[1])
    k = kv_ref[0:BLOCK, :]
    v_turned = kv_ref[BLOCK:, :].T
    for start in range(0, q_ref.shape[0], CHUNK):
        at = slice(start, start + CHUNK)
        s = scores_of(k, q_ref[at, :])
        key_at = lax.broadcasted_iota(jnp.int32, s.shape, 0)
        query_at = lax.broadcasted_iota(jnp.int32, s.shape, 1) & (BLOCK - 1)
        s = jnp.where(key_at <= query_at, s, -1e30)
        m = jnp.max(s, axis=0, keepdims=True)
        p = jnp.exp2((s - m) * scale)
        m_ref[:, at] = m
        l_ref[:, at] = jnp.sum(p, axis=0, keepdims=True)
        acc_ref[:, at] = weighted(v_turned, p)
    absorb_reached(xors, reached_ref, q_ref, refs[:len(xors)], state)


def others_kernel(xors, reached_ref, q_ref, m_in, l_in, acc_in, *refs):
    state = refs[len(xors):]
    absorb_reached(xors, reached_ref, q_ref, refs[:len(xors)], state)


def last_kernel(xors, tree_ref, q_ref, m_in, l_in, acc_in, *refs):
    kv_refs = refs[:max(len(xors), 1)]
    w_ref, att_ref, send_ref, keep_ref, *state = refs[len(kv_refs):]
    rows, head_dim = q_ref.shape
    if xors:
        absorb_reached(xors, tree_ref, q_ref, kv_refs, state)
    else:
        absorb_walk(tree_ref, q_ref, kv_refs[0], state)
    m_ref, l_ref, acc_ref = state

    for head in range(rows // BLOCK):
        at = slice(head * BLOCK, (head + 1) * BLOCK)
        part = acc_ref[:, at] / l_ref[:, at]
        att_ref[:, head * head_dim:(head + 1) * head_dim] = part.T.astype(jnp.bfloat16)

    project_pair(2, 0, att_ref, w_ref, send_ref, keep_ref)


def project_pair(flip, half, att_ref, w_ref, send_ref, keep_ref):
    target = lax.axis_index("tp") ^ flip
    width = w_ref.shape[1] // 4
    cols = keep_ref.shape[1]
    att = att_ref[...]
    send_ref[...] = project(att, w_ref, (target ^ 1) * width + half * cols, cols).astype(jnp.bfloat16)
    keep_ref[...] = project(att, w_ref, target * width + half * cols, cols)


def shards(ctx_size, tp_size, query_heads, key_heads, value_heads, parents, out_weight):
    tok_rows, local_heads, head_dim = query_heads.shape
    assert tok_rows == BLOCK and key_heads.shape[1] == 1 and parents.shape[0] == ctx_size and tp_size == 4
    width = out_weight.shape[1] // tp_size
    rows = local_heads * tok_rows
    params = pltpu.CompilerParams(vmem_limit_bytes=VMEM_LIMIT)
    vmem = pl.BlockSpec(memory_space=pltpu.VMEM)
    hbm = pl.BlockSpec(memory_space=pltpu.HBM)
    smem = pl.BlockSpec(memory_space=pltpu.SMEM)

    def in_hbm(x):
        return pltpu.with_memory_space_constraint(x, pltpu.HBM)

    def swap(x, axis, size, other):
        return lax.ppermute(x, axis, [(i, i ^ other) for i in range(size)])

    def forward(x, other):
        route = []
        for i in range(ctx_size):
            for j in range(tp_size):
                target = (i ^ 1, j) if i ^ other < i else (i, j ^ 1)
                route.append((i * tp_size + j, target[0] * tp_size + target[1]))
        return lax.ppermute(x, ("ctx", "tp"), route)

    kv, reached = pl.pallas_call(
        functools.partial(pack_kernel, ctx_size == DIRECT_SIZE),
        out_shape=(
            jax.ShapeDtypeStruct((2 * tok_rows, head_dim), jnp.bfloat16),
            jax.ShapeDtypeStruct((8, 128), jnp.int32),
        ),
        in_specs=[hbm, hbm, hbm],
        out_specs=(vmem, vmem),
        scratch_shapes=[pltpu.SMEM(parents.shape, jnp.int32), pltpu.SemaphoreType.DMA((3,))],
        compiler_params=params,
        cost_estimate=pl.CostEstimate(flops=8_000_000_000, bytes_accessed=130_000, transcendentals=0),
    )(in_hbm(key_heads[:, 0, :]), in_hbm(value_heads[:, 0, :]), in_hbm(parents))
    if ctx_size == DIRECT_SIZE:
        columns = [swap(kv, "ctx", ctx_size, other) for other in (4, 2, 6)]
        beside = swap(kv, "ctx", ctx_size, 1)
        pairs = [forward(x, other) for x, other in zip(columns, (4, 2, 6))]
        early, early_xors = [beside, *columns], (1, 4, 2, 6)
    else:
        early, early_xors = [], ()
    q = jnp.transpose(query_heads, (1, 0, 2)).reshape(rows, head_dim)

    m, l, acc = pl.pallas_call(
        functools.partial(own_block_kernel, early_xors),
        out_shape=(
            jax.ShapeDtypeStruct((1, rows), jnp.float32),
            jax.ShapeDtypeStruct((1, rows), jnp.float32),
            jax.ShapeDtypeStruct((head_dim, rows), jnp.float32),
        ),
        in_specs=[vmem] * (3 + len(early)),
        out_specs=(vmem,) * 3,
        compiler_params=params,
        cost_estimate=pl.CostEstimate(flops=130_000_000, bytes_accessed=1_000_000, transcendentals=260_000),
    )(reached, q, kv, *early)

    state = (m, l, acc)
    state_shapes = tuple(jax.ShapeDtypeStruct(x.shape, x.dtype) for x in state)
    if ctx_size == DIRECT_SIZE:
        def absorbed(state, xors, arrived):
            return pl.pallas_call(
                functools.partial(others_kernel, xors),
                out_shape=state_shapes,
                in_specs=[vmem] * (5 + len(xors)),
                out_specs=(vmem,) * 3,
                input_output_aliases={2: 0, 3: 1, 4: 2},
                compiler_params=params,
                cost_estimate=pl.CostEstimate(flops=270_000_000, bytes_accessed=1_000_000, transcendentals=500_000),
            )(reached, q, *state, *arrived)

        state = absorbed(state, (3, 7), pairs[1:])
        xors, pieces, tree, tree_spec = (5,), pairs[:1], reached, vmem
    else:
        xors, pieces, tree, tree_spec = (), [lax.all_gather(kv, "ctx", axis=0, tiled=True)], parents, smem

    half = width // 2
    pair_shapes = (
        jax.ShapeDtypeStruct((tok_rows, half), jnp.bfloat16),
        jax.ShapeDtypeStruct((tok_rows, half), jnp.float32),
    )
    att, send_a, keep_a, *_ = pl.pallas_call(
        functools.partial(last_kernel, xors),
        out_shape=(jax.ShapeDtypeStruct((tok_rows, local_heads * head_dim), jnp.bfloat16),) + pair_shapes + state_shapes,
        in_specs=[tree_spec] + [vmem] * (5 + len(pieces)),
        out_specs=(vmem,) * 6,
        input_output_aliases={2: 3, 3: 4, 4: 5},
        compiler_params=params,
        cost_estimate=pl.CostEstimate(flops=1_000_000_000, bytes_accessed=10_000_000, transcendentals=1_000_000),
    )(tree, q, *state, *pieces, out_weight)

    def projected(flip, part, shapes, att):
        return pl.pallas_call(
            functools.partial(project_pair, flip, part),
            out_shape=shapes,
            in_specs=[vmem, vmem],
            out_specs=(vmem, vmem),
            compiler_params=params,
            cost_estimate=pl.CostEstimate(flops=540_000_000, bytes_accessed=4_000_000, transcendentals=0),
        )(att, out_weight)

    def added(keep, arrived):
        return (keep + arrived.astype(jnp.float32)).astype(jnp.bfloat16)

    in_a = swap(send_a, "tp", tp_size, 1)
    send_b, keep_b = projected(2, 1, pair_shapes, att)
    in_b = swap(send_b, "tp", tp_size, 1)
    far_a = added(keep_a, in_a)
    from_a = swap(far_a, "tp", tp_size, 2)
    far_b = added(keep_b, in_b)
    from_b = swap(far_b, "tp", tp_size, 2)
    att, _ = lax.optimization_barrier((att, far_a))
    send_near, keep_near = projected(
        0,
        0,
        (jax.ShapeDtypeStruct((tok_rows, width), jnp.bfloat16), jax.ShapeDtypeStruct((tok_rows, width), jnp.float32)),
        att,
    )
    near_in = swap(send_near, "tp", tp_size, 1)
    from_far = jnp.concatenate([from_a, from_b], axis=1).astype(jnp.float32)
    return (keep_near + near_in.astype(jnp.float32) + from_far).astype(jnp.bfloat16)


def solution(mesh):
    return jax.shard_map(
        functools.partial(shards, mesh.shape["ctx"], mesh.shape["tp"]),
        mesh=mesh,
        in_specs=(
            P("ctx", "tp", None),
            P("ctx", "tp", None),
            P("ctx", "tp", None),
            P(),
            P("tp", None),
        ),
        out_specs=P("ctx", "tp"),
        check_vma=False,
    )
```

```python
import functools
import math

import jax
import jax.numpy as jnp
from jax import lax
from jax.experimental import pallas as pl
from jax.experimental.pallas import tpu as pltpu
from jax.sharding import PartitionSpec as P

BLOCK = 128
DIRECT_SIZE = 8
VMEM_LIMIT = 32 * 1024 * 1024


def scores_of(k, q):
    return lax.dot_general(k, q, (((1,), (1,)), ((), ())), preferred_element_type=jnp.float32)


def weighted(v, p):
    return lax.dot_general(v, p.astype(jnp.bfloat16), (((0,), (0,)), ((), ())), preferred_element_type=jnp.float32)


def exponent_scale(head_dim):
    return math.log2(math.e) / math.sqrt(head_dim)


def reached_mask(parents_ref):
    me = lax.axis_index("ctx")
    wanted = parents_ref[me]
    reached = jnp.int32(0)
    for step in range(1, DIRECT_SIZE):
        block = me - step
        hit = (block >= 0) & (block == wanted)
        block = jnp.maximum(block, 0)
        reached = jnp.where(hit, reached | lax.shift_left(jnp.int32(1), block), reached)
        wanted = jnp.where(hit, parents_ref[block], wanted)
    return reached


def pack_kernel(walk, k_hbm, v_hbm, parents_hbm, kv_ref, reached_ref, parents_ref, sems):
    copies = [
        pltpu.make_async_copy(parents_hbm, parents_ref, sems.at[0]),
        pltpu.make_async_copy(k_hbm, kv_ref.at[0:BLOCK, :], sems.at[1]),
        pltpu.make_async_copy(v_hbm, kv_ref.at[BLOCK:2 * BLOCK, :], sems.at[2]),
    ]
    for copy in copies:
        copy.start()
    copies[0].wait()
    reached = reached_mask(parents_ref) if walk else jnp.int32(0)
    reached_ref[...] = jnp.full(reached_ref.shape, reached, jnp.int32)
    copies[1].wait()
    copies[2].wait()


def project(att, w_ref, start, width):
    start = pl.multiple_of(start, 128)
    return jnp.dot(att, w_ref[:, pl.ds(start, width)], preferred_element_type=jnp.float32)


def absorb(scale, q_ref, k, v, m_ref, l_ref, acc_ref):
    s = scores_of(k, q_ref[...])
    m_old = m_ref[...]
    m_new = jnp.maximum(m_old, jnp.max(s, axis=0, keepdims=True))
    p = jnp.exp2((s - m_new) * scale)
    factor = jnp.exp2((m_old - m_new) * scale)
    m_ref[...] = m_new
    l_ref[...] = l_ref[...] * factor + jnp.sum(p, axis=0, keepdims=True)
    acc_ref[...] = acc_ref[...] * factor + weighted(v, p)


def absorb_reached(xors, reached_ref, q_ref, kv_refs, state):
    scale = exponent_scale(q_ref.shape[1])
    me = lax.axis_index("ctx")
    reached = jnp.max(reached_ref[...])
    for other, kv_ref in zip(xors, kv_refs):
        @pl.when((lax.shift_right_logical(reached, me ^ other) & 1) == 1)
        def _():
            absorb(scale, q_ref, kv_ref[0:BLOCK, :], kv_ref[BLOCK:, :], *state)


def absorb_walk(parents_ref, q_ref, piece, state):
    scale = exponent_scale(q_ref.shape[1])
    me = lax.axis_index("ctx")

    def visit(step, wanted):
        block = me - step
        hit = (block >= 0) & (block == wanted)
        block = jnp.maximum(block, 0)

        @pl.when(hit)
        def _():
            start = pl.multiple_of(block * 2 * BLOCK, 2 * BLOCK)
            absorb(scale, q_ref, piece[pl.ds(start, BLOCK), :], piece[pl.ds(start + BLOCK, BLOCK), :], *state)

        return jnp.where(hit, parents_ref[block], wanted)

    lax.fori_loop(1, parents_ref.shape[0], visit, parents_ref[me])


def own_block_kernel(xors, reached_ref, q_ref, kv_ref, *refs):
    state = refs[len(xors):]
    m_ref, l_ref, acc_ref = state
    scale = exponent_scale(q_ref.shape[1])
    s = scores_of(kv_ref[0:BLOCK, :], q_ref[...])
    key_at = lax.broadcasted_iota(jnp.int32, s.shape, 0)
    query_at = lax.broadcasted_iota(jnp.int32, s.shape, 1) & (BLOCK - 1)
    s = jnp.where(key_at <= query_at, s, -1e30)
    m = jnp.max(s, axis=0, keepdims=True)
    p = jnp.exp2((s - m) * scale)
    m_ref[...] = m
    l_ref[...] = jnp.sum(p, axis=0, keepdims=True)
    acc_ref[...] = weighted(kv_ref[BLOCK:, :], p)
    absorb_reached(xors, reached_ref, q_ref, refs[:len(xors)], state)


def others_kernel(xors, reached_ref, q_ref, m_in, l_in, acc_in, *refs):
    state = refs[len(xors):]
    absorb_reached(xors, reached_ref, q_ref, refs[:len(xors)], state)


def last_kernel(xors, tree_ref, q_ref, m_in, l_in, acc_in, *refs):
    kv_refs = refs[:max(len(xors), 1)]
    w_ref, att_ref, send_ref, keep_ref, *state = refs[len(kv_refs):]
    rows, head_dim = q_ref.shape
    if xors:
        absorb_reached(xors, tree_ref, q_ref, kv_refs, state)
    else:
        absorb_walk(tree_ref, q_ref, kv_refs[0], state)
    m_ref, l_ref, acc_ref = state

    for head in range(rows // BLOCK):
        at = slice(head * BLOCK, (head + 1) * BLOCK)
        part = acc_ref[:, at] / l_ref[:, at]
        att_ref[:, head * head_dim:(head + 1) * head_dim] = part.T.astype(jnp.bfloat16)

    project_pair(2, 0, att_ref, w_ref, send_ref, keep_ref)


def project_pair(flip, half, att_ref, w_ref, send_ref, keep_ref):
    target = lax.axis_index("tp") ^ flip
    width = w_ref.shape[1] // 4
    cols = keep_ref.shape[1]
    att = att_ref[...]
    send_ref[...] = project(att, w_ref, (target ^ 1) * width + half * cols, cols).astype(jnp.bfloat16)
    keep_ref[...] = project(att, w_ref, target * width + half * cols, cols)


def shards(ctx_size, tp_size, query_heads, key_heads, value_heads, parents, out_weight):
    tok_rows, local_heads, head_dim = query_heads.shape
    assert tok_rows == BLOCK and key_heads.shape[1] == 1 and parents.shape[0] == ctx_size and tp_size == 4
    width = out_weight.shape[1] // tp_size
    rows = local_heads * tok_rows
    params = pltpu.CompilerParams(vmem_limit_bytes=VMEM_LIMIT)
    vmem = pl.BlockSpec(memory_space=pltpu.VMEM)
    hbm = pl.BlockSpec(memory_space=pltpu.HBM)
    smem = pl.BlockSpec(memory_space=pltpu.SMEM)

    def in_hbm(x):
        return pltpu.with_memory_space_constraint(x, pltpu.HBM)

    def swap(x, axis, size, other):
        return lax.ppermute(x, axis, [(i, i ^ other) for i in range(size)])

    def forward(x, other):
        route = []
        for i in range(ctx_size):
            for j in range(tp_size):
                target = (i ^ 1, j) if i ^ other < i else (i, j ^ 1)
                route.append((i * tp_size + j, target[0] * tp_size + target[1]))
        return lax.ppermute(x, ("ctx", "tp"), route)

    kv, reached = pl.pallas_call(
        functools.partial(pack_kernel, ctx_size == DIRECT_SIZE),
        out_shape=(
            jax.ShapeDtypeStruct((2 * tok_rows, head_dim), jnp.bfloat16),
            jax.ShapeDtypeStruct((8, 128), jnp.int32),
        ),
        in_specs=[hbm, hbm, hbm],
        out_specs=(vmem, vmem),
        scratch_shapes=[pltpu.SMEM(parents.shape, jnp.int32), pltpu.SemaphoreType.DMA((3,))],
        compiler_params=params,
        cost_estimate=pl.CostEstimate(flops=8_000_000_000, bytes_accessed=130_000, transcendentals=0),
    )(in_hbm(key_heads[:, 0, :]), in_hbm(value_heads[:, 0, :]), in_hbm(parents))
    if ctx_size == DIRECT_SIZE:
        by_6, by_1, by_4, by_2 = [swap(kv, "ctx", ctx_size, other) for other in (6, 1, 4, 2)]
        early, early_xors = [by_1], (1,)
    else:
        early, early_xors = [], ()
    q = jnp.transpose(query_heads, (1, 0, 2)).reshape(rows, head_dim)

    m, l, acc = pl.pallas_call(
        functools.partial(own_block_kernel, early_xors),
        out_shape=(
            jax.ShapeDtypeStruct((1, rows), jnp.float32),
            jax.ShapeDtypeStruct((1, rows), jnp.float32),
            jax.ShapeDtypeStruct((head_dim, rows), jnp.float32),
        ),
        in_specs=[vmem] * (3 + len(early)),
        out_specs=(vmem,) * 3,
        compiler_params=params,
        cost_estimate=pl.CostEstimate(flops=130_000_000, bytes_accessed=1_000_000, transcendentals=260_000),
    )(reached, q, kv, *early)

    state = (m, l, acc)
    state_shapes = tuple(jax.ShapeDtypeStruct(x.shape, x.dtype) for x in state)
    if ctx_size == DIRECT_SIZE:
        def absorbed(state, xors, arrived):
            return pl.pallas_call(
                functools.partial(others_kernel, xors),
                out_shape=state_shapes,
                in_specs=[vmem] * (5 + len(xors)),
                out_specs=(vmem,) * 3,
                input_output_aliases={2: 0, 3: 1, 4: 2},
                compiler_params=params,
                cost_estimate=pl.CostEstimate(flops=270_000_000, bytes_accessed=1_000_000, transcendentals=500_000),
            )(reached, q, *state, *arrived)

        by_7 = forward(by_6, 6)
        by_3 = swap(by_1, "ctx", ctx_size, 2)
        by_5 = forward(by_4, 4)
        state = absorbed(state, (2, 4, 6), [by_2, by_4, by_6])
        state = absorbed(state, (3, 7), [by_3, by_7])
        xors, pieces, tree, tree_spec = (5,), [by_5], reached, vmem
    else:
        xors, pieces, tree, tree_spec = (), [lax.all_gather(kv, "ctx", axis=0, tiled=True)], parents, smem

    half = width // 2
    pair_shapes = (
        jax.ShapeDtypeStruct((tok_rows, half), jnp.bfloat16),
        jax.ShapeDtypeStruct((tok_rows, half), jnp.float32),
    )
    att, send_a, keep_a, *_ = pl.pallas_call(
        functools.partial(last_kernel, xors),
        out_shape=(jax.ShapeDtypeStruct((tok_rows, local_heads * head_dim), jnp.bfloat16),) + pair_shapes + state_shapes,
        in_specs=[tree_spec] + [vmem] * (5 + len(pieces)),
        out_specs=(vmem,) * 6,
        input_output_aliases={2: 3, 3: 4, 4: 5},
        compiler_params=params,
        cost_estimate=pl.CostEstimate(flops=1_000_000_000, bytes_accessed=10_000_000, transcendentals=1_000_000),
    )(tree, q, *state, *pieces, out_weight)

    def projected(flip, part, shapes, att):
        return pl.pallas_call(
            functools.partial(project_pair, flip, part),
            out_shape=shapes,
            in_specs=[vmem, vmem],
            out_specs=(vmem, vmem),
            compiler_params=params,
            cost_estimate=pl.CostEstimate(flops=540_000_000, bytes_accessed=4_000_000, transcendentals=0),
        )(att, out_weight)

    def added(keep, arrived):
        return (keep + arrived.astype(jnp.float32)).astype(jnp.bfloat16)

    in_a = swap(send_a, "tp", tp_size, 1)
    send_b, keep_b = projected(2, 1, pair_shapes, att)
    in_b = swap(send_b, "tp", tp_size, 1)
    far_a = added(keep_a, in_a)
    from_a = swap(far_a, "tp", tp_size, 2)
    far_b = added(keep_b, in_b)
    from_b = swap(far_b, "tp", tp_size, 2)
    att, _ = lax.optimization_barrier((att, far_a))
    send_near, keep_near = projected(
        0,
        0,
        (jax.ShapeDtypeStruct((tok_rows, width), jnp.bfloat16), jax.ShapeDtypeStruct((tok_rows, width), jnp.float32)),
        att,
    )
    near_in = swap(send_near, "tp", tp_size, 1)
    from_far = jnp.concatenate([from_a, from_b], axis=1).astype(jnp.float32)
    return (keep_near + near_in.astype(jnp.float32) + from_far).astype(jnp.bfloat16)


def solution(mesh):
    return jax.shard_map(
        functools.partial(shards, mesh.shape["ctx"], mesh.shape["tp"]),
        mesh=mesh,
        in_specs=(
            P("ctx", "tp", None),
            P("ctx", "tp", None),
            P("ctx", "tp", None),
            P(),
            P("tp", None),
        ),
        out_specs=P("ctx", "tp"),
        check_vma=False,
    )
```

```python
import functools
import math

import jax
import jax.numpy as jnp
from jax import lax
from jax.experimental import pallas as pl
from jax.experimental.pallas import tpu as pltpu
from jax.sharding import PartitionSpec as P

BLOCK = 128
DIRECT_SIZE = 8
VMEM_LIMIT = 32 * 1024 * 1024


def scores_of(q, k):
    return lax.dot_general(q, k, (((1,), (1,)), ((), ())), preferred_element_type=jnp.float32)


def weighted_and_sums(p, v):
    beside = jnp.concatenate([v, jnp.ones_like(v)], axis=1)
    both = jnp.dot(p.astype(jnp.bfloat16), beside, preferred_element_type=jnp.float32)
    return both[:, :v.shape[1]], both[:, v.shape[1]:]


def exponent_scale(head_dim):
    return math.log2(math.e) / math.sqrt(head_dim)


def reached_mask(parents_ref):
    me = lax.axis_index("ctx")
    wanted = parents_ref[me]
    reached = jnp.int32(0)
    for step in range(1, DIRECT_SIZE):
        block = me - step
        hit = (block >= 0) & (block == wanted)
        block = jnp.maximum(block, 0)
        reached = jnp.where(hit, reached | lax.shift_left(jnp.int32(1), block), reached)
        wanted = jnp.where(hit, parents_ref[block], wanted)
    return reached


def pack_kernel(walk, k_hbm, v_hbm, parents_hbm, kv_ref, reached_ref, parents_ref, sems):
    copies = [
        pltpu.make_async_copy(parents_hbm, parents_ref, sems.at[0]),
        pltpu.make_async_copy(k_hbm, kv_ref.at[0:BLOCK, :], sems.at[1]),
        pltpu.make_async_copy(v_hbm, kv_ref.at[BLOCK:2 * BLOCK, :], sems.at[2]),
    ]
    for copy in copies:
        copy.start()
    copies[0].wait()
    reached = reached_mask(parents_ref) if walk else jnp.int32(0)
    reached_ref[...] = jnp.full(reached_ref.shape, reached, jnp.int32)
    copies[1].wait()
    copies[2].wait()


def project(att, w_ref, start, width):
    start = pl.multiple_of(start, 128)
    return jnp.dot(att, w_ref[:, pl.ds(start, width)], preferred_element_type=jnp.float32)


def absorb(scale, q_ref, k, v, m_ref, l_ref, acc_ref):
    s = scores_of(q_ref[...], k)
    m_old = m_ref[...]
    m_new = jnp.maximum(m_old, jnp.max(s, axis=1, keepdims=True))
    p = jnp.exp2((s - m_new) * scale)
    factor = jnp.exp2((m_old - m_new) * scale)
    part, sums = weighted_and_sums(p, v)
    m_ref[...] = m_new
    l_ref[...] = l_ref[...] * factor + sums
    acc_ref[...] = acc_ref[...] * factor + part


def absorb_reached(xors, reached_ref, q_ref, kv_refs, state):
    scale = exponent_scale(q_ref.shape[1])
    me = lax.axis_index("ctx")
    reached = jnp.max(reached_ref[...])
    for other, kv_ref in zip(xors, kv_refs):
        @pl.when((lax.shift_right_logical(reached, me ^ other) & 1) == 1)
        def _():
            absorb(scale, q_ref, kv_ref[0:BLOCK, :], kv_ref[BLOCK:, :], *state)


def absorb_walk(parents_ref, q_ref, piece, state):
    scale = exponent_scale(q_ref.shape[1])
    me = lax.axis_index("ctx")

    def visit(step, wanted):
        block = me - step
        hit = (block >= 0) & (block == wanted)
        block = jnp.maximum(block, 0)

        @pl.when(hit)
        def _():
            start = pl.multiple_of(block * 2 * BLOCK, 2 * BLOCK)
            absorb(scale, q_ref, piece[pl.ds(start, BLOCK), :], piece[pl.ds(start + BLOCK, BLOCK), :], *state)

        return jnp.where(hit, parents_ref[block], wanted)

    lax.fori_loop(1, parents_ref.shape[0], visit, parents_ref[me])


def own_block_kernel(xors, reached_ref, q_ref, kv_ref, *refs):
    state = refs[len(xors):]
    m_ref, l_ref, acc_ref = state
    scale = exponent_scale(q_ref.shape[1])
    s = scores_of(q_ref[...], kv_ref[0:BLOCK, :])
    query_at = lax.broadcasted_iota(jnp.int32, s.shape, 0) & (BLOCK - 1)
    key_at = lax.broadcasted_iota(jnp.int32, s.shape, 1)
    s = jnp.where(key_at <= query_at, s, -1e30)
    m = jnp.broadcast_to(jnp.max(s, axis=1, keepdims=True), s.shape)
    p = jnp.exp2((s - m) * scale)
    part, sums = weighted_and_sums(p, kv_ref[BLOCK:, :])
    m_ref[...] = m
    l_ref[...] = sums
    acc_ref[...] = part
    absorb_reached(xors, reached_ref, q_ref, refs[:len(xors)], state)


def others_kernel(xors, reached_ref, q_ref, m_in, l_in, acc_in, *refs):
    state = refs[len(xors):]
    absorb_reached(xors, reached_ref, q_ref, refs[:len(xors)], state)


def last_kernel(xors, tree_ref, q_ref, m_in, l_in, acc_in, *refs):
    kv_refs = refs[:max(len(xors), 1)]
    w_ref, att_ref, send_ref, keep_ref, *state = refs[len(kv_refs):]
    rows, head_dim = q_ref.shape
    if xors:
        absorb_reached(xors, tree_ref, q_ref, kv_refs, state)
    else:
        absorb_walk(tree_ref, q_ref, kv_refs[0], state)
    m_ref, l_ref, acc_ref = state

    for head in range(rows // BLOCK):
        at = slice(head * BLOCK, (head + 1) * BLOCK)
        att_ref[:, head * head_dim:(head + 1) * head_dim] = (acc_ref[at, :] / l_ref[at, :]).astype(jnp.bfloat16)

    project_pair(2, 0, att_ref, w_ref, send_ref, keep_ref)


def project_pair(flip, half, att_ref, w_ref, send_ref, keep_ref):
    target = lax.axis_index("tp") ^ flip
    width = w_ref.shape[1] // 4
    cols = keep_ref.shape[1]
    att = att_ref[...]
    send_ref[...] = project(att, w_ref, (target ^ 1) * width + half * cols, cols).astype(jnp.bfloat16)
    keep_ref[...] = project(att, w_ref, target * width + half * cols, cols)


def shards(ctx_size, tp_size, query_heads, key_heads, value_heads, parents, out_weight):
    tok_rows, local_heads, head_dim = query_heads.shape
    assert tok_rows == BLOCK and key_heads.shape[1] == 1 and parents.shape[0] == ctx_size and tp_size == 4
    width = out_weight.shape[1] // tp_size
    rows = local_heads * tok_rows
    params = pltpu.CompilerParams(vmem_limit_bytes=VMEM_LIMIT)
    vmem = pl.BlockSpec(memory_space=pltpu.VMEM)
    hbm = pl.BlockSpec(memory_space=pltpu.HBM)
    smem = pl.BlockSpec(memory_space=pltpu.SMEM)

    def in_hbm(x):
        return pltpu.with_memory_space_constraint(x, pltpu.HBM)

    def swap(x, axis, size, other):
        return lax.ppermute(x, axis, [(i, i ^ other) for i in range(size)])

    def forward(x, other):
        route = []
        for i in range(ctx_size):
            for j in range(tp_size):
                target = (i ^ 1, j) if i ^ other < i else (i, j ^ 1)
                route.append((i * tp_size + j, target[0] * tp_size + target[1]))
        return lax.ppermute(x, ("ctx", "tp"), route)

    kv, reached = pl.pallas_call(
        functools.partial(pack_kernel, ctx_size == DIRECT_SIZE),
        out_shape=(
            jax.ShapeDtypeStruct((2 * tok_rows, head_dim), jnp.bfloat16),
            jax.ShapeDtypeStruct((8, 128), jnp.int32),
        ),
        in_specs=[hbm, hbm, hbm],
        out_specs=(vmem, vmem),
        scratch_shapes=[pltpu.SMEM(parents.shape, jnp.int32), pltpu.SemaphoreType.DMA((3,))],
        compiler_params=params,
        cost_estimate=pl.CostEstimate(flops=8_000_000_000, bytes_accessed=130_000, transcendentals=0),
    )(in_hbm(key_heads[:, 0, :]), in_hbm(value_heads[:, 0, :]), in_hbm(parents))
    if ctx_size == DIRECT_SIZE:
        columns = [swap(kv, "ctx", ctx_size, other) for other in (4, 2, 6)]
        beside = swap(kv, "ctx", ctx_size, 1)
        pairs = [forward(x, other) for x, other in zip(columns, (4, 2, 6))]
        early, early_xors = [beside, *columns], (1, 4, 2, 6)
    else:
        early, early_xors = [], ()
    q = jnp.transpose(query_heads, (1, 0, 2)).reshape(rows, head_dim)

    m, l, acc = pl.pallas_call(
        functools.partial(own_block_kernel, early_xors),
        out_shape=(
            jax.ShapeDtypeStruct((rows, BLOCK), jnp.float32),
            jax.ShapeDtypeStruct((rows, head_dim), jnp.float32),
            jax.ShapeDtypeStruct((rows, head_dim), jnp.float32),
        ),
        in_specs=[vmem] * (3 + len(early)),
        out_specs=(vmem,) * 3,
        compiler_params=params,
        cost_estimate=pl.CostEstimate(flops=130_000_000, bytes_accessed=1_000_000, transcendentals=260_000),
    )(reached, q, kv, *early)

    state = (m, l, acc)
    state_shapes = tuple(jax.ShapeDtypeStruct(x.shape, x.dtype) for x in state)
    if ctx_size == DIRECT_SIZE:
        def absorbed(state, xors, arrived):
            return pl.pallas_call(
                functools.partial(others_kernel, xors),
                out_shape=state_shapes,
                in_specs=[vmem] * (5 + len(xors)),
                out_specs=(vmem,) * 3,
                input_output_aliases={2: 0, 3: 1, 4: 2},
                compiler_params=params,
                cost_estimate=pl.CostEstimate(flops=270_000_000, bytes_accessed=1_000_000, transcendentals=500_000),
            )(reached, q, *state, *arrived)

        state = absorbed(state, (3, 7), pairs[1:])
        xors, pieces, tree, tree_spec = (5,), pairs[:1], reached, vmem
    else:
        xors, pieces, tree, tree_spec = (), [lax.all_gather(kv, "ctx", axis=0, tiled=True)], parents, smem

    half = width // 2
    pair_shapes = (
        jax.ShapeDtypeStruct((tok_rows, half), jnp.bfloat16),
        jax.ShapeDtypeStruct((tok_rows, half), jnp.float32),
    )
    att, send_a, keep_a, *_ = pl.pallas_call(
        functools.partial(last_kernel, xors),
        out_shape=(jax.ShapeDtypeStruct((tok_rows, local_heads * head_dim), jnp.bfloat16),) + pair_shapes + state_shapes,
        in_specs=[tree_spec] + [vmem] * (5 + len(pieces)),
        out_specs=(vmem,) * 6,
        input_output_aliases={2: 3, 3: 4, 4: 5},
        compiler_params=params,
        cost_estimate=pl.CostEstimate(flops=1_000_000_000, bytes_accessed=10_000_000, transcendentals=1_000_000),
    )(tree, q, *state, *pieces, out_weight)

    def projected(flip, part, shapes, att):
        return pl.pallas_call(
            functools.partial(project_pair, flip, part),
            out_shape=shapes,
            in_specs=[vmem, vmem],
            out_specs=(vmem, vmem),
            compiler_params=params,
            cost_estimate=pl.CostEstimate(flops=540_000_000, bytes_accessed=4_000_000, transcendentals=0),
        )(att, out_weight)

    def added(keep, arrived):
        return (keep + arrived.astype(jnp.float32)).astype(jnp.bfloat16)

    in_a = swap(send_a, "tp", tp_size, 1)
    send_b, keep_b = projected(2, 1, pair_shapes, att)
    in_b = swap(send_b, "tp", tp_size, 1)
    far_a = added(keep_a, in_a)
    from_a = swap(far_a, "tp", tp_size, 2)
    far_b = added(keep_b, in_b)
    from_b = swap(far_b, "tp", tp_size, 2)
    att, _ = lax.optimization_barrier((att, far_a))
    send_near, keep_near = projected(
        0,
        0,
        (jax.ShapeDtypeStruct((tok_rows, width), jnp.bfloat16), jax.ShapeDtypeStruct((tok_rows, width), jnp.float32)),
        att,
    )
    near_in = swap(send_near, "tp", tp_size, 1)
    from_far = jnp.concatenate([from_a, from_b], axis=1).astype(jnp.float32)
    return (keep_near + near_in.astype(jnp.float32) + from_far).astype(jnp.bfloat16)


def solution(mesh):
    return jax.shard_map(
        functools.partial(shards, mesh.shape["ctx"], mesh.shape["tp"]),
        mesh=mesh,
        in_specs=(
            P("ctx", "tp", None),
            P("ctx", "tp", None),
            P("ctx", "tp", None),
            P(),
            P("tp", None),
        ),
        out_specs=P("ctx", "tp"),
        check_vma=False,
    )
```

```python
import functools
import math

import jax
import jax.numpy as jnp
from jax import lax
from jax.experimental import pallas as pl
from jax.experimental.pallas import tpu as pltpu
from jax.sharding import PartitionSpec as P

BLOCK = 128
DIRECT_SIZE = 8
VMEM_LIMIT = 32 * 1024 * 1024


def scores_of(k, q):
    return lax.dot_general(k, q, (((1,), (1,)), ((), ())), preferred_element_type=jnp.float32)


def weighted(v, p):
    return lax.dot_general(v, p.astype(jnp.bfloat16), (((0,), (0,)), ((), ())), preferred_element_type=jnp.float32)


def exponent_scale(head_dim):
    return math.log2(math.e) / math.sqrt(head_dim)


def reached_mask(parents_ref):
    me = lax.axis_index("ctx")
    wanted = parents_ref[me]
    reached = jnp.int32(0)
    for step in range(1, DIRECT_SIZE):
        block = me - step
        hit = (block >= 0) & (block == wanted)
        block = jnp.maximum(block, 0)
        reached = jnp.where(hit, reached | lax.shift_left(jnp.int32(1), block), reached)
        wanted = jnp.where(hit, parents_ref[block], wanted)
    return reached


def pack_kernel(walk, k_hbm, v_hbm, parents_hbm, kv_ref, reached_ref, parents_ref, sems):
    copies = [
        pltpu.make_async_copy(parents_hbm, parents_ref, sems.at[0]),
        pltpu.make_async_copy(k_hbm, kv_ref.at[0:BLOCK, :], sems.at[1]),
        pltpu.make_async_copy(v_hbm, kv_ref.at[BLOCK:2 * BLOCK, :], sems.at[2]),
    ]
    for copy in copies:
        copy.start()
    copies[0].wait()
    reached = reached_mask(parents_ref) if walk else jnp.int32(0)
    reached_ref[...] = jnp.full(reached_ref.shape, reached, jnp.int32)
    copies[1].wait()
    copies[2].wait()


def project(att, w_ref, start, width):
    start = pl.multiple_of(start, 128)
    return jnp.dot(att, w_ref[:, pl.ds(start, width)], preferred_element_type=jnp.float32)


def absorb(scale, q_ref, k, v, m_ref, l_ref, acc_ref):
    s = scores_of(k, q_ref[...])
    m_old = m_ref[...]
    m_new = jnp.maximum(m_old, jnp.max(s, axis=0, keepdims=True))
    p = jnp.exp2((s - m_new) * scale)
    factor = jnp.exp2((m_old - m_new) * scale)
    m_ref[...] = m_new
    l_ref[...] = l_ref[...] * factor + jnp.sum(p, axis=0, keepdims=True)
    acc_ref[...] = acc_ref[...] * factor + weighted(v, p)


def absorb_reached(xors, reached_ref, q_ref, kv_refs, state):
    scale = exponent_scale(q_ref.shape[1])
    me = lax.axis_index("ctx")
    reached = jnp.max(reached_ref[...])
    for other, kv_ref in zip(xors, kv_refs):
        @pl.when((lax.shift_right_logical(reached, me ^ other) & 1) == 1)
        def _():
            absorb(scale, q_ref, kv_ref[0:BLOCK, :], kv_ref[BLOCK:, :], *state)


def absorb_walk(parents_ref, q_ref, piece, state):
    scale = exponent_scale(q_ref.shape[1])
    me = lax.axis_index("ctx")

    def visit(step, wanted):
        block = me - step
        hit = (block >= 0) & (block == wanted)
        block = jnp.maximum(block, 0)

        @pl.when(hit)
        def _():
            start = pl.multiple_of(block * 2 * BLOCK, 2 * BLOCK)
            absorb(scale, q_ref, piece[pl.ds(start, BLOCK), :], piece[pl.ds(start + BLOCK, BLOCK), :], *state)

        return jnp.where(hit, parents_ref[block], wanted)

    lax.fori_loop(1, parents_ref.shape[0], visit, parents_ref[me])


def own_block_kernel(xors, reached_ref, q_ref, kv_ref, *refs):
    state = refs[len(xors):]
    m_ref, l_ref, acc_ref = state
    scale = exponent_scale(q_ref.shape[1])
    s = scores_of(kv_ref[0:BLOCK, :], q_ref[...])
    key_at = lax.broadcasted_iota(jnp.int32, s.shape, 0)
    query_at = lax.broadcasted_iota(jnp.int32, s.shape, 1) & (BLOCK - 1)
    s = jnp.where(key_at <= query_at, s, -1e30)
    m = jnp.max(s, axis=0, keepdims=True)
    p = jnp.exp2((s - m) * scale)
    m_ref[...] = m
    l_ref[...] = jnp.sum(p, axis=0, keepdims=True)
    acc_ref[...] = weighted(kv_ref[BLOCK:, :], p)
    absorb_reached(xors, reached_ref, q_ref, refs[:len(xors)], state)


def others_kernel(xors, reached_ref, q_ref, m_in, l_in, acc_in, *refs):
    state = refs[len(xors):]
    absorb_reached(xors, reached_ref, q_ref, refs[:len(xors)], state)


def last_kernel(xors, tree_ref, q_ref, m_in, l_in, acc_in, *refs):
    kv_refs = refs[:max(len(xors), 1)]
    w_ref, att_ref, send_ref, keep_ref, *state = refs[len(kv_refs):]
    rows, head_dim = q_ref.shape
    if xors:
        absorb_reached(xors, tree_ref, q_ref, kv_refs, state)
    else:
        absorb_walk(tree_ref, q_ref, kv_refs[0], state)
    m_ref, l_ref, acc_ref = state

    for head in range(rows // BLOCK):
        at = slice(head * BLOCK, (head + 1) * BLOCK)
        part = acc_ref[:, at] / l_ref[:, at]
        att_ref[:, head * head_dim:(head + 1) * head_dim] = part.T.astype(jnp.bfloat16)

    project_pair(2, 0, att_ref, w_ref, send_ref, keep_ref)


def project_pair(flip, half, att_ref, w_ref, send_ref, keep_ref):
    target = lax.axis_index("tp") ^ flip
    width = w_ref.shape[1] // 4
    cols = keep_ref.shape[1]
    att = att_ref[...]
    send_ref[...] = project(att, w_ref, (target ^ 1) * width + half * cols, cols).astype(jnp.bfloat16)
    keep_ref[...] = project(att, w_ref, target * width + half * cols, cols)


def shards(ctx_size, tp_size, query_heads, key_heads, value_heads, parents, out_weight):
    tok_rows, local_heads, head_dim = query_heads.shape
    assert tok_rows == BLOCK and key_heads.shape[1] == 1 and parents.shape[0] == ctx_size and tp_size == 4
    width = out_weight.shape[1] // tp_size
    rows = local_heads * tok_rows
    params = pltpu.CompilerParams(vmem_limit_bytes=VMEM_LIMIT)
    vmem = pl.BlockSpec(memory_space=pltpu.VMEM)
    hbm = pl.BlockSpec(memory_space=pltpu.HBM)
    smem = pl.BlockSpec(memory_space=pltpu.SMEM)

    def in_hbm(x):
        return pltpu.with_memory_space_constraint(x, pltpu.HBM)

    def swap(x, axis, size, other):
        return lax.ppermute(x, axis, [(i, i ^ other) for i in range(size)])

    def forward(x, other):
        route = []
        for i in range(ctx_size):
            for j in range(tp_size):
                target = (i ^ 1, j) if i ^ other < i else (i, j ^ 1)
                route.append((i * tp_size + j, target[0] * tp_size + target[1]))
        return lax.ppermute(x, ("ctx", "tp"), route)

    kv, reached = pl.pallas_call(
        functools.partial(pack_kernel, ctx_size == DIRECT_SIZE),
        out_shape=(
            jax.ShapeDtypeStruct((2 * tok_rows, head_dim), jnp.bfloat16),
            jax.ShapeDtypeStruct((8, 128), jnp.int32),
        ),
        in_specs=[hbm, hbm, hbm],
        out_specs=(vmem, vmem),
        scratch_shapes=[pltpu.SMEM(parents.shape, jnp.int32), pltpu.SemaphoreType.DMA((3,))],
        compiler_params=params,
        cost_estimate=pl.CostEstimate(flops=8_000_000_000, bytes_accessed=130_000, transcendentals=0),
    )(in_hbm(key_heads[:, 0, :]), in_hbm(value_heads[:, 0, :]), in_hbm(parents))
    early, early_xors = [], ()
    if ctx_size == DIRECT_SIZE:
        columns = [swap(kv, "ctx", ctx_size, other) for other in (2, 4, 6)]
        beside = swap(kv, "ctx", ctx_size, 1)
    q = jnp.transpose(query_heads, (1, 0, 2)).reshape(rows, head_dim)

    m, l, acc = pl.pallas_call(
        functools.partial(own_block_kernel, early_xors),
        out_shape=(
            jax.ShapeDtypeStruct((1, rows), jnp.float32),
            jax.ShapeDtypeStruct((1, rows), jnp.float32),
            jax.ShapeDtypeStruct((head_dim, rows), jnp.float32),
        ),
        in_specs=[vmem] * (3 + len(early)),
        out_specs=(vmem,) * 3,
        compiler_params=params,
        cost_estimate=pl.CostEstimate(flops=130_000_000, bytes_accessed=1_000_000, transcendentals=260_000),
    )(reached, q, kv, *early)

    if ctx_size == DIRECT_SIZE:
        columns[2], m = lax.optimization_barrier((columns[2], m))
        pairs = [forward(x, other) for x, other in zip(columns, (2, 4, 6))]
    state = (m, l, acc)
    state_shapes = tuple(jax.ShapeDtypeStruct(x.shape, x.dtype) for x in state)
    if ctx_size == DIRECT_SIZE:
        def absorbed(state, xors, arrived):
            return pl.pallas_call(
                functools.partial(others_kernel, xors),
                out_shape=state_shapes,
                in_specs=[vmem] * (5 + len(xors)),
                out_specs=(vmem,) * 3,
                input_output_aliases={2: 0, 3: 1, 4: 2},
                compiler_params=params,
                cost_estimate=pl.CostEstimate(flops=270_000_000, bytes_accessed=1_000_000, transcendentals=500_000),
            )(reached, q, *state, *arrived)

        state = absorbed(state, (1, 2, 4, 6), [beside, *columns])
        state = absorbed(state, (5, 7), pairs[1:])
        xors, pieces, tree, tree_spec = (3,), pairs[:1], reached, vmem
    else:
        xors, pieces, tree, tree_spec = (), [lax.all_gather(kv, "ctx", axis=0, tiled=True)], parents, smem

    half = width // 2
    pair_shapes = (
        jax.ShapeDtypeStruct((tok_rows, half), jnp.bfloat16),
        jax.ShapeDtypeStruct((tok_rows, half), jnp.float32),
    )
    att, send_a, keep_a, *_ = pl.pallas_call(
        functools.partial(last_kernel, xors),
        out_shape=(jax.ShapeDtypeStruct((tok_rows, local_heads * head_dim), jnp.bfloat16),) + pair_shapes + state_shapes,
        in_specs=[tree_spec] + [vmem] * (5 + len(pieces)),
        out_specs=(vmem,) * 6,
        input_output_aliases={2: 3, 3: 4, 4: 5},
        compiler_params=params,
        cost_estimate=pl.CostEstimate(flops=1_000_000_000, bytes_accessed=10_000_000, transcendentals=1_000_000),
    )(tree, q, *state, *pieces, out_weight)

    def projected(flip, part, shapes, att):
        return pl.pallas_call(
            functools.partial(project_pair, flip, part),
            out_shape=shapes,
            in_specs=[vmem, vmem],
            out_specs=(vmem, vmem),
            compiler_params=params,
            cost_estimate=pl.CostEstimate(flops=540_000_000, bytes_accessed=4_000_000, transcendentals=0),
        )(att, out_weight)

    def added(keep, arrived):
        return (keep + arrived.astype(jnp.float32)).astype(jnp.bfloat16)

    in_a = swap(send_a, "tp", tp_size, 1)
    send_b, keep_b = projected(2, 1, pair_shapes, att)
    in_b = swap(send_b, "tp", tp_size, 1)
    far_a = added(keep_a, in_a)
    from_a = swap(far_a, "tp", tp_size, 2)
    far_b = added(keep_b, in_b)
    from_b = swap(far_b, "tp", tp_size, 2)
    att, _ = lax.optimization_barrier((att, far_a))
    send_near, keep_near = projected(
        0,
        0,
        (jax.ShapeDtypeStruct((tok_rows, width), jnp.bfloat16), jax.ShapeDtypeStruct((tok_rows, width), jnp.float32)),
        att,
    )
    near_in = swap(send_near, "tp", tp_size, 1)
    from_far = jnp.concatenate([from_a, from_b], axis=1).astype(jnp.float32)
    return (keep_near + near_in.astype(jnp.float32) + from_far).astype(jnp.bfloat16)


def solution(mesh):
    return jax.shard_map(
        functools.partial(shards, mesh.shape["ctx"], mesh.shape["tp"]),
        mesh=mesh,
        in_specs=(
            P("ctx", "tp", None),
            P("ctx", "tp", None),
            P("ctx", "tp", None),
            P(),
            P("tp", None),
        ),
        out_specs=P("ctx", "tp"),
        check_vma=False,
    )
```

```python
import functools
import math

import jax
import jax.numpy as jnp
from jax import lax
from jax.experimental import pallas as pl
from jax.experimental.pallas import tpu as pltpu
from jax.sharding import PartitionSpec as P

BLOCK = 128
DIRECT_SIZE = 8
VMEM_LIMIT = 32 * 1024 * 1024


def scores_of(k, q):
    return lax.dot_general(k, q, (((1,), (1,)), ((), ())), preferred_element_type=jnp.float32)


def weighted(v, p):
    return lax.dot_general(v, p.astype(jnp.bfloat16), (((0,), (0,)), ((), ())), preferred_element_type=jnp.float32)


def exponent_scale(head_dim):
    return math.log2(math.e) / math.sqrt(head_dim)


def reached_mask(parents_ref):
    me = lax.axis_index("ctx")
    wanted = parents_ref[me]
    reached = jnp.int32(0)
    for step in range(1, DIRECT_SIZE):
        block = me - step
        hit = (block >= 0) & (block == wanted)
        block = jnp.maximum(block, 0)
        reached = jnp.where(hit, reached | lax.shift_left(jnp.int32(1), block), reached)
        wanted = jnp.where(hit, parents_ref[block], wanted)
    return reached


def pack_kernel(walk, k_hbm, v_hbm, parents_hbm, kv_ref, reached_ref, parents_ref, sems):
    copies = [
        pltpu.make_async_copy(parents_hbm, parents_ref, sems.at[0]),
        pltpu.make_async_copy(k_hbm, kv_ref.at[0:BLOCK, :], sems.at[1]),
        pltpu.make_async_copy(v_hbm, kv_ref.at[BLOCK:2 * BLOCK, :], sems.at[2]),
    ]
    for copy in copies:
        copy.start()
    copies[0].wait()
    reached = reached_mask(parents_ref) if walk else jnp.int32(0)
    reached_ref[...] = jnp.full(reached_ref.shape, reached, jnp.int32)
    copies[1].wait()
    copies[2].wait()


def project(att, w_ref, start, width):
    start = pl.multiple_of(start, 128)
    return jnp.dot(att, w_ref[:, pl.ds(start, width)], preferred_element_type=jnp.float32)


def absorb(scale, q_ref, k, v, m_ref, l_ref, acc_ref):
    s = scores_of(k, q_ref[...])
    m_old = m_ref[...]
    m_new = jnp.maximum(m_old, jnp.max(s, axis=0, keepdims=True))
    p = jnp.exp2((s - m_new) * scale)
    factor = jnp.exp2((m_old - m_new) * scale)
    m_ref[...] = m_new
    l_ref[...] = l_ref[...] * factor + jnp.sum(p, axis=0, keepdims=True)
    acc_ref[...] = acc_ref[...] * factor + weighted(v, p)


def absorb_reached(xors, reached_ref, q_ref, kv_refs, state):
    scale = exponent_scale(q_ref.shape[1])
    me = lax.axis_index("ctx")
    reached = jnp.max(reached_ref[...])
    for other, kv_ref in zip(xors, kv_refs):
        @pl.when((lax.shift_right_logical(reached, me ^ other) & 1) == 1)
        def _():
            absorb(scale, q_ref, kv_ref[0:BLOCK, :], kv_ref[BLOCK:, :], *state)


def absorb_walk(parents_ref, q_ref, piece, state):
    scale = exponent_scale(q_ref.shape[1])
    me = lax.axis_index("ctx")

    def visit(step, wanted):
        block = me - step
        hit = (block >= 0) & (block == wanted)
        block = jnp.maximum(block, 0)

        @pl.when(hit)
        def _():
            start = pl.multiple_of(block * 2 * BLOCK, 2 * BLOCK)
            absorb(scale, q_ref, piece[pl.ds(start, BLOCK), :], piece[pl.ds(start + BLOCK, BLOCK), :], *state)

        return jnp.where(hit, parents_ref[block], wanted)

    lax.fori_loop(1, parents_ref.shape[0], visit, parents_ref[me])


def own_block_kernel(xors, reached_ref, q_ref, kv_ref, *refs):
    state = refs[len(xors):]
    m_ref, l_ref, acc_ref = state
    scale = exponent_scale(q_ref.shape[1])
    s = scores_of(kv_ref[0:BLOCK, :], q_ref[...])
    key_at = lax.broadcasted_iota(jnp.int32, s.shape, 0)
    query_at = lax.broadcasted_iota(jnp.int32, s.shape, 1) & (BLOCK - 1)
    s = jnp.where(key_at <= query_at, s, -1e30)
    m = jnp.max(s, axis=0, keepdims=True)
    p = jnp.exp2((s - m) * scale)
    m_ref[...] = m
    l_ref[...] = jnp.sum(p, axis=0, keepdims=True)
    acc_ref[...] = weighted(kv_ref[BLOCK:, :], p)
    absorb_reached(xors, reached_ref, q_ref, refs[:len(xors)], state)


def others_kernel(xors, reached_ref, q_ref, m_in, l_in, acc_in, *refs):
    state = refs[len(xors):]
    absorb_reached(xors, reached_ref, q_ref, refs[:len(xors)], state)


def last_kernel(xors, tree_ref, q_ref, m_in, l_in, acc_in, *refs):
    kv_refs = refs[:max(len(xors), 1)]
    w_ref, att_ref, send_ref, keep_ref, *state = refs[len(kv_refs):]
    rows, head_dim = q_ref.shape
    if xors:
        absorb_reached(xors, tree_ref, q_ref, kv_refs, state)
    else:
        absorb_walk(tree_ref, q_ref, kv_refs[0], state)
    m_ref, l_ref, acc_ref = state

    for head in range(rows // BLOCK):
        at = slice(head * BLOCK, (head + 1) * BLOCK)
        part = (acc_ref[:, at] / l_ref[:, at]).astype(jnp.bfloat16)
        att_ref[:, head * head_dim:(head + 1) * head_dim] = part.T

    project_pair(2, 0, att_ref, w_ref, send_ref, keep_ref)


def project_pair(flip, half, att_ref, w_ref, send_ref, keep_ref):
    target = lax.axis_index("tp") ^ flip
    width = w_ref.shape[1] // 4
    cols = keep_ref.shape[1]
    att = att_ref[...]
    send_ref[...] = project(att, w_ref, (target ^ 1) * width + half * cols, cols).astype(jnp.bfloat16)
    keep_ref[...] = project(att, w_ref, target * width + half * cols, cols)


def shards(ctx_size, tp_size, query_heads, key_heads, value_heads, parents, out_weight):
    tok_rows, local_heads, head_dim = query_heads.shape
    assert tok_rows == BLOCK and key_heads.shape[1] == 1 and parents.shape[0] == ctx_size and tp_size == 4
    width = out_weight.shape[1] // tp_size
    rows = local_heads * tok_rows
    params = pltpu.CompilerParams(vmem_limit_bytes=VMEM_LIMIT)
    vmem = pl.BlockSpec(memory_space=pltpu.VMEM)
    hbm = pl.BlockSpec(memory_space=pltpu.HBM)
    smem = pl.BlockSpec(memory_space=pltpu.SMEM)

    def in_hbm(x):
        return pltpu.with_memory_space_constraint(x, pltpu.HBM)

    def swap(x, axis, size, other):
        return lax.ppermute(x, axis, [(i, i ^ other) for i in range(size)])

    def forward(x, other):
        route = []
        for i in range(ctx_size):
            for j in range(tp_size):
                target = (i ^ 1, j) if i ^ other < i else (i, j ^ 1)
                route.append((i * tp_size + j, target[0] * tp_size + target[1]))
        return lax.ppermute(x, ("ctx", "tp"), route)

    kv, reached = pl.pallas_call(
        functools.partial(pack_kernel, ctx_size == DIRECT_SIZE),
        out_shape=(
            jax.ShapeDtypeStruct((2 * tok_rows, head_dim), jnp.bfloat16),
            jax.ShapeDtypeStruct((8, 128), jnp.int32),
        ),
        in_specs=[hbm, hbm, hbm],
        out_specs=(vmem, vmem),
        scratch_shapes=[pltpu.SMEM(parents.shape, jnp.int32), pltpu.SemaphoreType.DMA((3,))],
        compiler_params=params,
        cost_estimate=pl.CostEstimate(flops=8_000_000_000, bytes_accessed=130_000, transcendentals=0),
    )(in_hbm(key_heads[:, 0, :]), in_hbm(value_heads[:, 0, :]), in_hbm(parents))
    early, early_xors = [], ()
    if ctx_size == DIRECT_SIZE:
        columns = [swap(kv, "ctx", ctx_size, other) for other in (4, 2, 6)]
        beside = swap(kv, "ctx", ctx_size, 1)
    q = jnp.transpose(query_heads, (1, 0, 2)).reshape(rows, head_dim)

    m, l, acc = pl.pallas_call(
        functools.partial(own_block_kernel, early_xors),
        out_shape=(
            jax.ShapeDtypeStruct((1, rows), jnp.float32),
            jax.ShapeDtypeStruct((1, rows), jnp.float32),
            jax.ShapeDtypeStruct((head_dim, rows), jnp.float32),
        ),
        in_specs=[vmem] * (3 + len(early)),
        out_specs=(vmem,) * 3,
        compiler_params=params,
        cost_estimate=pl.CostEstimate(flops=130_000_000, bytes_accessed=1_000_000, transcendentals=260_000),
    )(reached, q, kv, *early)

    if ctx_size == DIRECT_SIZE:
        columns[2], m = lax.optimization_barrier((columns[2], m))
        pairs = [forward(x, other) for x, other in zip(columns, (4, 2, 6))]
    state = (m, l, acc)
    state_shapes = tuple(jax.ShapeDtypeStruct(x.shape, x.dtype) for x in state)
    if ctx_size == DIRECT_SIZE:
        def absorbed(state, xors, arrived):
            return pl.pallas_call(
                functools.partial(others_kernel, xors),
                out_shape=state_shapes,
                in_specs=[vmem] * (5 + len(xors)),
                out_specs=(vmem,) * 3,
                input_output_aliases={2: 0, 3: 1, 4: 2},
                compiler_params=params,
                cost_estimate=pl.CostEstimate(flops=270_000_000, bytes_accessed=1_000_000, transcendentals=500_000),
            )(reached, q, *state, *arrived)

        state = absorbed(state, (1, 4, 2, 6), [beside, *columns])
        state = absorbed(state, (3, 7), pairs[1:])
        xors, pieces, tree, tree_spec = (5,), pairs[:1], reached, vmem
    else:
        xors, pieces, tree, tree_spec = (), [lax.all_gather(kv, "ctx", axis=0, tiled=True)], parents, smem

    half = width // 2
    pair_shapes = (
        jax.ShapeDtypeStruct((tok_rows, half), jnp.bfloat16),
        jax.ShapeDtypeStruct((tok_rows, half), jnp.float32),
    )
    att, send_a, keep_a, *_ = pl.pallas_call(
        functools.partial(last_kernel, xors),
        out_shape=(jax.ShapeDtypeStruct((tok_rows, local_heads * head_dim), jnp.bfloat16),) + pair_shapes + state_shapes,
        in_specs=[tree_spec] + [vmem] * (5 + len(pieces)),
        out_specs=(vmem,) * 6,
        input_output_aliases={2: 3, 3: 4, 4: 5},
        compiler_params=params,
        cost_estimate=pl.CostEstimate(flops=1_000_000_000, bytes_accessed=10_000_000, transcendentals=1_000_000),
    )(tree, q, *state, *pieces, out_weight)

    def projected(flip, part, shapes, att):
        return pl.pallas_call(
            functools.partial(project_pair, flip, part),
            out_shape=shapes,
            in_specs=[vmem, vmem],
            out_specs=(vmem, vmem),
            compiler_params=params,
            cost_estimate=pl.CostEstimate(flops=540_000_000, bytes_accessed=4_000_000, transcendentals=0),
        )(att, out_weight)

    def added(keep, arrived):
        return (keep + arrived.astype(jnp.float32)).astype(jnp.bfloat16)

    in_a = swap(send_a, "tp", tp_size, 1)
    send_b, keep_b = projected(2, 1, pair_shapes, att)
    in_b = swap(send_b, "tp", tp_size, 1)
    far_a = added(keep_a, in_a)
    from_a = swap(far_a, "tp", tp_size, 2)
    far_b = added(keep_b, in_b)
    from_b = swap(far_b, "tp", tp_size, 2)
    att, _ = lax.optimization_barrier((att, far_a))
    send_near, keep_near = projected(
        0,
        0,
        (jax.ShapeDtypeStruct((tok_rows, width), jnp.bfloat16), jax.ShapeDtypeStruct((tok_rows, width), jnp.float32)),
        att,
    )
    near_in = swap(send_near, "tp", tp_size, 1)
    from_far = jnp.concatenate([from_a, from_b], axis=1).astype(jnp.float32)
    return (keep_near + near_in.astype(jnp.float32) + from_far).astype(jnp.bfloat16)


def solution(mesh):
    return jax.shard_map(
        functools.partial(shards, mesh.shape["ctx"], mesh.shape["tp"]),
        mesh=mesh,
        in_specs=(
            P("ctx", "tp", None),
            P("ctx", "tp", None),
            P("ctx", "tp", None),
            P(),
            P("tp", None),
        ),
        out_specs=P("ctx", "tp"),
        check_vma=False,
    )
```

```python
import functools
import math

import jax
import jax.numpy as jnp
from jax import lax
from jax.experimental import pallas as pl
from jax.experimental.pallas import tpu as pltpu
from jax.sharding import PartitionSpec as P

BLOCK = 128
DIRECT_SIZE = 8
VMEM_LIMIT = 32 * 1024 * 1024


def scores_of(k, q):
    return lax.dot_general(k, q, (((1,), (1,)), ((), ())), preferred_element_type=jnp.float32)


def weighted(v, p):
    return lax.dot_general(v, p.astype(jnp.bfloat16), (((0,), (0,)), ((), ())), preferred_element_type=jnp.float32)


def exponent_scale(head_dim):
    return math.log2(math.e) / math.sqrt(head_dim)


def reached_mask(parents_ref):
    me = lax.axis_index("ctx")
    wanted = parents_ref[me]
    reached = jnp.int32(0)
    for step in range(1, DIRECT_SIZE):
        block = me - step
        hit = (block >= 0) & (block == wanted)
        block = jnp.maximum(block, 0)
        reached = jnp.where(hit, reached | lax.shift_left(jnp.int32(1), block), reached)
        wanted = jnp.where(hit, parents_ref[block], wanted)
    return reached


def pack_kernel(walk, k_hbm, v_hbm, parents_hbm, kv_ref, reached_ref, parents_ref, sems):
    copies = [
        pltpu.make_async_copy(parents_hbm, parents_ref, sems.at[0]),
        pltpu.make_async_copy(k_hbm, kv_ref.at[0:BLOCK, :], sems.at[1]),
        pltpu.make_async_copy(v_hbm, kv_ref.at[BLOCK:2 * BLOCK, :], sems.at[2]),
    ]
    for copy in copies:
        copy.start()
    copies[0].wait()
    reached = reached_mask(parents_ref) if walk else jnp.int32(0)
    reached_ref[...] = jnp.full(reached_ref.shape, reached, jnp.int32)
    copies[1].wait()
    copies[2].wait()


def project(att, w_ref, start, width):
    start = pl.multiple_of(start, 128)
    return jnp.dot(att, w_ref[:, pl.ds(start, width)], preferred_element_type=jnp.float32)


def absorb(scale, q_ref, k, v, m_ref, l_ref, acc_ref):
    s = scores_of(k, q_ref[...])
    m_old = m_ref[...]
    m_new = jnp.maximum(m_old, jnp.max(s, axis=0, keepdims=True))
    p = jnp.exp2((s - m_new) * scale)
    factor = jnp.exp2((m_old - m_new) * scale)
    m_ref[...] = m_new
    l_ref[...] = l_ref[...] * factor + jnp.sum(p, axis=0, keepdims=True)
    acc_ref[...] = acc_ref[...] * factor + weighted(v, p)


def absorb_reached(xors, reached_ref, q_ref, kv_refs, state):
    scale = exponent_scale(q_ref.shape[1])
    me = lax.axis_index("ctx")
    reached = jnp.max(reached_ref[...])
    for others, kv_ref in zip(xors, kv_refs):
        for at, other in enumerate(others):
            keys = slice(2 * at * BLOCK, (2 * at + 1) * BLOCK)
            values = slice((2 * at + 1) * BLOCK, (2 * at + 2) * BLOCK)

            @pl.when((lax.shift_right_logical(reached, me ^ other) & 1) == 1)
            def _():
                absorb(scale, q_ref, kv_ref[keys, :], kv_ref[values, :], *state)


def absorb_walk(parents_ref, q_ref, piece, state):
    scale = exponent_scale(q_ref.shape[1])
    me = lax.axis_index("ctx")

    def visit(step, wanted):
        block = me - step
        hit = (block >= 0) & (block == wanted)
        block = jnp.maximum(block, 0)

        @pl.when(hit)
        def _():
            start = pl.multiple_of(block * 2 * BLOCK, 2 * BLOCK)
            absorb(scale, q_ref, piece[pl.ds(start, BLOCK), :], piece[pl.ds(start + BLOCK, BLOCK), :], *state)

        return jnp.where(hit, parents_ref[block], wanted)

    lax.fori_loop(1, parents_ref.shape[0], visit, parents_ref[me])


def own_block_kernel(xors, reached_ref, q_ref, kv_ref, *refs):
    state = refs[len(xors):]
    m_ref, l_ref, acc_ref = state
    scale = exponent_scale(q_ref.shape[1])
    s = scores_of(kv_ref[0:BLOCK, :], q_ref[...])
    key_at = lax.broadcasted_iota(jnp.int32, s.shape, 0)
    query_at = lax.broadcasted_iota(jnp.int32, s.shape, 1) & (BLOCK - 1)
    s = jnp.where(key_at <= query_at, s, -1e30)
    m = jnp.max(s, axis=0, keepdims=True)
    p = jnp.exp2((s - m) * scale)
    m_ref[...] = m
    l_ref[...] = jnp.sum(p, axis=0, keepdims=True)
    acc_ref[...] = weighted(kv_ref[BLOCK:, :], p)
    absorb_reached(xors, reached_ref, q_ref, refs[:len(xors)], state)


def others_kernel(xors, reached_ref, q_ref, m_in, l_in, acc_in, *refs):
    state = refs[len(xors):]
    absorb_reached(xors, reached_ref, q_ref, refs[:len(xors)], state)


def last_kernel(xors, tree_ref, q_ref, m_in, l_in, acc_in, *refs):
    kv_refs = refs[:max(len(xors), 1)]
    w_ref, att_ref, send_ref, keep_ref, *state = refs[len(kv_refs):]
    rows, head_dim = q_ref.shape
    if xors:
        absorb_reached(xors, tree_ref, q_ref, kv_refs, state)
    else:
        absorb_walk(tree_ref, q_ref, kv_refs[0], state)
    m_ref, l_ref, acc_ref = state

    for head in range(rows // BLOCK):
        at = slice(head * BLOCK, (head + 1) * BLOCK)
        part = acc_ref[:, at] / l_ref[:, at]
        att_ref[:, head * head_dim:(head + 1) * head_dim] = part.T.astype(jnp.bfloat16)

    project_pair(2, 0, att_ref, w_ref, send_ref, keep_ref)


def project_pair(flip, half, att_ref, w_ref, send_ref, keep_ref):
    target = lax.axis_index("tp") ^ flip
    width = w_ref.shape[1] // 4
    cols = keep_ref.shape[1]
    att = att_ref[...]
    send_ref[...] = project(att, w_ref, (target ^ 1) * width + half * cols, cols).astype(jnp.bfloat16)
    keep_ref[...] = project(att, w_ref, target * width + half * cols, cols)


def shards(ctx_size, tp_size, query_heads, key_heads, value_heads, parents, out_weight):
    tok_rows, local_heads, head_dim = query_heads.shape
    assert tok_rows == BLOCK and key_heads.shape[1] == 1 and parents.shape[0] == ctx_size and tp_size == 4
    width = out_weight.shape[1] // tp_size
    rows = local_heads * tok_rows
    params = pltpu.CompilerParams(vmem_limit_bytes=VMEM_LIMIT)
    vmem = pl.BlockSpec(memory_space=pltpu.VMEM)
    hbm = pl.BlockSpec(memory_space=pltpu.HBM)
    smem = pl.BlockSpec(memory_space=pltpu.SMEM)

    def in_hbm(x):
        return pltpu.with_memory_space_constraint(x, pltpu.HBM)

    def swap(x, axis, size, other):
        return lax.ppermute(x, axis, [(i, i ^ other) for i in range(size)])

    def forward(x, other):
        route = []
        for i in range(ctx_size):
            for j in range(tp_size):
                target = (i ^ 1, j) if i ^ other < i else (i, j ^ 1)
                route.append((i * tp_size + j, target[0] * tp_size + target[1]))
        return lax.ppermute(x, ("ctx", "tp"), route)

    kv, reached = pl.pallas_call(
        functools.partial(pack_kernel, ctx_size == DIRECT_SIZE),
        out_shape=(
            jax.ShapeDtypeStruct((2 * tok_rows, head_dim), jnp.bfloat16),
            jax.ShapeDtypeStruct((8, 128), jnp.int32),
        ),
        in_specs=[hbm, hbm, hbm],
        out_specs=(vmem, vmem),
        scratch_shapes=[pltpu.SMEM(parents.shape, jnp.int32), pltpu.SemaphoreType.DMA((3,))],
        compiler_params=params,
        cost_estimate=pl.CostEstimate(flops=8_000_000_000, bytes_accessed=130_000, transcendentals=0),
    )(in_hbm(key_heads[:, 0, :]), in_hbm(value_heads[:, 0, :]), in_hbm(parents))
    if ctx_size == DIRECT_SIZE:
        by_6 = swap(kv, "ctx", ctx_size, 6)
        by_1 = swap(kv, "ctx", ctx_size, 1)
        by_4 = swap(kv, "ctx", ctx_size, 4)
        pair = jnp.concatenate([kv, by_1], axis=0)
        by_23 = swap(pair, "ctx", ctx_size, 2)
        held, _ = lax.optimization_barrier((by_6, pair))
        by_7 = forward(held, 6)
        by_5 = forward(by_4, 4)
        early, early_xors = [by_1, by_6, by_4], ((1,), (6,), (4,))
    else:
        early, early_xors = [], ()
    q = jnp.transpose(query_heads, (1, 0, 2)).reshape(rows, head_dim)

    m, l, acc = pl.pallas_call(
        functools.partial(own_block_kernel, early_xors),
        out_shape=(
            jax.ShapeDtypeStruct((1, rows), jnp.float32),
            jax.ShapeDtypeStruct((1, rows), jnp.float32),
            jax.ShapeDtypeStruct((head_dim, rows), jnp.float32),
        ),
        in_specs=[vmem] * (3 + len(early)),
        out_specs=(vmem,) * 3,
        compiler_params=params,
        cost_estimate=pl.CostEstimate(flops=130_000_000, bytes_accessed=1_000_000, transcendentals=260_000),
    )(reached, q, kv, *early)

    state = (m, l, acc)
    state_shapes = tuple(jax.ShapeDtypeStruct(x.shape, x.dtype) for x in state)
    if ctx_size == DIRECT_SIZE:
        def absorbed(state, xors, flops, *arrived):
            return pl.pallas_call(
                functools.partial(others_kernel, xors),
                out_shape=state_shapes,
                in_specs=[vmem] * (5 + len(xors)),
                out_specs=(vmem,) * 3,
                input_output_aliases={2: 0, 3: 1, 4: 2},
                compiler_params=params,
                cost_estimate=pl.CostEstimate(flops=flops, bytes_accessed=1_000_000, transcendentals=500_000),
            )(reached, q, *state, *arrived)

        state = absorbed(state, ((7,),), 270_000_000, by_7)
        xors, pieces, tree, tree_spec = ((2, 3), (5,)), [by_23, by_5], reached, vmem
    else:
        xors, pieces, tree, tree_spec = (), [lax.all_gather(kv, "ctx", axis=0, tiled=True)], parents, smem

    half = width // 2
    pair_shapes = (
        jax.ShapeDtypeStruct((tok_rows, half), jnp.bfloat16),
        jax.ShapeDtypeStruct((tok_rows, half), jnp.float32),
    )
    att, send_a, keep_a, *_ = pl.pallas_call(
        functools.partial(last_kernel, xors),
        out_shape=(jax.ShapeDtypeStruct((tok_rows, local_heads * head_dim), jnp.bfloat16),) + pair_shapes + state_shapes,
        in_specs=[tree_spec] + [vmem] * (5 + len(pieces)),
        out_specs=(vmem,) * 6,
        input_output_aliases={2: 3, 3: 4, 4: 5},
        compiler_params=params,
        cost_estimate=pl.CostEstimate(flops=1_000_000_000, bytes_accessed=10_000_000, transcendentals=1_000_000),
    )(tree, q, *state, *pieces, out_weight)

    def projected(flip, part, shapes, att):
        return pl.pallas_call(
            functools.partial(project_pair, flip, part),
            out_shape=shapes,
            in_specs=[vmem, vmem],
            out_specs=(vmem, vmem),
            compiler_params=params,
            cost_estimate=pl.CostEstimate(flops=540_000_000, bytes_accessed=4_000_000, transcendentals=0),
        )(att, out_weight)

    def added(keep, arrived):
        return (keep + arrived.astype(jnp.float32)).astype(jnp.bfloat16)

    in_a = swap(send_a, "tp", tp_size, 1)
    send_b, keep_b = projected(2, 1, pair_shapes, att)
    in_b = swap(send_b, "tp", tp_size, 1)
    far_a = added(keep_a, in_a)
    from_a = swap(far_a, "tp", tp_size, 2)
    far_b = added(keep_b, in_b)
    from_b = swap(far_b, "tp", tp_size, 2)
    att, _ = lax.optimization_barrier((att, far_a))
    send_near, keep_near = projected(
        0,
        0,
        (jax.ShapeDtypeStruct((tok_rows, width), jnp.bfloat16), jax.ShapeDtypeStruct((tok_rows, width), jnp.float32)),
        att,
    )
    near_in = swap(send_near, "tp", tp_size, 1)
    from_far = jnp.concatenate([from_a, from_b], axis=1).astype(jnp.float32)
    return (keep_near + near_in.astype(jnp.float32) + from_far).astype(jnp.bfloat16)


def solution(mesh):
    return jax.shard_map(
        functools.partial(shards, mesh.shape["ctx"], mesh.shape["tp"]),
        mesh=mesh,
        in_specs=(
            P("ctx", "tp", None),
            P("ctx", "tp", None),
            P("ctx", "tp", None),
            P(),
            P("tp", None),
        ),
        out_specs=P("ctx", "tp"),
        check_vma=False,
    )
```

```python
import functools
import math

import jax
import jax.numpy as jnp
from jax import lax
from jax.experimental import pallas as pl
from jax.experimental.pallas import tpu as pltpu
from jax.sharding import PartitionSpec as P

BLOCK = 128
DIRECT_SIZE = 8
VMEM_LIMIT = 32 * 1024 * 1024


def scores_of(k, q):
    return lax.dot_general(k, q, (((1,), (1,)), ((), ())), preferred_element_type=jnp.float32)


def weighted(v, p):
    return lax.dot_general(v, p.astype(jnp.bfloat16), (((0,), (0,)), ((), ())), preferred_element_type=jnp.float32)


def exponent_scale(head_dim):
    return math.log2(math.e) / math.sqrt(head_dim)


def reached_mask(parents_ref):
    me = lax.axis_index("ctx")
    wanted = parents_ref[me]
    reached = jnp.int32(0)
    for step in range(1, DIRECT_SIZE):
        block = me - step
        hit = (block >= 0) & (block == wanted)
        block = jnp.maximum(block, 0)
        reached = jnp.where(hit, reached | lax.shift_left(jnp.int32(1), block), reached)
        wanted = jnp.where(hit, parents_ref[block], wanted)
    return reached


def pack_kernel(walk, k_hbm, v_hbm, parents_hbm, kv_ref, reached_ref, parents_ref, sems):
    copies = [
        pltpu.make_async_copy(parents_hbm, parents_ref, sems.at[0]),
        pltpu.make_async_copy(k_hbm, kv_ref.at[0:BLOCK, :], sems.at[1]),
        pltpu.make_async_copy(v_hbm, kv_ref.at[BLOCK:2 * BLOCK, :], sems.at[2]),
    ]
    for copy in copies:
        copy.start()
    copies[0].wait()
    reached = reached_mask(parents_ref) if walk else jnp.int32(0)
    reached_ref[...] = jnp.full(reached_ref.shape, reached, jnp.int32)
    copies[1].wait()
    copies[2].wait()


def project(att, w_ref, start, width):
    start = pl.multiple_of(start, 128)
    return jnp.dot(att, w_ref[:, pl.ds(start, width)], preferred_element_type=jnp.float32)


def absorb(scale, q_ref, k, v, m_ref, l_ref, acc_ref):
    s = scores_of(k, q_ref[...])
    m_old = m_ref[...]
    m_new = jnp.maximum(m_old, jnp.max(s, axis=0, keepdims=True))
    p = jnp.exp2((s - m_new) * scale)
    factor = jnp.exp2((m_old - m_new) * scale)
    m_ref[...] = m_new
    l_ref[...] = l_ref[...] * factor + jnp.sum(p, axis=0, keepdims=True)
    acc_ref[...] = acc_ref[...] * factor + weighted(v, p)


def absorb_reached(xors, reached_ref, q_ref, kv_refs, state):
    scale = exponent_scale(q_ref.shape[1])
    me = lax.axis_index("ctx")
    reached = jnp.max(reached_ref[...])
    for other, kv_ref in zip(xors, kv_refs):
        @pl.when((lax.shift_right_logical(reached, me ^ other) & 1) == 1)
        def _():
            absorb(scale, q_ref, kv_ref[0:BLOCK, :], kv_ref[BLOCK:, :], *state)


def absorb_walk(parents_ref, q_ref, piece, state):
    scale = exponent_scale(q_ref.shape[1])
    me = lax.axis_index("ctx")

    def visit(step, wanted):
        block = me - step
        hit = (block >= 0) & (block == wanted)
        block = jnp.maximum(block, 0)

        @pl.when(hit)
        def _():
            start = pl.multiple_of(block * 2 * BLOCK, 2 * BLOCK)
            absorb(scale, q_ref, piece[pl.ds(start, BLOCK), :], piece[pl.ds(start + BLOCK, BLOCK), :], *state)

        return jnp.where(hit, parents_ref[block], wanted)

    lax.fori_loop(1, parents_ref.shape[0], visit, parents_ref[me])


def own_block_kernel(xors, reached_ref, q_ref, kv_ref, *refs):
    state = refs[len(xors):]
    m_ref, l_ref, acc_ref = state
    scale = exponent_scale(q_ref.shape[1])
    s = scores_of(kv_ref[0:BLOCK, :], q_ref[...])
    key_at = lax.broadcasted_iota(jnp.int32, s.shape, 0)
    query_at = lax.broadcasted_iota(jnp.int32, s.shape, 1) & (BLOCK - 1)
    s = jnp.where(key_at <= query_at, s, -1e30)
    m = jnp.max(s, axis=0, keepdims=True)
    p = jnp.exp2((s - m) * scale)
    m_ref[...] = m
    l_ref[...] = jnp.sum(p, axis=0, keepdims=True)
    acc_ref[...] = weighted(kv_ref[BLOCK:, :], p)
    absorb_reached(xors, reached_ref, q_ref, refs[:len(xors)], state)


def others_kernel(xors, reached_ref, q_ref, m_in, l_in, acc_in, *refs):
    state = refs[len(xors):]
    absorb_reached(xors, reached_ref, q_ref, refs[:len(xors)], state)


def last_kernel(xors, tree_ref, q_ref, m_in, l_in, acc_in, *refs):
    kv_refs = refs[:max(len(xors), 1)]
    w_ref, att_ref, send_ref, keep_ref, *state = refs[len(kv_refs):]
    rows, head_dim = q_ref.shape
    if xors:
        absorb_reached(xors, tree_ref, q_ref, kv_refs, state)
    else:
        absorb_walk(tree_ref, q_ref, kv_refs[0], state)
    m_ref, l_ref, acc_ref = state

    for head in range(rows // BLOCK):
        at = slice(head * BLOCK, (head + 1) * BLOCK)
        part = acc_ref[:, at] / l_ref[:, at]
        att_ref[:, head * head_dim:(head + 1) * head_dim] = part.T.astype(jnp.bfloat16)

    project_pair(2, 0, att_ref, w_ref, send_ref, keep_ref)


def project_pair(flip, half, att_ref, w_ref, send_ref, keep_ref):
    target = lax.axis_index("tp") ^ flip
    width = w_ref.shape[1] // 4
    cols = keep_ref.shape[1]
    att = att_ref[...]
    send_ref[...] = project(att, w_ref, (target ^ 1) * width + half * cols, cols).astype(jnp.bfloat16)
    keep_ref[...] = project(att, w_ref, target * width + half * cols, cols)


def shards(ctx_size, tp_size, query_heads, key_heads, value_heads, parents, out_weight):
    tok_rows, local_heads, head_dim = query_heads.shape
    assert tok_rows == BLOCK and key_heads.shape[1] == 1 and parents.shape[0] == ctx_size and tp_size == 4
    width = out_weight.shape[1] // tp_size
    rows = local_heads * tok_rows
    params = pltpu.CompilerParams(vmem_limit_bytes=VMEM_LIMIT)
    vmem = pl.BlockSpec(memory_space=pltpu.VMEM)
    hbm = pl.BlockSpec(memory_space=pltpu.HBM)
    smem = pl.BlockSpec(memory_space=pltpu.SMEM)

    def in_hbm(x):
        return pltpu.with_memory_space_constraint(x, pltpu.HBM)

    def swap(x, axis, size, other):
        return lax.ppermute(x, axis, [(i, i ^ other) for i in range(size)])

    def forward(x, other):
        route = []
        for i in range(ctx_size):
            for j in range(tp_size):
                target = (i ^ 1, j) if i ^ other < i else (i, j ^ 1)
                route.append((i * tp_size + j, target[0] * tp_size + target[1]))
        return lax.ppermute(x, ("ctx", "tp"), route)

    kv, reached = pl.pallas_call(
        functools.partial(pack_kernel, ctx_size == DIRECT_SIZE),
        out_shape=(
            jax.ShapeDtypeStruct((2 * tok_rows, head_dim), jnp.bfloat16),
            jax.ShapeDtypeStruct((8, 128), jnp.int32),
        ),
        in_specs=[hbm, hbm, hbm],
        out_specs=(vmem, vmem),
        scratch_shapes=[pltpu.SMEM(parents.shape, jnp.int32), pltpu.SemaphoreType.DMA((3,))],
        compiler_params=params,
        cost_estimate=pl.CostEstimate(flops=1_000_000, bytes_accessed=130_000, transcendentals=0),
    )(in_hbm(key_heads[:, 0, :]), in_hbm(value_heads[:, 0, :]), in_hbm(parents))
    if ctx_size == DIRECT_SIZE:
        columns = [swap(kv, "ctx", ctx_size, other) for other in (4, 2, 6)]
        beside = swap(kv, "ctx", ctx_size, 1)
        pairs = [forward(x, other) for x, other in zip(columns, (4, 2, 6))]
        early, early_xors = [beside, *columns], (1, 4, 2, 6)
    else:
        early, early_xors = [], ()
    q = jnp.transpose(query_heads, (1, 0, 2)).reshape(rows, head_dim)

    m, l, acc = pl.pallas_call(
        functools.partial(own_block_kernel, early_xors),
        out_shape=(
            jax.ShapeDtypeStruct((1, rows), jnp.float32),
            jax.ShapeDtypeStruct((1, rows), jnp.float32),
            jax.ShapeDtypeStruct((head_dim, rows), jnp.float32),
        ),
        in_specs=[vmem] * (3 + len(early)),
        out_specs=(vmem,) * 3,
        compiler_params=params,
        cost_estimate=pl.CostEstimate(flops=5000000000, bytes_accessed=1_000_000, transcendentals=260_000),
    )(reached, q, kv, *early)

    state = (m, l, acc)
    state_shapes = tuple(jax.ShapeDtypeStruct(x.shape, x.dtype) for x in state)
    if ctx_size == DIRECT_SIZE:
        def absorbed(state, xors, arrived):
            return pl.pallas_call(
                functools.partial(others_kernel, xors),
                out_shape=state_shapes,
                in_specs=[vmem] * (5 + len(xors)),
                out_specs=(vmem,) * 3,
                input_output_aliases={2: 0, 3: 1, 4: 2},
                compiler_params=params,
                cost_estimate=pl.CostEstimate(flops=270_000_000, bytes_accessed=1_000_000, transcendentals=500_000),
            )(reached, q, *state, *arrived)

        state = absorbed(state, (3, 7), pairs[1:])
        xors, pieces, tree, tree_spec = (5,), pairs[:1], reached, vmem
    else:
        xors, pieces, tree, tree_spec = (), [lax.all_gather(kv, "ctx", axis=0, tiled=True)], parents, smem

    half = width // 2
    pair_shapes = (
        jax.ShapeDtypeStruct((tok_rows, half), jnp.bfloat16),
        jax.ShapeDtypeStruct((tok_rows, half), jnp.float32),
    )
    att, send_a, keep_a, *_ = pl.pallas_call(
        functools.partial(last_kernel, xors),
        out_shape=(jax.ShapeDtypeStruct((tok_rows, local_heads * head_dim), jnp.bfloat16),) + pair_shapes + state_shapes,
        in_specs=[tree_spec] + [vmem] * (5 + len(pieces)),
        out_specs=(vmem,) * 6,
        input_output_aliases={2: 3, 3: 4, 4: 5},
        compiler_params=params,
        cost_estimate=pl.CostEstimate(flops=1_000_000_000, bytes_accessed=10_000_000, transcendentals=1_000_000),
    )(tree, q, *state, *pieces, out_weight)

    def projected(flip, part, shapes, att):
        return pl.pallas_call(
            functools.partial(project_pair, flip, part),
            out_shape=shapes,
            in_specs=[vmem, vmem],
            out_specs=(vmem, vmem),
            compiler_params=params,
            cost_estimate=pl.CostEstimate(flops=540_000_000, bytes_accessed=4_000_000, transcendentals=0),
        )(att, out_weight)

    def added(keep, arrived):
        return (keep + arrived.astype(jnp.float32)).astype(jnp.bfloat16)

    in_a = swap(send_a, "tp", tp_size, 1)
    send_b, keep_b = projected(2, 1, pair_shapes, att)
    in_b = swap(send_b, "tp", tp_size, 1)
    far_a = added(keep_a, in_a)
    from_a = swap(far_a, "tp", tp_size, 2)
    far_b = added(keep_b, in_b)
    from_b = swap(far_b, "tp", tp_size, 2)
    att, _ = lax.optimization_barrier((att, far_a))
    send_near, keep_near = projected(
        0,
        0,
        (jax.ShapeDtypeStruct((tok_rows, width), jnp.bfloat16), jax.ShapeDtypeStruct((tok_rows, width), jnp.float32)),
        att,
    )
    near_in = swap(send_near, "tp", tp_size, 1)
    from_far = jnp.concatenate([from_a, from_b], axis=1).astype(jnp.float32)
    return (keep_near + near_in.astype(jnp.float32) + from_far).astype(jnp.bfloat16)


def solution(mesh):
    return jax.shard_map(
        functools.partial(shards, mesh.shape["ctx"], mesh.shape["tp"]),
        mesh=mesh,
        in_specs=(
            P("ctx", "tp", None),
            P("ctx", "tp", None),
            P("ctx", "tp", None),
            P(),
            P("tp", None),
        ),
        out_specs=P("ctx", "tp"),
        check_vma=False,
    )
```

```python
import functools
import math

import jax
import jax.numpy as jnp
from jax import lax
from jax.experimental import pallas as pl
from jax.experimental.pallas import tpu as pltpu
from jax.sharding import PartitionSpec as P

BLOCK = 128
DIRECT_SIZE = 8
VMEM_LIMIT = 32 * 1024 * 1024


def scores_of(k, q):
    return lax.dot_general(k, q, (((1,), (1,)), ((), ())), preferred_element_type=jnp.float32)


def weighted(v, p):
    return lax.dot_general(v, p.astype(jnp.bfloat16), (((0,), (0,)), ((), ())), preferred_element_type=jnp.float32)


def exponent_scale(head_dim):
    return math.log2(math.e) / math.sqrt(head_dim)


def reached_mask(parents_ref):
    me = lax.axis_index("ctx")
    wanted = parents_ref[me]
    reached = jnp.int32(0)
    for step in range(1, DIRECT_SIZE):
        block = me - step
        hit = (block >= 0) & (block == wanted)
        block = jnp.maximum(block, 0)
        reached = jnp.where(hit, reached | lax.shift_left(jnp.int32(1), block), reached)
        wanted = jnp.where(hit, parents_ref[block], wanted)
    return reached


def pack_kernel(walk, k_hbm, v_hbm, q_hbm, parents_hbm, kv_ref, q_ref, reached_ref, parents_ref, sems):
    copies = [
        pltpu.make_async_copy(parents_hbm, parents_ref, sems.at[0]),
        pltpu.make_async_copy(k_hbm, kv_ref.at[0:BLOCK, :], sems.at[1]),
        pltpu.make_async_copy(v_hbm, kv_ref.at[BLOCK:2 * BLOCK, :], sems.at[2]),
        pltpu.make_async_copy(q_hbm, q_ref, sems.at[3]),
    ]
    for copy in copies:
        copy.start()
    copies[0].wait()
    reached = reached_mask(parents_ref) if walk else jnp.int32(0)
    reached_ref[...] = jnp.full(reached_ref.shape, reached, jnp.int32)
    for copy in copies[1:]:
        copy.wait()


def project(att, w_ref, start, width):
    start = pl.multiple_of(start, 128)
    return jnp.dot(att, w_ref[:, pl.ds(start, width)], preferred_element_type=jnp.float32)


def absorb(scale, q_ref, k, v, m_ref, l_ref, acc_ref):
    s = scores_of(k, q_ref[...])
    m_old = m_ref[...]
    m_new = jnp.maximum(m_old, jnp.max(s, axis=0, keepdims=True))
    p = jnp.exp2((s - m_new) * scale)
    factor = jnp.exp2((m_old - m_new) * scale)
    m_ref[...] = m_new
    l_ref[...] = l_ref[...] * factor + jnp.sum(p, axis=0, keepdims=True)
    acc_ref[...] = acc_ref[...] * factor + weighted(v, p)


def absorb_reached(xors, reached_ref, q_ref, kv_refs, state):
    scale = exponent_scale(q_ref.shape[1])
    me = lax.axis_index("ctx")
    reached = jnp.max(reached_ref[...])
    for other, kv_ref in zip(xors, kv_refs):
        @pl.when((lax.shift_right_logical(reached, me ^ other) & 1) == 1)
        def _():
            absorb(scale, q_ref, kv_ref[0:BLOCK, :], kv_ref[BLOCK:, :], *state)


def absorb_walk(parents_ref, q_ref, piece, state):
    scale = exponent_scale(q_ref.shape[1])
    me = lax.axis_index("ctx")

    def visit(step, wanted):
        block = me - step
        hit = (block >= 0) & (block == wanted)
        block = jnp.maximum(block, 0)

        @pl.when(hit)
        def _():
            start = pl.multiple_of(block * 2 * BLOCK, 2 * BLOCK)
            absorb(scale, q_ref, piece[pl.ds(start, BLOCK), :], piece[pl.ds(start + BLOCK, BLOCK), :], *state)

        return jnp.where(hit, parents_ref[block], wanted)

    lax.fori_loop(1, parents_ref.shape[0], visit, parents_ref[me])


def own_block_kernel(xors, reached_ref, q_ref, kv_ref, *refs):
    state = refs[len(xors):]
    m_ref, l_ref, acc_ref = state
    scale = exponent_scale(q_ref.shape[1])
    s = scores_of(kv_ref[0:BLOCK, :], q_ref[...])
    key_at = lax.broadcasted_iota(jnp.int32, s.shape, 0)
    query_at = lax.broadcasted_iota(jnp.int32, s.shape, 1) & (BLOCK - 1)
    s = jnp.where(key_at <= query_at, s, -1e30)
    m = jnp.max(s, axis=0, keepdims=True)
    p = jnp.exp2((s - m) * scale)
    m_ref[...] = m
    l_ref[...] = jnp.sum(p, axis=0, keepdims=True)
    acc_ref[...] = weighted(kv_ref[BLOCK:, :], p)
    absorb_reached(xors, reached_ref, q_ref, refs[:len(xors)], state)


def others_kernel(xors, reached_ref, q_ref, m_in, l_in, acc_in, *refs):
    state = refs[len(xors):]
    absorb_reached(xors, reached_ref, q_ref, refs[:len(xors)], state)


def last_kernel(xors, tree_ref, q_ref, m_in, l_in, acc_in, *refs):
    kv_refs = refs[:max(len(xors), 1)]
    w_ref, att_ref, send_ref, keep_ref, *state = refs[len(kv_refs):]
    rows, head_dim = q_ref.shape
    if xors:
        absorb_reached(xors, tree_ref, q_ref, kv_refs, state)
    else:
        absorb_walk(tree_ref, q_ref, kv_refs[0], state)
    m_ref, l_ref, acc_ref = state

    for head in range(rows // BLOCK):
        at = slice(head * BLOCK, (head + 1) * BLOCK)
        part = acc_ref[:, at] / l_ref[:, at]
        att_ref[:, head * head_dim:(head + 1) * head_dim] = part.T.astype(jnp.bfloat16)

    project_pair(2, 0, att_ref, w_ref, send_ref, keep_ref)


def project_pair(flip, half, att_ref, w_ref, send_ref, keep_ref):
    target = lax.axis_index("tp") ^ flip
    width = w_ref.shape[1] // 4
    cols = keep_ref.shape[1]
    att = att_ref[...]
    send_ref[...] = project(att, w_ref, (target ^ 1) * width + half * cols, cols).astype(jnp.bfloat16)
    keep_ref[...] = project(att, w_ref, target * width + half * cols, cols)


def shards(ctx_size, tp_size, query_heads, key_heads, value_heads, parents, out_weight):
    tok_rows, local_heads, head_dim = query_heads.shape
    assert tok_rows == BLOCK and key_heads.shape[1] == 1 and parents.shape[0] == ctx_size and tp_size == 4
    width = out_weight.shape[1] // tp_size
    rows = local_heads * tok_rows
    params = pltpu.CompilerParams(vmem_limit_bytes=VMEM_LIMIT)
    vmem = pl.BlockSpec(memory_space=pltpu.VMEM)
    hbm = pl.BlockSpec(memory_space=pltpu.HBM)
    smem = pl.BlockSpec(memory_space=pltpu.SMEM)

    def in_hbm(x):
        return pltpu.with_memory_space_constraint(x, pltpu.HBM)

    def swap(x, axis, size, other):
        return lax.ppermute(x, axis, [(i, i ^ other) for i in range(size)])

    def forward(x, other):
        route = []
        for i in range(ctx_size):
            for j in range(tp_size):
                target = (i ^ 1, j) if i ^ other < i else (i, j ^ 1)
                route.append((i * tp_size + j, target[0] * tp_size + target[1]))
        return lax.ppermute(x, ("ctx", "tp"), route)

    kv, queries, reached = pl.pallas_call(
        functools.partial(pack_kernel, ctx_size == DIRECT_SIZE),
        out_shape=(
            jax.ShapeDtypeStruct((2 * tok_rows, head_dim), jnp.bfloat16),
            jax.ShapeDtypeStruct(query_heads.shape, jnp.bfloat16),
            jax.ShapeDtypeStruct((8, 128), jnp.int32),
        ),
        in_specs=[hbm] * 4,
        out_specs=(vmem,) * 3,
        scratch_shapes=[pltpu.SMEM(parents.shape, jnp.int32), pltpu.SemaphoreType.DMA((4,))],
        compiler_params=params,
        cost_estimate=pl.CostEstimate(flops=1_000_000, bytes_accessed=130_000, transcendentals=0),
    )(in_hbm(key_heads[:, 0, :]), in_hbm(value_heads[:, 0, :]), in_hbm(query_heads), in_hbm(parents))
    if ctx_size == DIRECT_SIZE:
        columns = [swap(kv, "ctx", ctx_size, other) for other in (4, 2, 6)]
        beside = swap(kv, "ctx", ctx_size, 1)
        pairs = [forward(x, other) for x, other in zip(columns, (4, 2, 6))]
        early, early_xors = [beside, *columns], (1, 4, 2, 6)
    else:
        early, early_xors = [], ()
    q = jnp.transpose(queries, (1, 0, 2)).reshape(rows, head_dim)

    m, l, acc = pl.pallas_call(
        functools.partial(own_block_kernel, early_xors),
        out_shape=(
            jax.ShapeDtypeStruct((1, rows), jnp.float32),
            jax.ShapeDtypeStruct((1, rows), jnp.float32),
            jax.ShapeDtypeStruct((head_dim, rows), jnp.float32),
        ),
        in_specs=[vmem] * (3 + len(early)),
        out_specs=(vmem,) * 3,
        compiler_params=params,
        cost_estimate=pl.CostEstimate(flops=5000000000, bytes_accessed=1_000_000, transcendentals=260_000),
    )(reached, q, kv, *early)

    state = (m, l, acc)
    state_shapes = tuple(jax.ShapeDtypeStruct(x.shape, x.dtype) for x in state)
    if ctx_size == DIRECT_SIZE:
        def absorbed(state, xors, arrived):
            return pl.pallas_call(
                functools.partial(others_kernel, xors),
                out_shape=state_shapes,
                in_specs=[vmem] * (5 + len(xors)),
                out_specs=(vmem,) * 3,
                input_output_aliases={2: 0, 3: 1, 4: 2},
                compiler_params=params,
                cost_estimate=pl.CostEstimate(flops=270_000_000, bytes_accessed=1_000_000, transcendentals=500_000),
            )(reached, q, *state, *arrived)

        state = absorbed(state, (3, 7), pairs[1:])
        xors, pieces, tree, tree_spec = (5,), pairs[:1], reached, vmem
    else:
        xors, pieces, tree, tree_spec = (), [lax.all_gather(kv, "ctx", axis=0, tiled=True)], parents, smem

    half = width // 2
    pair_shapes = (
        jax.ShapeDtypeStruct((tok_rows, half), jnp.bfloat16),
        jax.ShapeDtypeStruct((tok_rows, half), jnp.float32),
    )
    att, send_a, keep_a, *_ = pl.pallas_call(
        functools.partial(last_kernel, xors),
        out_shape=(jax.ShapeDtypeStruct((tok_rows, local_heads * head_dim), jnp.bfloat16),) + pair_shapes + state_shapes,
        in_specs=[tree_spec] + [vmem] * (5 + len(pieces)),
        out_specs=(vmem,) * 6,
        input_output_aliases={2: 3, 3: 4, 4: 5},
        compiler_params=params,
        cost_estimate=pl.CostEstimate(flops=1_000_000_000, bytes_accessed=10_000_000, transcendentals=1_000_000),
    )(tree, q, *state, *pieces, out_weight)

    def projected(flip, part, shapes, att):
        return pl.pallas_call(
            functools.partial(project_pair, flip, part),
            out_shape=shapes,
            in_specs=[vmem, vmem],
            out_specs=(vmem, vmem),
            compiler_params=params,
            cost_estimate=pl.CostEstimate(flops=540_000_000, bytes_accessed=4_000_000, transcendentals=0),
        )(att, out_weight)

    def added(keep, arrived):
        return (keep + arrived.astype(jnp.float32)).astype(jnp.bfloat16)

    in_a = swap(send_a, "tp", tp_size, 1)
    send_b, keep_b = projected(2, 1, pair_shapes, att)
    in_b = swap(send_b, "tp", tp_size, 1)
    far_a = added(keep_a, in_a)
    from_a = swap(far_a, "tp", tp_size, 2)
    far_b = added(keep_b, in_b)
    from_b = swap(far_b, "tp", tp_size, 2)
    att, _ = lax.optimization_barrier((att, far_a))
    send_near, keep_near = projected(
        0,
        0,
        (jax.ShapeDtypeStruct((tok_rows, width), jnp.bfloat16), jax.ShapeDtypeStruct((tok_rows, width), jnp.float32)),
        att,
    )
    near_in = swap(send_near, "tp", tp_size, 1)
    from_far = jnp.concatenate([from_a, from_b], axis=1).astype(jnp.float32)
    return (keep_near + near_in.astype(jnp.float32) + from_far).astype(jnp.bfloat16)


def solution(mesh):
    return jax.shard_map(
        functools.partial(shards, mesh.shape["ctx"], mesh.shape["tp"]),
        mesh=mesh,
        in_specs=(
            P("ctx", "tp", None),
            P("ctx", "tp", None),
            P("ctx", "tp", None),
            P(),
            P("tp", None),
        ),
        out_specs=P("ctx", "tp"),
        check_vma=False,
    )
```

```python
import functools
import math

import jax
import jax.numpy as jnp
from jax import lax
from jax.experimental import pallas as pl
from jax.experimental.pallas import tpu as pltpu
from jax.sharding import PartitionSpec as P

BLOCK = 128
DIRECT_SIZE = 8
VMEM_LIMIT = 32 * 1024 * 1024


def scores_of(k, q):
    return lax.dot_general(k, q, (((1,), (1,)), ((), ())), preferred_element_type=jnp.float32)


def weighted(v, p):
    return lax.dot_general(v, p.astype(jnp.bfloat16), (((0,), (0,)), ((), ())), preferred_element_type=jnp.float32)


def exponent_scale(head_dim):
    return math.log2(math.e) / math.sqrt(head_dim)


def reached_mask(parents_ref):
    me = lax.axis_index("ctx")
    wanted = parents_ref[me]
    reached = jnp.int32(0)
    for step in range(1, DIRECT_SIZE):
        block = me - step
        hit = (block >= 0) & (block == wanted)
        block = jnp.maximum(block, 0)
        reached = jnp.where(hit, reached | lax.shift_left(jnp.int32(1), block), reached)
        wanted = jnp.where(hit, parents_ref[block], wanted)
    return reached


def pack_kernel(walk, k_hbm, v_hbm, parents_hbm, kv_ref, reached_ref, parents_ref, sems):
    copies = [
        pltpu.make_async_copy(parents_hbm, parents_ref, sems.at[0]),
        pltpu.make_async_copy(k_hbm, kv_ref.at[0:BLOCK, :], sems.at[1]),
        pltpu.make_async_copy(v_hbm, kv_ref.at[BLOCK:2 * BLOCK, :], sems.at[2]),
    ]
    for copy in copies:
        copy.start()
    copies[0].wait()
    reached = reached_mask(parents_ref) if walk else jnp.int32(0)
    reached_ref[...] = jnp.full(reached_ref.shape, reached, jnp.int32)
    copies[1].wait()
    copies[2].wait()


def project(att, w_ref, start, width):
    start = pl.multiple_of(start, 128)
    return jnp.dot(att, w_ref[:, pl.ds(start, width)], preferred_element_type=jnp.float32)


def absorb(scale, q_ref, k, v, m_ref, l_ref, acc_ref):
    s = scores_of(k, q_ref[...])
    m_old = m_ref[...]
    m_new = jnp.maximum(m_old, jnp.max(s, axis=0, keepdims=True))
    p = jnp.exp2((s - m_new) * scale)
    factor = jnp.exp2((m_old - m_new) * scale)
    m_ref[...] = m_new
    l_ref[...] = l_ref[...] * factor + jnp.sum(p, axis=0, keepdims=True)
    acc_ref[...] = acc_ref[...] * factor + weighted(v, p)


def absorb_reached(xors, reached_ref, q_ref, kv_refs, state):
    scale = exponent_scale(q_ref.shape[1])
    me = lax.axis_index("ctx")
    reached = jnp.max(reached_ref[...])
    for other, kv_ref in zip(xors, kv_refs):
        @pl.when((lax.shift_right_logical(reached, me ^ other) & 1) == 1)
        def _():
            absorb(scale, q_ref, kv_ref[0:BLOCK, :], kv_ref[BLOCK:, :], *state)


def absorb_walk(parents_ref, q_ref, piece, state):
    scale = exponent_scale(q_ref.shape[1])
    me = lax.axis_index("ctx")

    def visit(step, wanted):
        block = me - step
        hit = (block >= 0) & (block == wanted)
        block = jnp.maximum(block, 0)

        @pl.when(hit)
        def _():
            start = pl.multiple_of(block * 2 * BLOCK, 2 * BLOCK)
            absorb(scale, q_ref, piece[pl.ds(start, BLOCK), :], piece[pl.ds(start + BLOCK, BLOCK), :], *state)

        return jnp.where(hit, parents_ref[block], wanted)

    lax.fori_loop(1, parents_ref.shape[0], visit, parents_ref[me])


def own_block_kernel(xors, reached_ref, q_ref, kv_ref, *refs):
    state = refs[len(xors):]
    m_ref, l_ref, acc_ref = state
    scale = exponent_scale(q_ref.shape[1])
    s = scores_of(kv_ref[0:BLOCK, :], q_ref[...])
    key_at = lax.broadcasted_iota(jnp.int32, s.shape, 0)
    query_at = lax.broadcasted_iota(jnp.int32, s.shape, 1) & (BLOCK - 1)
    s = jnp.where(key_at <= query_at, s, -1e30)
    m = jnp.max(s, axis=0, keepdims=True)
    p = jnp.exp2((s - m) * scale)
    m_ref[...] = m
    l_ref[...] = jnp.sum(p, axis=0, keepdims=True)
    acc_ref[...] = weighted(kv_ref[BLOCK:, :], p)
    absorb_reached(xors, reached_ref, q_ref, refs[:len(xors)], state)


def others_kernel(xors, reached_ref, q_ref, m_in, l_in, acc_in, *refs):
    state = refs[len(xors):]
    absorb_reached(xors, reached_ref, q_ref, refs[:len(xors)], state)


def last_kernel(xors, tree_ref, q_ref, m_in, l_in, acc_in, *refs):
    kv_refs = refs[:max(len(xors), 1)]
    w_ref, att_ref, send_ref, keep_ref, *state = refs[len(kv_refs):]
    rows, head_dim = q_ref.shape
    if xors:
        absorb_reached(xors, tree_ref, q_ref, kv_refs, state)
    else:
        absorb_walk(tree_ref, q_ref, kv_refs[0], state)
    m_ref, l_ref, acc_ref = state

    for head in range(rows // BLOCK):
        at = slice(head * BLOCK, (head + 1) * BLOCK)
        part = acc_ref[:, at] / l_ref[:, at]
        att_ref[:, head * head_dim:(head + 1) * head_dim] = part.T.astype(jnp.bfloat16)

    project_pair(2, 0, att_ref, w_ref, send_ref, keep_ref)


def project_pair(flip, half, att_ref, w_ref, send_ref, keep_ref):
    target = lax.axis_index("tp") ^ flip
    width = w_ref.shape[1] // 4
    cols = keep_ref.shape[1]
    att = att_ref[...]
    send_ref[...] = project(att, w_ref, (target ^ 1) * width + half * cols, cols).astype(jnp.bfloat16)
    keep_ref[...] = project(att, w_ref, target * width + half * cols, cols)


def shards(ctx_size, tp_size, query_heads, key_heads, value_heads, parents, out_weight):
    tok_rows, local_heads, head_dim = query_heads.shape
    assert tok_rows == BLOCK and key_heads.shape[1] == 1 and parents.shape[0] == ctx_size and tp_size == 4
    width = out_weight.shape[1] // tp_size
    rows = local_heads * tok_rows
    params = pltpu.CompilerParams(vmem_limit_bytes=VMEM_LIMIT)
    vmem = pl.BlockSpec(memory_space=pltpu.VMEM)
    hbm = pl.BlockSpec(memory_space=pltpu.HBM)
    smem = pl.BlockSpec(memory_space=pltpu.SMEM)

    def in_hbm(x):
        return pltpu.with_memory_space_constraint(x, pltpu.HBM)

    def swap(x, axis, size, other):
        return lax.ppermute(x, axis, [(i, i ^ other) for i in range(size)])

    def forward(x, other):
        route = []
        for i in range(ctx_size):
            for j in range(tp_size):
                target = (i ^ 1, j) if i ^ other < i else (i, j ^ 1)
                route.append((i * tp_size + j, target[0] * tp_size + target[1]))
        return lax.ppermute(x, ("ctx", "tp"), route)

    kv, reached = pl.pallas_call(
        functools.partial(pack_kernel, ctx_size == DIRECT_SIZE),
        out_shape=(
            jax.ShapeDtypeStruct((2 * tok_rows, head_dim), jnp.bfloat16),
            jax.ShapeDtypeStruct((8, 128), jnp.int32),
        ),
        in_specs=[hbm, hbm, hbm],
        out_specs=(vmem, vmem),
        scratch_shapes=[pltpu.SMEM(parents.shape, jnp.int32), pltpu.SemaphoreType.DMA((3,))],
        compiler_params=params,
        cost_estimate=pl.CostEstimate(flops=1_000_000, bytes_accessed=130_000, transcendentals=0),
    )(in_hbm(key_heads[:, 0, :]), in_hbm(value_heads[:, 0, :]), in_hbm(parents))
    if ctx_size == DIRECT_SIZE:
        columns = [swap(kv, "ctx", ctx_size, other) for other in (4, 2, 6)]
        beside = swap(kv, "ctx", ctx_size, 1)
        pairs = [forward(x, other) for x, other in zip(columns, (4, 2, 6))]
        early, early_xors = [beside, *columns], (1, 4, 2, 6)
    else:
        early, early_xors = [], ()
    q = jnp.transpose(query_heads, (1, 0, 2)).reshape(rows, head_dim)

    m, l, acc = pl.pallas_call(
        functools.partial(own_block_kernel, early_xors),
        out_shape=(
            jax.ShapeDtypeStruct((1, rows), jnp.float32),
            jax.ShapeDtypeStruct((1, rows), jnp.float32),
            jax.ShapeDtypeStruct((head_dim, rows), jnp.float32),
        ),
        in_specs=[vmem] * (3 + len(early)),
        out_specs=(vmem,) * 3,
        compiler_params=params,
        cost_estimate=pl.CostEstimate(flops=5000000000, bytes_accessed=1_000_000, transcendentals=260_000),
    )(reached, q, kv, *early)

    state = (m, l, acc)
    state_shapes = tuple(jax.ShapeDtypeStruct(x.shape, x.dtype) for x in state)
    if ctx_size == DIRECT_SIZE:
        def absorbed(state, xors, arrived):
            return pl.pallas_call(
                functools.partial(others_kernel, xors),
                out_shape=state_shapes,
                in_specs=[vmem] * (5 + len(xors)),
                out_specs=(vmem,) * 3,
                input_output_aliases={2: 0, 3: 1, 4: 2},
                compiler_params=params,
                cost_estimate=pl.CostEstimate(flops=270_000_000, bytes_accessed=1_000_000, transcendentals=500_000),
            )(reached, q, *state, *arrived)

        state = absorbed(state, (3,), pairs[1:2])
        state = absorbed(state, (7,), pairs[2:])
        xors, pieces, tree, tree_spec = (5,), pairs[:1], reached, vmem
    else:
        xors, pieces, tree, tree_spec = (), [lax.all_gather(kv, "ctx", axis=0, tiled=True)], parents, smem

    half = width // 2
    pair_shapes = (
        jax.ShapeDtypeStruct((tok_rows, half), jnp.bfloat16),
        jax.ShapeDtypeStruct((tok_rows, half), jnp.float32),
    )
    att, send_a, keep_a, *_ = pl.pallas_call(
        functools.partial(last_kernel, xors),
        out_shape=(jax.ShapeDtypeStruct((tok_rows, local_heads * head_dim), jnp.bfloat16),) + pair_shapes + state_shapes,
        in_specs=[tree_spec] + [vmem] * (5 + len(pieces)),
        out_specs=(vmem,) * 6,
        input_output_aliases={2: 3, 3: 4, 4: 5},
        compiler_params=params,
        cost_estimate=pl.CostEstimate(flops=1_000_000_000, bytes_accessed=10_000_000, transcendentals=1_000_000),
    )(tree, q, *state, *pieces, out_weight)

    def projected(flip, part, shapes, att):
        return pl.pallas_call(
            functools.partial(project_pair, flip, part),
            out_shape=shapes,
            in_specs=[vmem, vmem],
            out_specs=(vmem, vmem),
            compiler_params=params,
            cost_estimate=pl.CostEstimate(flops=540_000_000, bytes_accessed=4_000_000, transcendentals=0),
        )(att, out_weight)

    def added(keep, arrived):
        return (keep + arrived.astype(jnp.float32)).astype(jnp.bfloat16)

    in_a = swap(send_a, "tp", tp_size, 1)
    send_b, keep_b = projected(2, 1, pair_shapes, att)
    in_b = swap(send_b, "tp", tp_size, 1)
    far_a = added(keep_a, in_a)
    from_a = swap(far_a, "tp", tp_size, 2)
    far_b = added(keep_b, in_b)
    from_b = swap(far_b, "tp", tp_size, 2)
    att, _ = lax.optimization_barrier((att, far_a))
    send_near, keep_near = projected(
        0,
        0,
        (jax.ShapeDtypeStruct((tok_rows, width), jnp.bfloat16), jax.ShapeDtypeStruct((tok_rows, width), jnp.float32)),
        att,
    )
    near_in = swap(send_near, "tp", tp_size, 1)
    from_far = jnp.concatenate([from_a, from_b], axis=1).astype(jnp.float32)
    return (keep_near + near_in.astype(jnp.float32) + from_far).astype(jnp.bfloat16)


def solution(mesh):
    return jax.shard_map(
        functools.partial(shards, mesh.shape["ctx"], mesh.shape["tp"]),
        mesh=mesh,
        in_specs=(
            P("ctx", "tp", None),
            P("ctx", "tp", None),
            P("ctx", "tp", None),
            P(),
            P("tp", None),
        ),
        out_specs=P("ctx", "tp"),
        check_vma=False,
    )
```

```python
import functools
import math

import jax
import jax.numpy as jnp
from jax import lax
from jax.experimental import pallas as pl
from jax.experimental.pallas import tpu as pltpu
from jax.sharding import PartitionSpec as P

BLOCK = 128
DIRECT_SIZE = 8
VMEM_LIMIT = 32 * 1024 * 1024


def scores_of(k, q):
    return lax.dot_general(k, q, (((1,), (1,)), ((), ())), preferred_element_type=jnp.float32)


def weighted(v, p):
    return lax.dot_general(v, p.astype(jnp.bfloat16), (((0,), (0,)), ((), ())), preferred_element_type=jnp.float32)


def exponent_scale(head_dim):
    return math.log2(math.e) / math.sqrt(head_dim)


def reached_mask(parents_ref):
    me = lax.axis_index("ctx")
    wanted = parents_ref[me]
    reached = jnp.int32(0)
    for step in range(1, DIRECT_SIZE):
        block = me - step
        hit = (block >= 0) & (block == wanted)
        block = jnp.maximum(block, 0)
        reached = jnp.where(hit, reached | lax.shift_left(jnp.int32(1), block), reached)
        wanted = jnp.where(hit, parents_ref[block], wanted)
    return reached


def pack_kernel(walk, k_hbm, v_hbm, parents_hbm, kv_ref, reached_ref, parents_ref, sems):
    copies = [
        pltpu.make_async_copy(parents_hbm, parents_ref, sems.at[0]),
        pltpu.make_async_copy(k_hbm, kv_ref.at[0:BLOCK, :], sems.at[1]),
        pltpu.make_async_copy(v_hbm, kv_ref.at[BLOCK:2 * BLOCK, :], sems.at[2]),
    ]
    for copy in copies:
        copy.start()
    copies[0].wait()
    reached = reached_mask(parents_ref) if walk else jnp.int32(0)
    reached_ref[...] = jnp.full(reached_ref.shape, reached, jnp.int32)
    copies[1].wait()
    copies[2].wait()


def project(att, w_ref, start, width):
    start = pl.multiple_of(start, 128)
    return jnp.dot(att, w_ref[:, pl.ds(start, width)], preferred_element_type=jnp.float32)


def absorb(scale, q_ref, k, v, m_ref, l_ref, acc_ref):
    s = scores_of(k, q_ref[...])
    m_old = m_ref[...]
    m_new = jnp.maximum(m_old, jnp.max(s, axis=0, keepdims=True))
    p = jnp.exp2((s - m_new) * scale)
    factor = jnp.exp2((m_old - m_new) * scale)
    m_ref[...] = m_new
    l_ref[...] = l_ref[...] * factor + jnp.sum(p, axis=0, keepdims=True)
    acc_ref[...] = acc_ref[...] * factor + weighted(v, p)


def absorb_reached(xors, reached_ref, q_ref, kv_refs, state):
    scale = exponent_scale(q_ref.shape[1])
    me = lax.axis_index("ctx")
    reached = jnp.max(reached_ref[...])
    for other, kv_ref in zip(xors, kv_refs):
        @pl.when((lax.shift_right_logical(reached, me ^ other) & 1) == 1)
        def _():
            absorb(scale, q_ref, kv_ref[0:BLOCK, :], kv_ref[BLOCK:, :], *state)


def absorb_walk(parents_ref, q_ref, piece, state):
    scale = exponent_scale(q_ref.shape[1])
    me = lax.axis_index("ctx")

    def visit(step, wanted):
        block = me - step
        hit = (block >= 0) & (block == wanted)
        block = jnp.maximum(block, 0)

        @pl.when(hit)
        def _():
            start = pl.multiple_of(block * 2 * BLOCK, 2 * BLOCK)
            absorb(scale, q_ref, piece[pl.ds(start, BLOCK), :], piece[pl.ds(start + BLOCK, BLOCK), :], *state)

        return jnp.where(hit, parents_ref[block], wanted)

    lax.fori_loop(1, parents_ref.shape[0], visit, parents_ref[me])


def own_block_kernel(xors, reached_ref, q_ref, kv_ref, *refs):
    state = refs[len(xors):]
    m_ref, l_ref, acc_ref = state
    scale = exponent_scale(q_ref.shape[1])
    s = scores_of(kv_ref[0:BLOCK, :], q_ref[...])
    key_at = lax.broadcasted_iota(jnp.int32, s.shape, 0)
    query_at = lax.broadcasted_iota(jnp.int32, s.shape, 1) & (BLOCK - 1)
    s = jnp.where(key_at <= query_at, s, -1e30)
    m = jnp.max(s, axis=0, keepdims=True)
    p = jnp.exp2((s - m) * scale)
    m_ref[...] = m
    l_ref[...] = jnp.sum(p, axis=0, keepdims=True)
    acc_ref[...] = weighted(kv_ref[BLOCK:, :], p)
    absorb_reached(xors, reached_ref, q_ref, refs[:len(xors)], state)


def others_kernel(xors, reached_ref, q_ref, m_in, l_in, acc_in, *refs):
    state = refs[len(xors):]
    absorb_reached(xors, reached_ref, q_ref, refs[:len(xors)], state)


def last_kernel(xors, tree_ref, q_ref, m_in, l_in, acc_in, *refs):
    kv_refs = refs[:max(len(xors), 1)]
    w_ref, att_ref, send_ref, keep_ref, *state = refs[len(kv_refs):]
    rows, head_dim = q_ref.shape
    if xors:
        absorb_reached(xors, tree_ref, q_ref, kv_refs, state)
    else:
        absorb_walk(tree_ref, q_ref, kv_refs[0], state)
    m_ref, l_ref, acc_ref = state

    for head in range(rows // BLOCK):
        at = slice(head * BLOCK, (head + 1) * BLOCK)
        part = acc_ref[:, at] / l_ref[:, at]
        att_ref[:, head * head_dim:(head + 1) * head_dim] = part.T.astype(jnp.bfloat16)

    project_pair(2, 0, att_ref, w_ref, send_ref, keep_ref)


def project_pair(flip, half, att_ref, w_ref, send_ref, keep_ref):
    target = lax.axis_index("tp") ^ flip
    width = w_ref.shape[1] // 4
    cols = keep_ref.shape[1]
    att = att_ref[...]
    send_ref[...] = project(att, w_ref, (target ^ 1) * width + half * cols, cols).astype(jnp.bfloat16)
    keep_ref[...] = project(att, w_ref, target * width + half * cols, cols)


def finish_kernel(part, keep_ref, near_ref, arrived_ref, *refs):
    out_hbm, sum_ref, sem = refs[-3:]
    cols = arrived_ref.shape[1]
    at = slice(part * cols, (part + 1) * cols)
    total = keep_ref[:, at] + near_ref[:, at].astype(jnp.float32) + arrived_ref[...].astype(jnp.float32)
    sum_ref[...] = total.astype(jnp.bfloat16)
    copy = pltpu.make_async_copy(sum_ref, out_hbm.at[:, at], sem)
    copy.start()
    copy.wait()


def shards(ctx_size, tp_size, query_heads, key_heads, value_heads, parents, out_weight):
    tok_rows, local_heads, head_dim = query_heads.shape
    assert tok_rows == BLOCK and key_heads.shape[1] == 1 and parents.shape[0] == ctx_size and tp_size == 4
    width = out_weight.shape[1] // tp_size
    rows = local_heads * tok_rows
    params = pltpu.CompilerParams(vmem_limit_bytes=VMEM_LIMIT)
    vmem = pl.BlockSpec(memory_space=pltpu.VMEM)
    hbm = pl.BlockSpec(memory_space=pltpu.HBM)
    smem = pl.BlockSpec(memory_space=pltpu.SMEM)

    def in_hbm(x):
        return pltpu.with_memory_space_constraint(x, pltpu.HBM)

    def swap(x, axis, size, other):
        return lax.ppermute(x, axis, [(i, i ^ other) for i in range(size)])

    def forward(x, other):
        route = []
        for i in range(ctx_size):
            for j in range(tp_size):
                target = (i ^ 1, j) if i ^ other < i else (i, j ^ 1)
                route.append((i * tp_size + j, target[0] * tp_size + target[1]))
        return lax.ppermute(x, ("ctx", "tp"), route)

    kv, reached = pl.pallas_call(
        functools.partial(pack_kernel, ctx_size == DIRECT_SIZE),
        out_shape=(
            jax.ShapeDtypeStruct((2 * tok_rows, head_dim), jnp.bfloat16),
            jax.ShapeDtypeStruct((8, 128), jnp.int32),
        ),
        in_specs=[hbm, hbm, hbm],
        out_specs=(vmem, vmem),
        scratch_shapes=[pltpu.SMEM(parents.shape, jnp.int32), pltpu.SemaphoreType.DMA((3,))],
        compiler_params=params,
        cost_estimate=pl.CostEstimate(flops=1_000_000, bytes_accessed=130_000, transcendentals=0),
    )(in_hbm(key_heads[:, 0, :]), in_hbm(value_heads[:, 0, :]), in_hbm(parents))
    if ctx_size == DIRECT_SIZE:
        columns = [swap(kv, "ctx", ctx_size, other) for other in (4, 2, 6)]
        beside = swap(kv, "ctx", ctx_size, 1)
        pairs = [forward(x, other) for x, other in zip(columns, (4, 2, 6))]
        early, early_xors = [beside, *columns], (1, 4, 2, 6)
    else:
        early, early_xors = [], ()
    q = jnp.transpose(query_heads, (1, 0, 2)).reshape(rows, head_dim)

    m, l, acc = pl.pallas_call(
        functools.partial(own_block_kernel, early_xors),
        out_shape=(
            jax.ShapeDtypeStruct((1, rows), jnp.float32),
            jax.ShapeDtypeStruct((1, rows), jnp.float32),
            jax.ShapeDtypeStruct((head_dim, rows), jnp.float32),
        ),
        in_specs=[vmem] * (3 + len(early)),
        out_specs=(vmem,) * 3,
        compiler_params=params,
        cost_estimate=pl.CostEstimate(flops=5000000000, bytes_accessed=1_000_000, transcendentals=260_000),
    )(reached, q, kv, *early)

    state = (m, l, acc)
    state_shapes = tuple(jax.ShapeDtypeStruct(x.shape, x.dtype) for x in state)
    if ctx_size == DIRECT_SIZE:
        def absorbed(state, xors, arrived):
            return pl.pallas_call(
                functools.partial(others_kernel, xors),
                out_shape=state_shapes,
                in_specs=[vmem] * (5 + len(xors)),
                out_specs=(vmem,) * 3,
                input_output_aliases={2: 0, 3: 1, 4: 2},
                compiler_params=params,
                cost_estimate=pl.CostEstimate(flops=270_000_000, bytes_accessed=1_000_000, transcendentals=500_000),
            )(reached, q, *state, *arrived)

        state = absorbed(state, (3, 7), pairs[1:])
        xors, pieces, tree, tree_spec = (5,), pairs[:1], reached, vmem
    else:
        xors, pieces, tree, tree_spec = (), [lax.all_gather(kv, "ctx", axis=0, tiled=True)], parents, smem

    half = width // 2
    pair_shapes = (
        jax.ShapeDtypeStruct((tok_rows, half), jnp.bfloat16),
        jax.ShapeDtypeStruct((tok_rows, half), jnp.float32),
    )
    att, send_a, keep_a, *_ = pl.pallas_call(
        functools.partial(last_kernel, xors),
        out_shape=(jax.ShapeDtypeStruct((tok_rows, local_heads * head_dim), jnp.bfloat16),) + pair_shapes + state_shapes,
        in_specs=[tree_spec] + [vmem] * (5 + len(pieces)),
        out_specs=(vmem,) * 6,
        input_output_aliases={2: 3, 3: 4, 4: 5},
        compiler_params=params,
        cost_estimate=pl.CostEstimate(flops=1_000_000_000, bytes_accessed=10_000_000, transcendentals=1_000_000),
    )(tree, q, *state, *pieces, out_weight)

    def projected(flip, part, shapes, att):
        return pl.pallas_call(
            functools.partial(project_pair, flip, part),
            out_shape=shapes,
            in_specs=[vmem, vmem],
            out_specs=(vmem, vmem),
            compiler_params=params,
            cost_estimate=pl.CostEstimate(flops=540_000_000, bytes_accessed=4_000_000, transcendentals=0),
        )(att, out_weight)

    def added(keep, arrived):
        return (keep + arrived.astype(jnp.float32)).astype(jnp.bfloat16)

    in_a = swap(send_a, "tp", tp_size, 1)
    send_b, keep_b = projected(2, 1, pair_shapes, att)
    in_b = swap(send_b, "tp", tp_size, 1)
    far_a = added(keep_a, in_a)
    from_a = swap(far_a, "tp", tp_size, 2)
    far_b = added(keep_b, in_b)
    from_b = swap(far_b, "tp", tp_size, 2)
    att, _ = lax.optimization_barrier((att, far_a))
    send_near, keep_near = projected(
        0,
        0,
        (jax.ShapeDtypeStruct((tok_rows, width), jnp.bfloat16), jax.ShapeDtypeStruct((tok_rows, width), jnp.float32)),
        att,
    )
    near_in = swap(send_near, "tp", tp_size, 1)
    def finished(part, arrived, *begun):
        return pl.pallas_call(
            functools.partial(finish_kernel, part),
            out_shape=jax.ShapeDtypeStruct((tok_rows, width), jnp.bfloat16),
            in_specs=[vmem] * 3 + [hbm] * len(begun),
            out_specs=hbm,
            scratch_shapes=[pltpu.VMEM((tok_rows, half), jnp.bfloat16), pltpu.SemaphoreType.DMA],
            input_output_aliases={3: 0} if begun else {},
            compiler_params=params,
            cost_estimate=pl.CostEstimate(flops=300_000, bytes_accessed=800_000, transcendentals=0),
        )(keep_near, near_in, arrived, *begun)

    return finished(1, from_b, finished(0, from_a))


def solution(mesh):
    return jax.shard_map(
        functools.partial(shards, mesh.shape["ctx"], mesh.shape["tp"]),
        mesh=mesh,
        in_specs=(
            P("ctx", "tp", None),
            P("ctx", "tp", None),
            P("ctx", "tp", None),
            P(),
            P("tp", None),
        ),
        out_specs=P("ctx", "tp"),
        check_vma=False,
    )
```

```python
import functools
import math

import jax
import jax.numpy as jnp
from jax import lax
from jax.experimental import pallas as pl
from jax.experimental.pallas import tpu as pltpu
from jax.sharding import PartitionSpec as P

BLOCK = 128
DIRECT_SIZE = 8
VMEM_LIMIT = 32 * 1024 * 1024


def scores_of(k, q):
    return lax.dot_general(k, q, (((1,), (1,)), ((), ())), preferred_element_type=jnp.float32)


def weighted(v, p):
    return lax.dot_general(v, p.astype(jnp.bfloat16), (((0,), (0,)), ((), ())), preferred_element_type=jnp.float32)


def exponent_scale(head_dim):
    return math.log2(math.e) / math.sqrt(head_dim)


def reached_mask(parents_ref):
    me = lax.axis_index("ctx")
    wanted = parents_ref[me]
    reached = jnp.int32(0)
    for step in range(1, DIRECT_SIZE):
        block = me - step
        hit = (block >= 0) & (block == wanted)
        block = jnp.maximum(block, 0)
        reached = jnp.where(hit, reached | lax.shift_left(jnp.int32(1), block), reached)
        wanted = jnp.where(hit, parents_ref[block], wanted)
    return reached


def pack_kernel(walk, k_hbm, v_hbm, parents_hbm, kv_ref, reached_ref, parents_ref, sems):
    copies = [
        pltpu.make_async_copy(parents_hbm, parents_ref, sems.at[0]),
        pltpu.make_async_copy(k_hbm, kv_ref.at[0:BLOCK, :], sems.at[1]),
        pltpu.make_async_copy(v_hbm, kv_ref.at[BLOCK:2 * BLOCK, :], sems.at[2]),
    ]
    for copy in copies:
        copy.start()
    copies[0].wait()
    reached = reached_mask(parents_ref) if walk else jnp.int32(0)
    reached_ref[...] = jnp.full(reached_ref.shape, reached, jnp.int32)
    copies[1].wait()
    copies[2].wait()


def project(att, w_ref, start, width):
    start = pl.multiple_of(start, 128)
    return jnp.dot(att, w_ref[:, pl.ds(start, width)], preferred_element_type=jnp.float32)


def absorb(scale, q_ref, k, v, m_ref, l_ref, acc_ref):
    s = scores_of(k, q_ref[...])
    m_old = m_ref[...]
    m_new = jnp.maximum(m_old, jnp.max(s, axis=0, keepdims=True))
    p = jnp.exp2((s - m_new) * scale)
    factor = jnp.exp2((m_old - m_new) * scale)
    m_ref[...] = m_new
    l_ref[...] = l_ref[...] * factor + jnp.sum(p, axis=0, keepdims=True)
    acc_ref[...] = acc_ref[...] * factor + weighted(v, p)


def absorb_reached(xors, reached_ref, q_ref, kv_refs, state):
    scale = exponent_scale(q_ref.shape[1])
    me = lax.axis_index("ctx")
    reached = jnp.max(reached_ref[...])
    for other, kv_ref in zip(xors, kv_refs):
        @pl.when((lax.shift_right_logical(reached, me ^ other) & 1) == 1)
        def _():
            absorb(scale, q_ref, kv_ref[0:BLOCK, :], kv_ref[BLOCK:, :], *state)


def absorb_walk(parents_ref, q_ref, piece, state):
    scale = exponent_scale(q_ref.shape[1])
    me = lax.axis_index("ctx")

    def visit(step, wanted):
        block = me - step
        hit = (block >= 0) & (block == wanted)
        block = jnp.maximum(block, 0)

        @pl.when(hit)
        def _():
            start = pl.multiple_of(block * 2 * BLOCK, 2 * BLOCK)
            absorb(scale, q_ref, piece[pl.ds(start, BLOCK), :], piece[pl.ds(start + BLOCK, BLOCK), :], *state)

        return jnp.where(hit, parents_ref[block], wanted)

    lax.fori_loop(1, parents_ref.shape[0], visit, parents_ref[me])


def own_block_kernel(xors, reached_ref, q_ref, kv_ref, *refs):
    state = refs[len(xors):]
    m_ref, l_ref, acc_ref = state
    scale = exponent_scale(q_ref.shape[1])
    s = scores_of(kv_ref[0:BLOCK, :], q_ref[...])
    key_at = lax.broadcasted_iota(jnp.int32, s.shape, 0)
    query_at = lax.broadcasted_iota(jnp.int32, s.shape, 1) & (BLOCK - 1)
    s = jnp.where(key_at <= query_at, s, -1e30)
    m = jnp.max(s, axis=0, keepdims=True)
    p = jnp.exp2((s - m) * scale)
    m_ref[...] = m
    l_ref[...] = jnp.sum(p, axis=0, keepdims=True)
    acc_ref[...] = weighted(kv_ref[BLOCK:, :], p)
    absorb_reached(xors, reached_ref, q_ref, refs[:len(xors)], state)


def others_kernel(xors, reached_ref, q_ref, m_in, l_in, acc_in, *refs):
    state = refs[len(xors):]
    absorb_reached(xors, reached_ref, q_ref, refs[:len(xors)], state)


def last_kernel(xors, tree_ref, q_ref, m_in, l_in, acc_in, *refs):
    kv_refs = refs[:max(len(xors), 1)]
    w_ref, att_ref, send_ref, keep_ref, *state = refs[len(kv_refs):]
    rows, head_dim = q_ref.shape
    if xors:
        absorb_reached(xors, tree_ref, q_ref, kv_refs, state)
    else:
        absorb_walk(tree_ref, q_ref, kv_refs[0], state)
    m_ref, l_ref, acc_ref = state

    for head in range(rows // BLOCK):
        at = slice(head * BLOCK, (head + 1) * BLOCK)
        part = (acc_ref[:, at] / l_ref[:, at]).astype(jnp.bfloat16)
        att_ref[:, head * head_dim:(head + 1) * head_dim] = part.T

    project_pair(2, 0, att_ref, w_ref, send_ref, keep_ref)


def project_pair(flip, half, att_ref, w_ref, send_ref, keep_ref):
    target = lax.axis_index("tp") ^ flip
    width = w_ref.shape[1] // 4
    cols = keep_ref.shape[1]
    att = att_ref[...]
    send_ref[...] = project(att, w_ref, (target ^ 1) * width + half * cols, cols).astype(jnp.bfloat16)
    keep_ref[...] = project(att, w_ref, target * width + half * cols, cols)


def finish_kernel(part, keep_ref, near_ref, arrived_ref, *refs):
    out_hbm, sum_ref, sem = refs[-3:]
    cols = arrived_ref.shape[1]
    at = slice(part * cols, (part + 1) * cols)
    total = keep_ref[:, at] + near_ref[:, at].astype(jnp.float32) + arrived_ref[...].astype(jnp.float32)
    sum_ref[...] = total.astype(jnp.bfloat16)
    copy = pltpu.make_async_copy(sum_ref, out_hbm.at[:, at], sem)
    copy.start()
    copy.wait()


def shards(ctx_size, tp_size, query_heads, key_heads, value_heads, parents, out_weight):
    tok_rows, local_heads, head_dim = query_heads.shape
    assert tok_rows == BLOCK and key_heads.shape[1] == 1 and parents.shape[0] == ctx_size and tp_size == 4
    width = out_weight.shape[1] // tp_size
    rows = local_heads * tok_rows
    params = pltpu.CompilerParams(vmem_limit_bytes=VMEM_LIMIT)
    vmem = pl.BlockSpec(memory_space=pltpu.VMEM)
    hbm = pl.BlockSpec(memory_space=pltpu.HBM)
    smem = pl.BlockSpec(memory_space=pltpu.SMEM)

    def in_hbm(x):
        return pltpu.with_memory_space_constraint(x, pltpu.HBM)

    def swap(x, axis, size, other):
        return lax.ppermute(x, axis, [(i, i ^ other) for i in range(size)])

    def forward(x, other):
        route = []
        for i in range(ctx_size):
            for j in range(tp_size):
                target = (i ^ 1, j) if i ^ other < i else (i, j ^ 1)
                route.append((i * tp_size + j, target[0] * tp_size + target[1]))
        return lax.ppermute(x, ("ctx", "tp"), route)

    kv, reached = pl.pallas_call(
        functools.partial(pack_kernel, ctx_size == DIRECT_SIZE),
        out_shape=(
            jax.ShapeDtypeStruct((2 * tok_rows, head_dim), jnp.bfloat16),
            jax.ShapeDtypeStruct((8, 128), jnp.int32),
        ),
        in_specs=[hbm, hbm, hbm],
        out_specs=(vmem, vmem),
        scratch_shapes=[pltpu.SMEM(parents.shape, jnp.int32), pltpu.SemaphoreType.DMA((3,))],
        compiler_params=params,
        cost_estimate=pl.CostEstimate(flops=1_000_000, bytes_accessed=130_000, transcendentals=0),
    )(in_hbm(key_heads[:, 0, :]), in_hbm(value_heads[:, 0, :]), in_hbm(parents))
    if ctx_size == DIRECT_SIZE:
        columns = [swap(kv, "ctx", ctx_size, other) for other in (4, 2, 6)]
        beside = swap(kv, "ctx", ctx_size, 1)
        pairs = [forward(x, other) for x, other in zip(columns, (4, 2, 6))]
        early, early_xors = [beside, *columns], (1, 4, 2, 6)
    else:
        early, early_xors = [], ()
    q = jnp.transpose(query_heads, (1, 0, 2)).reshape(rows, head_dim)

    m, l, acc = pl.pallas_call(
        functools.partial(own_block_kernel, early_xors),
        out_shape=(
            jax.ShapeDtypeStruct((1, rows), jnp.float32),
            jax.ShapeDtypeStruct((1, rows), jnp.float32),
            jax.ShapeDtypeStruct((head_dim, rows), jnp.float32),
        ),
        in_specs=[vmem] * (3 + len(early)),
        out_specs=(vmem,) * 3,
        compiler_params=params,
        cost_estimate=pl.CostEstimate(flops=5000000000, bytes_accessed=1_000_000, transcendentals=260_000),
    )(reached, q, kv, *early)

    state = (m, l, acc)
    state_shapes = tuple(jax.ShapeDtypeStruct(x.shape, x.dtype) for x in state)
    if ctx_size == DIRECT_SIZE:
        def absorbed(state, xors, arrived):
            return pl.pallas_call(
                functools.partial(others_kernel, xors),
                out_shape=state_shapes,
                in_specs=[vmem] * (5 + len(xors)),
                out_specs=(vmem,) * 3,
                input_output_aliases={2: 0, 3: 1, 4: 2},
                compiler_params=params,
                cost_estimate=pl.CostEstimate(flops=270_000_000, bytes_accessed=1_000_000, transcendentals=500_000),
            )(reached, q, *state, *arrived)

        state = absorbed(state, (3, 7), pairs[1:])
        xors, pieces, tree, tree_spec = (5,), pairs[:1], reached, vmem
    else:
        xors, pieces, tree, tree_spec = (), [lax.all_gather(kv, "ctx", axis=0, tiled=True)], parents, smem

    half = width // 2
    pair_shapes = (
        jax.ShapeDtypeStruct((tok_rows, half), jnp.bfloat16),
        jax.ShapeDtypeStruct((tok_rows, half), jnp.float32),
    )
    att, send_a, keep_a, *_ = pl.pallas_call(
        functools.partial(last_kernel, xors),
        out_shape=(jax.ShapeDtypeStruct((tok_rows, local_heads * head_dim), jnp.bfloat16),) + pair_shapes + state_shapes,
        in_specs=[tree_spec] + [vmem] * (5 + len(pieces)),
        out_specs=(vmem,) * 6,
        input_output_aliases={2: 3, 3: 4, 4: 5},
        compiler_params=params,
        cost_estimate=pl.CostEstimate(flops=1_000_000_000, bytes_accessed=10_000_000, transcendentals=1_000_000),
    )(tree, q, *state, *pieces, out_weight)

    def projected(flip, part, shapes, att):
        return pl.pallas_call(
            functools.partial(project_pair, flip, part),
            out_shape=shapes,
            in_specs=[vmem, vmem],
            out_specs=(vmem, vmem),
            compiler_params=params,
            cost_estimate=pl.CostEstimate(flops=540_000_000, bytes_accessed=4_000_000, transcendentals=0),
        )(att, out_weight)

    def added(keep, arrived):
        return (keep + arrived.astype(jnp.float32)).astype(jnp.bfloat16)

    in_a = swap(send_a, "tp", tp_size, 1)
    send_b, keep_b = projected(2, 1, pair_shapes, att)
    in_b = swap(send_b, "tp", tp_size, 1)
    far_a = added(keep_a, in_a)
    from_a = swap(far_a, "tp", tp_size, 2)
    far_b = added(keep_b, in_b)
    from_b = swap(far_b, "tp", tp_size, 2)
    att, _ = lax.optimization_barrier((att, far_a))
    send_near, keep_near = projected(
        0,
        0,
        (jax.ShapeDtypeStruct((tok_rows, width), jnp.bfloat16), jax.ShapeDtypeStruct((tok_rows, width), jnp.float32)),
        att,
    )
    near_in = swap(send_near, "tp", tp_size, 1)
    def finished(part, arrived, *begun):
        return pl.pallas_call(
            functools.partial(finish_kernel, part),
            out_shape=jax.ShapeDtypeStruct((tok_rows, width), jnp.bfloat16),
            in_specs=[vmem] * 3 + [hbm] * len(begun),
            out_specs=hbm,
            scratch_shapes=[pltpu.VMEM((tok_rows, half), jnp.bfloat16), pltpu.SemaphoreType.DMA],
            input_output_aliases={3: 0} if begun else {},
            compiler_params=params,
            cost_estimate=pl.CostEstimate(flops=300_000, bytes_accessed=800_000, transcendentals=0),
        )(keep_near, near_in, arrived, *begun)

    return finished(1, from_b, finished(0, from_a))


def solution(mesh):
    return jax.shard_map(
        functools.partial(shards, mesh.shape["ctx"], mesh.shape["tp"]),
        mesh=mesh,
        in_specs=(
            P("ctx", "tp", None),
            P("ctx", "tp", None),
            P("ctx", "tp", None),
            P(),
            P("tp", None),
        ),
        out_specs=P("ctx", "tp"),
        check_vma=False,
    )
```
